512 devices in a mesh: group: 16 (over y, core), member: 32 (over z, x).
Axes of the slice: x: 4, y: 8, z: 8, core: 2. Of those that a mesh axis runs over, the one named last changes fastest.
Arguments:
- teacher_patches: bfloat16 [131072, 256], P(('group', 'member')), may hold values from -16 to 16
- student_patches: bfloat16 [131072, 256], P(('group', 'member')), may hold values from -16 to 16
- mask_index: int32 [65536], P(('group', 'member')), may hold values from 0 to 255, as said below
- teacher_weight: bfloat16 [256, 32768], P(None, 'member'), may hold values from -2 to 2
- student_weight: bfloat16 [256, 32768], P(None, 'member'), may hold values from -2 to 2
Outputs:
- grad_weight: bfloat16 [256, 32768], P(None, 'member')
The draws below stay inside these ranges and needn't reach their ends.
Inputs may be any that keep to these rules, and one draw needn't show every extreme that they name: `mask_index`: within each aligned block of 128 entries the entries are distinct, and each names one of the 256 patch rows of that block's own device shard.
All inputs are finite; a program needn't handle non-finite values.
Results may differ from the reference program's by a relative error of at most 0.0065.
Values may be sent and summed in bfloat16 or wider, within the bound.
No kernel may reach another device: no remote copies, remote signals or barrier semaphores. Data moves between devices by JAX's collectives and lax.ppermute only.
A program may use at most 128 MiB of HBM per device.

```python
import math
import jax
import jax.numpy as jnp
from jax import lax

D = 256
K = 32768
ITERS = 3
ROWS_DEV = 128
PATCH_DEV = 256
ROWS = 65536
PATCHES = 131072


def common_direction(key):
    return jax.random.normal(jax.random.fold_in(key, 97), (D,), jnp.float32) * (1.0 / math.sqrt(D))


def ramped_rows(noise, direction, top):
    count = noise.shape[0]
    ramp = top * jnp.arange(count, dtype=jnp.float32) / count
    return (noise + ramp[:, None] * direction[None, :]).astype(jnp.bfloat16)


def ramped_columns(noise, direction, lowest, highest):
    count = noise.shape[1]
    ramp = lowest + (highest - lowest) * jnp.arange(count, dtype=jnp.float32) / count
    return (noise + direction[:, None] * ramp[None, :]).astype(jnp.bfloat16)


def draw_teacher_patches(key, part):
    direction = common_direction(key)
    key = jax.random.fold_in(key, 1)
    noise = jnp.clip(jax.random.normal(key, (PATCHES, D), jnp.float32), -6.0, 6.0)
    return ramped_rows(noise, direction, 8.0)


def draw_student_patches(key, part):
    direction = common_direction(key)
    key = jax.random.fold_in(key, 2)
    noise = jnp.clip(jax.random.normal(key, (PATCHES, D), jnp.float32), -6.0, 6.0)
    return ramped_rows(noise, direction, 6.0)


def draw_teacher_weight(key, part):
    direction = common_direction(key)
    key = jax.random.fold_in(key, 3)
    noise = jnp.clip(jax.random.normal(key, (D, K), jnp.float32), -6.0, 6.0) * (1.0 / math.sqrt(D))
    return ramped_columns(noise, direction, -0.5, 1.0)


def draw_student_weight(key, part):
    direction = common_direction(key)
    key = jax.random.fold_in(key, 4)
    noise = jnp.clip(jax.random.normal(key, (D, K), jnp.float32), -6.0, 6.0) * (1.0 / math.sqrt(D))
    return ramped_columns(noise, direction, -0.8, 0.6)


def draw_mask_index(key, part):
    key = jax.random.fold_in(key, 5)
    owners = ROWS // ROWS_DEV
    keys = jax.random.split(key, owners)
    picks = jax.vmap(lambda single: jax.random.permutation(single, PATCH_DEV)[:ROWS_DEV])(keys)
    return picks.reshape(ROWS).astype(jnp.int32)


def setup_inputs(seed: int = 0) -> dict:
    arg_keys = jax.random.split(jax.random.key(seed), 6)
    teacher_patches = draw_teacher_patches(jax.random.fold_in(arg_keys[5], 71), 0)
    student_patches = draw_student_patches(jax.random.fold_in(arg_keys[5], 71), 0)
    mask_index = draw_mask_index(jax.random.fold_in(arg_keys[5], 71), 0)
    teacher_weight = draw_teacher_weight(jax.random.fold_in(arg_keys[5], 71), 0)
    student_weight = draw_student_weight(jax.random.fold_in(arg_keys[5], 71), 0)
    return dict(teacher_patches=teacher_patches, student_patches=student_patches, mask_index=mask_index, teacher_weight=teacher_weight, student_weight=student_weight)


epsilon = 1e-06
teacher_scale = 1.0 / 0.07
student_scale = 1.0 / 0.1
grad_factor = 256.0 / 0.1

def unit_rows(values):
    values = values.astype(jnp.float32)
    return (values * lax.rsqrt(lax.optimization_barrier(jnp.sum(values * values, axis=1, keepdims=True)) + epsilon)).astype(jnp.bfloat16)

def unit_columns(values):
    values = values.astype(jnp.float32)
    return (values * lax.rsqrt(lax.optimization_barrier(jnp.sum(values * values, axis=0, keepdims=True)) + epsilon)).astype(jnp.bfloat16)

def exp_scores(rows, protos, scale):
    return jnp.exp(jnp.dot(rows, protos, preferred_element_type=jnp.float32) * scale).astype(jnp.bfloat16)

def weight_back(grad_sum, weight):
    weight = weight.astype(jnp.float32)
    inverse = lax.rsqrt(lax.optimization_barrier(jnp.sum(weight * weight, axis=0, keepdims=True)) + epsilon)
    along = lax.optimization_barrier(jnp.sum(grad_sum * weight, axis=0, keepdims=True))
    return (grad_sum * inverse - weight * (inverse * inverse * inverse * along)).astype(jnp.bfloat16)

def reference(teacher_patches, student_patches, mask_index, teacher_weight, student_weight):
    count = mask_index.shape[0]
    owner = jnp.arange(count, dtype=jnp.int32) // ROWS_DEV
    chosen = (owner * PATCH_DEV + mask_index.astype(jnp.int32)).astype(jnp.int32)
    teach_rows = unit_rows(teacher_patches[chosen])
    stud_rows = unit_rows(student_patches[chosen])
    teach_protos = unit_columns(teacher_weight)
    stud_protos = unit_columns(student_weight)
    width = math.gcd(count, 512)
    blocks = count // width
    teach_blocks = teach_rows.reshape(blocks, width, teach_rows.shape[1])
    stud_blocks = stud_rows.reshape(blocks, width, stud_rows.shape[1])
    start_mass = jnp.zeros((teach_protos.shape[1],), jnp.float32)

    def first_pass(carry, rows):
        codes = exp_scores(rows, teach_protos, teacher_scale)
        return (carry + lax.optimization_barrier(jnp.sum(codes.astype(jnp.float32), axis=0)), None)
    col_mass, _ = lax.scan(first_pass, start_mass, teach_blocks)
    for sweep in range(ITERS - 1):
        col_scale = 1.0 / col_mass

        def sweep_pass(carry, rows, col_scale=col_scale):
            codes = exp_scores(rows, teach_protos, teacher_scale).astype(jnp.float32)
            row_scale = 1.0 / lax.optimization_barrier(jnp.sum(codes * col_scale[None, :], axis=1))
            return (carry + lax.optimization_barrier(jnp.sum(codes * row_scale[:, None], axis=0)), None)
        col_mass, _ = lax.scan(sweep_pass, start_mass, teach_blocks)
    col_scale = 1.0 / col_mass

    def last_pass(carry, pair):
        rows, stud = pair
        codes = exp_scores(rows, teach_protos, teacher_scale).astype(jnp.float32)
        row_scale = 1.0 / lax.optimization_barrier(jnp.sum(codes * col_scale[None, :], axis=1))
        target = codes * row_scale[:, None] * col_scale[None, :]
        expo = exp_scores(stud, stud_protos, student_scale).astype(jnp.float32)
        probs = expo / lax.optimization_barrier(jnp.sum(expo, axis=1, keepdims=True))
        slope = (grad_factor * (probs - target)).astype(jnp.bfloat16)
        term = lax.dot_general(stud, slope, (((0,), (0,)), ((), ())), preferred_element_type=jnp.float32)
        return (carry + term, None)
    grad_sum, _ = lax.scan(last_pass, jnp.zeros(student_weight.shape, jnp.float32), (teach_blocks, stud_blocks))
    return weight_back(grad_sum, student_weight)
```

```python
import functools

import jax
import jax.numpy as jnp
from jax import lax
from jax.experimental import pallas as pl
from jax.experimental.pallas import tpu as pltpu
from jax.sharding import Mesh
from jax.sharding import PartitionSpec as P

GROUP = ("y", "core")
MEMBER = ("z", "x")
ITERS = 3
LANES = 128
CHUNK = 512
VMEM_LIMIT = 48 * 1024 * 1024

epsilon = 1e-06
teacher_scale = 1.0 / 0.07
student_scale = 1.0 / 0.1
grad_factor = 256.0 / 0.1
NT = (((1,), (1,)), ((), ()))
TN = (((0,), (0,)), ((), ()))
f32 = jnp.float32
bf16 = jnp.bfloat16


def params():
    return pltpu.CompilerParams(vmem_limit_bytes=VMEM_LIMIT)


def cost(flops, transcendentals, nbytes):
    return pl.CostEstimate(flops=flops, transcendentals=transcendentals, bytes_accessed=nbytes)


def whole(shape):
    return pl.BlockSpec(shape, lambda *_: (0,) * len(shape))


def lane_row(block, start, count):
    return jnp.concatenate([block[start + j : start + j + 1, :] for j in range(count)], axis=1)


def split_rows(row):
    high = row.astype(bf16).astype(f32)
    low = row - high
    index = lax.broadcasted_iota(jnp.int32, (16, row.shape[1]), 0)
    return jnp.where(index == 0, high, jnp.where(index == 1, low, 0.0)).astype(bf16)


def rows_kernel(teacher_ref, student_ref, mask_ref, out_ref):
    patches = teacher_ref.shape[0]
    count = mask_ref.shape[1]
    chosen = lax.broadcasted_iota(jnp.int32, (patches, count), 0) == mask_ref[...]
    chosen = chosen.astype(f32).astype(bf16)
    for part, ref in enumerate((teacher_ref, student_ref)):
        rows = lax.dot_general(chosen, ref[...], TN, preferred_element_type=f32)
        square = jnp.sum(rows * rows, axis=1, keepdims=True)
        out_ref[part] = (rows * lax.rsqrt(square + epsilon)).astype(bf16)


def masked_rows(teacher, student, mask):
    count = mask.shape[1]
    return pl.pallas_call(
        rows_kernel,
        out_shape=jax.ShapeDtypeStruct((2, count, teacher.shape[1]), bf16),
        compiler_params=params(),
        name="masked_rows",
    )(teacher, student, mask)


def pack_piece(block, piece, pieces):
    rows, columns = block.shape
    width = columns // pieces
    part = block[:, piece * width : (piece + 1) * width]
    return jnp.concatenate([part[: rows // 2], part[rows // 2 :]], axis=1)


def protos_kernel(pieces, teacher_ref, student_ref, teach_ref, stud_ref, pack_ref):
    for source, out in ((teacher_ref, teach_ref), (student_ref, stud_ref)):
        values = source[...].astype(f32)
        square = jnp.sum(values * values, axis=0, keepdims=True)
        out[...] = (values * lax.rsqrt(square + epsilon)).astype(bf16)
    weight = student_ref[...].astype(f32)
    for piece in range(pieces):
        pack_ref[piece] = pack_piece(weight, piece, pieces)


def prototypes(teacher, student, pieces):
    rows, columns = teacher.shape
    like = jax.ShapeDtypeStruct(teacher.shape, bf16)
    return pl.pallas_call(
        functools.partial(protos_kernel, pieces),
        out_shape=(like, like, jax.ShapeDtypeStruct((pieces, rows // 2, 2 * columns // pieces), f32)),
        compiler_params=params(),
        name="prototypes",
    )(teacher, student)


def codes_kernel(rows_ref, protos_ref, codes_ref, cols_ref, total_ref):
    step = pl.program_id(0)

    @pl.when(step == 0)
    def _():
        total_ref[...] = jnp.zeros_like(total_ref)

    scores = jnp.dot(rows_ref[...], protos_ref[...], preferred_element_type=f32)
    codes = jnp.exp(scores * teacher_scale)
    codes_ref[...] = codes.astype(bf16)
    total_ref[...] += jnp.sum(codes, axis=0, keepdims=True)

    @pl.when(step == pl.num_programs(0) - 1)
    def _():
        spread_cols(total_ref[...], cols_ref)


def spread_cols(total, cols_ref):
    for j in range(cols_ref.shape[1]):
        part = total[:, j * LANES : (j + 1) * LANES]
        cols_ref[:, j, :] = jnp.broadcast_to(part, (cols_ref.shape[0], LANES))


def first_codes(rows, protos, groups):
    count, width = rows.shape
    columns = protos.shape[1]
    tiles = columns // LANES
    return pl.pallas_call(
        codes_kernel,
        grid=(count // CHUNK,),
        in_specs=[pl.BlockSpec((CHUNK, width), lambda i: (i, 0)), whole(protos.shape)],
        out_specs=(pl.BlockSpec((CHUNK, columns), lambda i: (i, 0)), whole((groups, tiles, LANES))),
        out_shape=(
            jax.ShapeDtypeStruct((count, columns), bf16),
            jax.ShapeDtypeStruct((groups, tiles, LANES), f32),
        ),
        scratch_shapes=[pltpu.VMEM((1, columns), f32)],
        compiler_params=params(),
        cost_estimate=cost(2 * count * width * columns, count * columns, 2 * count * columns),
        name="first_codes",
    )(rows, protos)


def row_pass_kernel(extra, *refs):
    recv_ref, codes_ref = refs[:2]
    out_ref, scale_ref = refs[-2:]
    step = pl.program_id(0)
    tiles = recv_ref.shape[1]

    @pl.when(step == 0)
    def _():
        mass = jnp.sum(recv_ref[...], axis=0)
        scale_ref[...] = split_rows(lane_row(1.0 / mass, 0, tiles))
        if extra:
            out_ref[:, 1, :, :] = jnp.broadcast_to(refs[2][...][None], out_ref.shape[:1] + out_ref.shape[2:])

    sums = lax.dot_general(scale_ref[...], codes_ref[...], NT, preferred_element_type=f32)
    sums = sums[0:1] + sums[1:2]
    lines = CHUNK // LANES
    block = jnp.concatenate([sums[:, j * LANES : (j + 1) * LANES] for j in range(lines)], axis=0)
    block = jnp.broadcast_to(block[None], (out_ref.shape[0], lines, LANES))
    out_ref[:, 0, pl.ds(step * lines, lines), :] = block


def row_pass(recv, codes, members, norm=None):
    count, columns = codes.shape
    lines = count // LANES
    extra = norm is not None
    parts = 2 if extra else 1
    shape = (members, parts, lines, LANES)
    return pl.pallas_call(
        functools.partial(row_pass_kernel, extra),
        grid=(count // CHUNK,),
        in_specs=[whole(recv.shape), pl.BlockSpec((CHUNK, columns), lambda i: (i, 0))]
        + ([whole(norm.shape)] if extra else []),
        out_specs=whole(shape),
        out_shape=jax.ShapeDtypeStruct(shape, f32),
        scratch_shapes=[pltpu.VMEM((16, columns), bf16)],
        compiler_params=params(),
        cost_estimate=cost(32 * count * columns, 0, 2 * count * columns),
        name="row_pass",
    )(recv, codes, *((norm,) if extra else ()))


def col_pass_kernel(recv_ref, codes_ref, cols_ref, scale_ref, total_ref):
    step = pl.program_id(0)
    lines = CHUNK // LANES

    @pl.when(step == 0)
    def _():
        scale_ref[...] = 1.0 / jnp.sum(recv_ref[:, 0], axis=0)
        total_ref[...] = jnp.zeros_like(total_ref)

    scale = split_rows(lane_row(scale_ref[pl.ds(step * lines, lines), :], 0, lines))
    total_ref[...] += jnp.dot(scale, codes_ref[...], preferred_element_type=f32)

    @pl.when(step == pl.num_programs(0) - 1)
    def _():
        spread_cols(total_ref[0:1] + total_ref[1:2], cols_ref)


def col_pass(recv, codes, groups):
    count, columns = codes.shape
    tiles = columns // LANES
    return pl.pallas_call(
        col_pass_kernel,
        grid=(count // CHUNK,),
        in_specs=[whole(recv.shape), pl.BlockSpec((CHUNK, columns), lambda i: (i, 0))],
        out_specs=whole((groups, tiles, LANES)),
        out_shape=jax.ShapeDtypeStruct((groups, tiles, LANES), f32),
        scratch_shapes=[pltpu.VMEM((count // LANES, LANES), f32), pltpu.VMEM((16, columns), f32)],
        compiler_params=params(),
        cost_estimate=cost(32 * count * columns, 0, 2 * count * columns),
        name="col_pass",
    )(recv, codes)


def student_kernel(rows_ref, protos_ref, expo_ref, norm_ref, turned_ref):
    step = pl.program_id(0)
    lines = CHUNK // LANES
    rows = rows_ref[...]
    scores = jnp.dot(rows, protos_ref[...], preferred_element_type=f32)
    expo = jnp.exp(scores * student_scale).astype(bf16)
    expo_ref[...] = expo
    sums = lax.dot_general(jnp.ones((16, expo.shape[1]), bf16), expo, NT, preferred_element_type=f32)[0:1]
    for j in range(lines):
        norm_ref[pl.ds(step * lines + j, 1), :] = sums[:, j * LANES : (j + 1) * LANES]
    turned_ref[...] = rows.T


def student_expo(rows, protos):
    count, width = rows.shape
    columns = protos.shape[1]
    return pl.pallas_call(
        student_kernel,
        grid=(count // CHUNK,),
        in_specs=[pl.BlockSpec((CHUNK, width), lambda i: (i, 0)), whole(protos.shape)],
        out_specs=(
            pl.BlockSpec((CHUNK, columns), lambda i: (i, 0)),
            whole((count // LANES, LANES)),
            pl.BlockSpec((width, CHUNK), lambda i: (0, i)),
        ),
        out_shape=(
            jax.ShapeDtypeStruct((count, columns), bf16),
            jax.ShapeDtypeStruct((count // LANES, LANES), f32),
            jax.ShapeDtypeStruct((width, count), bf16),
        ),
        compiler_params=params(),
        cost_estimate=cost(2 * count * width * columns, count * columns, 2 * count * columns),
        name="student_expo",
    )(rows, protos)


def grad_kernel(recv_ref, cols_ref, turned_ref, codes_ref, expo_ref, out_ref, scale_ref, teach_ref, stud_ref):
    step = pl.program_id(0)
    lines = CHUNK // LANES

    @pl.when(step == 0)
    def _():
        scale_ref[...] = 1.0 / jnp.sum(recv_ref[...], axis=0)
        teach_ref[...] = jnp.zeros_like(teach_ref)
        stud_ref[...] = jnp.zeros_like(stud_ref)

    turned = turned_ref[...].astype(f32)
    for part, (source, total) in enumerate(((codes_ref, teach_ref), (expo_ref, stud_ref))):
        scale = lane_row(scale_ref[part, pl.ds(step * lines, lines), :], 0, lines)
        total[...] += jnp.dot((turned * scale).astype(bf16), source[...], preferred_element_type=f32)

    @pl.when(step == pl.num_programs(0) - 1)
    def _():
        mass = jnp.sum(cols_ref[...], axis=0)
        col_scale = lane_row(1.0 / mass, 0, cols_ref.shape[1])
        grad = grad_factor * (stud_ref[...] - teach_ref[...] * col_scale)
        for piece in range(out_ref.shape[0]):
            out_ref[piece] = pack_piece(grad, piece, out_ref.shape[0]).astype(bf16)


def grad_pieces(recv, cols, turned, codes, expo):
    count, columns = codes.shape
    width = turned.shape[0]
    pieces = cols.shape[0]
    shape = (pieces, width // 2, 2 * columns // pieces)
    return pl.pallas_call(
        grad_kernel,
        grid=(count // CHUNK,),
        in_specs=[
            whole(recv.shape),
            whole(cols.shape),
            pl.BlockSpec((width, CHUNK), lambda i: (0, i)),
            pl.BlockSpec((CHUNK, columns), lambda i: (i, 0)),
            pl.BlockSpec((CHUNK, columns), lambda i: (i, 0)),
        ],
        out_specs=whole(shape),
        out_shape=jax.ShapeDtypeStruct(shape, bf16),
        scratch_shapes=[
            pltpu.VMEM(recv.shape[1:], f32),
            pltpu.VMEM((width, columns), f32),
            pltpu.VMEM((width, columns), f32),
        ],
        compiler_params=params(),
        cost_estimate=cost(4 * count * width * columns, 0, 4 * count * columns),
        name="grad_pieces",
    )(recv, cols, turned, codes, expo)


def back_kernel(recv_ref, weight_ref, out_ref):
    grad = jnp.sum(recv_ref[...].astype(f32), axis=0)
    weight = weight_ref[...]
    half = weight.shape[1] // 2

    def column_sum(values):
        total = jnp.sum(values, axis=0, keepdims=True)
        return total + jnp.concatenate([total[:, half:], total[:, :half]], axis=1)

    inverse = lax.rsqrt(column_sum(weight * weight) + epsilon)
    along = column_sum(grad * weight)
    out_ref[...] = (grad * inverse - weight * (inverse * inverse * inverse * along)).astype(bf16)


def weight_back(recv, weight):
    return pl.pallas_call(
        back_kernel,
        out_shape=jax.ShapeDtypeStruct(weight.shape, bf16),
        compiler_params=params(),
        name="weight_back",
    )(recv, weight)


def join_kernel(pieces_ref, out_ref):
    pieces, rows, lanes = pieces_ref.shape
    half = lanes // 2
    for pair in range(pieces // 2):
        left, right = pieces_ref[2 * pair], pieces_ref[2 * pair + 1]
        columns = pl.ds(pair * lanes, lanes)
        out_ref[:rows, columns] = jnp.concatenate([left[:, :half], right[:, :half]], axis=1)
        out_ref[rows:, columns] = jnp.concatenate([left[:, half:], right[:, half:]], axis=1)


def join_pieces(pieces):
    count, rows, lanes = pieces.shape
    return pl.pallas_call(
        join_kernel,
        out_shape=jax.ShapeDtypeStruct((2 * rows, count * lanes // 2), pieces.dtype),
        compiler_params=params(),
        name="join_pieces",
    )(pieces)


def exchange(values, axes):
    return lax.all_to_all(values, axes, 0, 0, tiled=True)


def shards(groups, members, teacher_patches, student_patches, mask_index, teacher_weight, student_weight):
    local = masked_rows(teacher_patches, student_patches, mask_index.reshape(1, -1))
    count, width = local.shape[1:]
    along_x = lax.all_gather(local, "x", axis=1, tiled=True)
    teach_rows = lax.all_gather(along_x[0], "z", axis=0, tiled=True)
    stud_x, teach_rows = lax.optimization_barrier((along_x[1], teach_rows))
    stud_rows = lax.all_gather(stud_x, "z", axis=0, tiled=True)
    teach_protos, stud_protos, packed = prototypes(teacher_weight, student_weight, groups)
    own_weight = lax.dynamic_index_in_dim(packed, lax.axis_index(GROUP), 0, keepdims=False)

    codes, cols = first_codes(teach_rows, teach_protos, groups)
    for sweep in range(ITERS):
        cols = exchange(cols, GROUP)
        if sweep < ITERS - 1:
            rows = exchange(row_pass(cols, codes, members), MEMBER)
            cols = col_pass(rows, codes, groups)
    expo, norm, turned = student_expo(stud_rows, stud_protos)
    rows = exchange(row_pass(cols, codes, members, norm), MEMBER)
    pieces = exchange(grad_pieces(rows, cols, turned, codes, expo), GROUP)
    return join_pieces(lax.all_gather(weight_back(pieces, own_weight), GROUP, axis=0))


def solution(mesh):
    groups, members = mesh.devices.shape
    split = Mesh(mesh.devices.reshape(8, 2, 8, 4), GROUP + MEMBER)
    rows = P(GROUP + MEMBER, None)
    columns = P(None, MEMBER)
    return jax.shard_map(
        functools.partial(shards, groups, members),
        mesh=split,
        in_specs=(rows, rows, P(GROUP + MEMBER), columns, columns),
        out_specs=columns,
        check_vma=False,
    )
```

```python
import functools
import math

import jax
import jax.numpy as jnp
from jax import lax
from jax.experimental import pallas as pl
from jax.experimental.pallas import tpu as pltpu
from jax.sharding import Mesh
from jax.sharding import PartitionSpec as P

GROUP = ("y", "core")
MEMBER = ("z", "x")
LANES = 128
CHUNK = 1024
VMEM_LIMIT = 28 * 1024 * 1024
LOG2E = math.log2(math.e)
IN_VMEM = pl.BlockSpec(memory_space=pltpu.VMEM)
IN_HBM = pl.BlockSpec(memory_space=pltpu.HBM)

epsilon = 1e-06
teacher_scale = 1.0 / 0.07
student_scale = 1.0 / 0.1
grad_factor = 256.0 / 0.1
NT = (((1,), (1,)), ((), ()))
TN = (((0,), (0,)), ((), ()))
f32 = jnp.float32
bf16 = jnp.bfloat16


def params():
    return pltpu.CompilerParams(vmem_limit_bytes=VMEM_LIMIT)


def cost(flops, transcendentals, nbytes):
    return pl.CostEstimate(flops=flops, transcendentals=transcendentals, bytes_accessed=nbytes)


def lane_row(block, start, count):
    return jnp.concatenate([block[start + j : start + j + 1, :] for j in range(count)], axis=1)


def rows_kernel(teacher_ref, student_ref, mask_ref, out_ref):
    patches = teacher_ref.shape[0]
    count = mask_ref.shape[1]
    chosen = lax.broadcasted_iota(jnp.int32, (patches, count), 0) == mask_ref[...]
    chosen = chosen.astype(f32).astype(bf16)
    for part, ref in enumerate((teacher_ref, student_ref)):
        rows = lax.dot_general(chosen, ref[...], TN, preferred_element_type=f32)
        square = jnp.sum(rows * rows, axis=1, keepdims=True)
        out_ref[part] = (rows * lax.rsqrt(square + epsilon)).astype(bf16)


def masked_rows(teacher, student, mask):
    count = mask.shape[1]
    return pl.pallas_call(
        rows_kernel,
        out_shape=jax.ShapeDtypeStruct((2, count, teacher.shape[1]), bf16),
        compiler_params=params(),
        name="masked_rows",
    )(teacher, student, mask)


def pack_piece(block, piece, pieces):
    rows, columns = block.shape
    width = columns // pieces
    part = block[:, piece * width : (piece + 1) * width]
    return jnp.concatenate([part[: rows // 2], part[rows // 2 :]], axis=1)


def protos_kernel(pieces, teacher_ref, student_ref, teach_ref, stud_ref, pack_ref):
    for source, out in ((teacher_ref, teach_ref), (student_ref, stud_ref)):
        values = source[...].astype(f32)
        square = jnp.sum(values * values, axis=0, keepdims=True)
        out[...] = (values * lax.rsqrt(square + epsilon)).astype(bf16)
    weight = student_ref[...].astype(f32)
    for piece in range(pieces):
        pack_ref[piece] = pack_piece(weight, piece, pieces)


def prototypes(teacher, student, pieces):
    rows, columns = teacher.shape
    like = jax.ShapeDtypeStruct(teacher.shape, bf16)
    return pl.pallas_call(
        functools.partial(protos_kernel, pieces),
        out_shape=(like, like, jax.ShapeDtypeStruct((pieces, rows // 2, 2 * columns // pieces), f32)),
        compiler_params=params(),
        name="prototypes",
    )(teacher, student)


def spread_cols(total, cols_ref):
    for j in range(cols_ref.shape[1]):
        part = total[:, j * LANES : (j + 1) * LANES]
        cols_ref[:, j, :] = jnp.broadcast_to(part, (cols_ref.shape[0], LANES))


def fetch(source, target, sem):
    copy = pltpu.make_async_copy(source, target, sem)
    copy.start()
    copy.wait()


def codes_kernel(rows_ref, protos_ref, codes_ref, cols_ref, held_ref, sem):
    fetch(rows_ref, held_ref, sem)
    scores = jnp.dot(held_ref[...], protos_ref[...], preferred_element_type=f32)
    codes = jnp.exp2(scores * (teacher_scale * LOG2E))
    codes_ref[...] = codes.astype(bf16)
    spread_cols(jnp.sum(codes, axis=0, keepdims=True), cols_ref)


def first_codes(rows, protos, groups):
    count, width = rows.shape
    columns = protos.shape[1]
    return pl.pallas_call(
        codes_kernel,
        in_specs=[IN_HBM, IN_VMEM],
        out_specs=(IN_VMEM, IN_VMEM),
        out_shape=(
            pltpu.VMEM((count, columns), bf16),
            jax.ShapeDtypeStruct((groups, columns // LANES, LANES), f32),
        ),
        scratch_shapes=[pltpu.VMEM((count, width), bf16), pltpu.SemaphoreType.DMA],
        compiler_params=params(),
        cost_estimate=cost(2 * count * width * columns, count * columns, 2 * count * columns),
        name="first_codes",
    )(rows, protos)


def sum_lanes(block):
    ones = jnp.ones((16, LANES), bf16)
    sums = lax.dot_general(ones, block.astype(bf16), NT, preferred_element_type=f32)[0:1]
    lines = block.shape[0] // LANES
    return jnp.concatenate([sums[:, j * LANES : (j + 1) * LANES] for j in range(lines)], axis=0)


def row_pass_kernel(extra, *refs):
    recv_ref, codes_ref, out_ref = refs[0], refs[1], refs[-1]
    tiles = recv_ref.shape[1]
    lines = CHUNK // LANES
    scale = lane_row(1.0 / jnp.sum(recv_ref[...], axis=0), 0, tiles)
    for i in range(codes_ref.shape[0] // CHUNK):
        part = None
        for j in range(tiles):
            columns = slice(j * LANES, (j + 1) * LANES)
            term = codes_ref[i * CHUNK : (i + 1) * CHUNK, columns].astype(f32) * scale[:, columns]
            part = term if part is None else part + term
        block = jnp.broadcast_to(sum_lanes(part)[None], (out_ref.shape[0], lines, LANES))
        out_ref[:, 0, i * lines : (i + 1) * lines, :] = block.astype(out_ref.dtype)
    if extra:
        norm = refs[2][...]
        out_ref[:, 1, :, :] = jnp.broadcast_to(norm[None], out_ref.shape[:1] + norm.shape).astype(out_ref.dtype)


def row_pass(recv, codes, members, norm=None):
    count, columns = codes.shape
    extra = () if norm is None else (norm,)
    shape = (members, 1 + len(extra), count // LANES, LANES)
    return pl.pallas_call(
        functools.partial(row_pass_kernel, bool(extra)),
        in_specs=[IN_VMEM] * (2 + len(extra)),
        out_specs=IN_VMEM,
        out_shape=jax.ShapeDtypeStruct(shape, bf16),
        compiler_params=params(),
        cost_estimate=cost(2 * count * columns, 0, 2 * count * columns),
        name="row_pass",
    )(recv, codes, *extra)


def col_pass_kernel(recv_ref, codes_ref, cols_ref):
    count, columns = codes_ref.shape
    lines = CHUNK // LANES
    scale = 1.0 / jnp.sum(recv_ref[:, 0].astype(f32), axis=0)
    ones = jnp.ones((16, LANES), bf16)
    first = lax.broadcasted_iota(jnp.int32, (16, CHUNK), 0) == 0
    total = jnp.zeros((16, columns), f32)
    for i in range(count // CHUNK):
        row = jnp.where(first, lane_row(scale, i * lines, lines), 0.0).astype(bf16)
        spread = lax.dot_general(row, ones, TN, preferred_element_type=f32).astype(bf16)
        for g in range(lines):
            parts = []
            for j in range(columns // LANES):
                part = None
                for q in range(LANES // 16):
                    at = g * LANES + q * 16
                    term = codes_ref[i * CHUNK + at : i * CHUNK + at + 16, j * LANES : (j + 1) * LANES]
                    term = term * spread[at : at + 16]
                    part = term if part is None else part + term
                parts.append(part.astype(f32))
            total = total + jnp.concatenate(parts, axis=1)
    spread_cols(jnp.sum(total, axis=0, keepdims=True), cols_ref)


def col_pass(recv, codes, groups):
    count, columns = codes.shape
    return pl.pallas_call(
        col_pass_kernel,
        in_specs=[IN_VMEM, IN_VMEM],
        out_specs=IN_VMEM,
        out_shape=jax.ShapeDtypeStruct((groups, columns // LANES, LANES), f32),
        compiler_params=params(),
        cost_estimate=cost(2 * count * columns, 0, 2 * count * columns),
        name="col_pass",
    )(recv, codes)


def student_kernel(rows_ref, protos_ref, expo_ref, norm_ref, turned_ref, held_ref, sem):
    fetch(rows_ref, held_ref, sem)
    count, columns = expo_ref.shape
    lines = CHUNK // LANES
    for i in range(count // CHUNK):
        span = slice(i * CHUNK, (i + 1) * CHUNK)
        rows = held_ref[span, :]
        scores = jnp.dot(rows, protos_ref[...], preferred_element_type=f32)
        expo = jnp.exp2(scores * (student_scale * LOG2E))
        expo_ref[span, :] = expo.astype(bf16)
        part = expo[:, :LANES]
        for j in range(1, columns // LANES):
            part = part + expo[:, j * LANES : (j + 1) * LANES]
        norm_ref[i * lines : (i + 1) * lines, :] = sum_lanes(part)
        turned_ref[:, span] = rows.T


def student_expo(rows, protos):
    count, width = rows.shape
    columns = protos.shape[1]
    return pl.pallas_call(
        student_kernel,
        in_specs=[IN_HBM, IN_VMEM],
        out_specs=(IN_VMEM, IN_VMEM, IN_VMEM),
        out_shape=(
            pltpu.VMEM((count, columns), bf16),
            jax.ShapeDtypeStruct((count // LANES, LANES), f32),
            pltpu.VMEM((width, count), bf16),
        ),
        scratch_shapes=[pltpu.VMEM((count, width), bf16), pltpu.SemaphoreType.DMA],
        compiler_params=params(),
        cost_estimate=cost(2 * count * width * columns, count * columns, 2 * count * columns),
        name="student_expo",
    )(rows, protos)


def scaled_product(recv_ref, part, turned_ref, codes_ref):
    scale = 1.0 / jnp.sum(recv_ref[:, part].astype(f32), axis=0)
    turned = (turned_ref[...].astype(f32) * lane_row(scale, 0, scale.shape[0])).astype(bf16)
    return jnp.dot(turned, codes_ref[...], preferred_element_type=f32)


def student_grad_kernel(recv_ref, turned_ref, expo_ref, out_ref):
    out_ref[...] = scaled_product(recv_ref, 1, turned_ref, expo_ref)


def student_grad(recv, turned, expo):
    count, columns = expo.shape
    width = turned.shape[0]
    return pl.pallas_call(
        student_grad_kernel,
        in_specs=[IN_VMEM] * 3,
        out_specs=IN_VMEM,
        out_shape=pltpu.VMEM((width, columns), f32),
        compiler_params=params(),
        cost_estimate=cost(2 * count * width * columns, 0, 2 * count * columns),
        name="student_grad",
    )(recv, turned, expo)


def grad_kernel(recv_ref, cols_ref, turned_ref, codes_ref, stud_ref, out_ref):
    teach = scaled_product(recv_ref, 0, turned_ref, codes_ref)
    mass = jnp.sum(cols_ref[...], axis=0)
    col_scale = lane_row(1.0 / mass, 0, cols_ref.shape[1])
    grad = grad_factor * (stud_ref[...] - teach * col_scale)
    for piece in range(out_ref.shape[0]):
        out_ref[piece] = pack_piece(grad, piece, out_ref.shape[0]).astype(bf16)


def grad_pieces(recv, cols, turned, codes, stud):
    count, columns = codes.shape
    width = turned.shape[0]
    pieces = cols.shape[0]
    return pl.pallas_call(
        grad_kernel,
        in_specs=[IN_VMEM] * 5,
        out_specs=IN_VMEM,
        out_shape=jax.ShapeDtypeStruct((pieces, width // 2, 2 * columns // pieces), bf16),
        compiler_params=params(),
        cost_estimate=cost(2 * count * width * columns, 0, 2 * count * columns),
        name="grad_pieces",
    )(recv, cols, turned, codes, stud)


def back_kernel(recv_ref, weight_ref, out_ref):
    grad = jnp.sum(recv_ref[...].astype(f32), axis=0)
    weight = weight_ref[...]
    half = weight.shape[1] // 2

    def column_sum(values):
        total = jnp.sum(values, axis=0, keepdims=True)
        return total + jnp.concatenate([total[:, half:], total[:, :half]], axis=1)

    inverse = lax.rsqrt(column_sum(weight * weight) + epsilon)
    along = column_sum(grad * weight)
    out_ref[...] = (grad * inverse - weight * (inverse * inverse * inverse * along)).astype(bf16)


def weight_back(recv, weight):
    return pl.pallas_call(
        back_kernel,
        out_shape=jax.ShapeDtypeStruct(weight.shape, bf16),
        compiler_params=params(),
        name="weight_back",
    )(recv, weight)


def join_kernel(pieces_ref, out_ref):
    pieces, rows, lanes = pieces_ref.shape
    half = lanes // 2
    for pair in range(pieces // 2):
        left, right = pieces_ref[2 * pair], pieces_ref[2 * pair + 1]
        columns = pl.ds(pair * lanes, lanes)
        out_ref[:rows, columns] = jnp.concatenate([left[:, :half], right[:, :half]], axis=1)
        out_ref[rows:, columns] = jnp.concatenate([left[:, half:], right[:, half:]], axis=1)


def join_pieces(pieces):
    count, rows, lanes = pieces.shape
    return pl.pallas_call(
        join_kernel,
        out_shape=jax.ShapeDtypeStruct((2 * rows, count * lanes // 2), pieces.dtype),
        compiler_params=params(),
        name="join_pieces",
    )(pieces)


def exchange(values, axes):
    return lax.all_to_all(values, axes, 0, 0, tiled=True)


def shards(groups, members, teacher_patches, student_patches, mask_index, teacher_weight, student_weight):
    local = masked_rows(teacher_patches, student_patches, mask_index.reshape(1, -1))
    count, width = local.shape[1:]
    along_x = lax.all_gather(local, "x", axis=1, tiled=True)
    teach_rows = lax.all_gather(along_x[0], "z", axis=0, tiled=True)
    stud_x, teach_rows = lax.optimization_barrier((along_x[1], teach_rows))
    stud_rows = lax.all_gather(stud_x, "z", axis=0, tiled=True)
    teach_protos, stud_protos, packed = prototypes(teacher_weight, student_weight, groups)
    own_weight = lax.dynamic_index_in_dim(packed, lax.axis_index(GROUP), 0, keepdims=False)

    codes, cols = first_codes(teach_rows, teach_protos, groups)
    cols = exchange(cols, GROUP)
    rows = exchange(row_pass(cols, codes, members), MEMBER)
    cols = exchange(col_pass(rows, codes, groups), GROUP)
    expo, norm, turned = student_expo(stud_rows, stud_protos)
    both = exchange(row_pass(cols, codes, members, norm), MEMBER)
    cols = exchange(col_pass(both, codes, groups), GROUP)
    stud = student_grad(both, turned, expo)
    rows = exchange(row_pass(cols, codes, members), MEMBER)
    pieces = exchange(grad_pieces(rows, cols, turned, codes, stud), GROUP)
    return join_pieces(lax.all_gather(weight_back(pieces, own_weight), GROUP, axis=0))


def solution(mesh):
    groups, members = mesh.devices.shape
    split = Mesh(mesh.devices.reshape(8, 2, 8, 4), GROUP + MEMBER)
    rows = P(GROUP + MEMBER, None)
    columns = P(None, MEMBER)
    return jax.shard_map(
        functools.partial(shards, groups, members),
        mesh=split,
        in_specs=(rows, rows, P(GROUP + MEMBER), columns, columns),
        out_specs=columns,
        check_vma=False,
    )
```

```python
import functools
import math

import jax
import jax.numpy as jnp
from jax import lax
from jax.experimental import pallas as pl
from jax.experimental.pallas import tpu as pltpu
from jax.sharding import Mesh
from jax.sharding import PartitionSpec as P

GROUP = ("y", "core")
MEMBER = ("z", "x")
LANES = 128
CHUNK = 1024
EXTRA = 8
VMEM_LIMIT = 16 * 1024 * 1024
LOG2E = math.log2(math.e)
IN_VMEM = pl.BlockSpec(memory_space=pltpu.VMEM)
IN_HBM = pl.BlockSpec(memory_space=pltpu.HBM)

epsilon = 1e-06
teacher_scale = 1.0 / 0.07
student_scale = 1.0 / 0.1
grad_factor = 256.0 / 0.1
NT = (((1,), (1,)), ((), ()))
TN = (((0,), (0,)), ((), ()))
f32 = jnp.float32
bf16 = jnp.bfloat16


def params():
    return pltpu.CompilerParams(vmem_limit_bytes=VMEM_LIMIT)


def cost(flops, transcendentals, nbytes):
    return pl.CostEstimate(flops=flops, transcendentals=transcendentals, bytes_accessed=nbytes)


def lane_row(block, start, count):
    return jnp.concatenate([block[start + j : start + j + 1, :] for j in range(count)], axis=1)


def in_hbm(values):
    return pltpu.with_memory_space_constraint(values, pltpu.HBM)


def prepare_kernel(*refs):
    sources, (teach_ref, stud_ref, teach_protos_ref, stud_protos_ref), held, sems = refs[:5], refs[5:9], refs[9:14], refs[14]
    copies = [pltpu.make_async_copy(source, to, sems.at[i]) for i, (source, to) in enumerate(zip(sources, held))]
    for copy in copies:
        copy.start()
    copies[0].wait()
    count = held[0].shape[1]
    patches = held[1].shape[0]
    chosen = lax.broadcasted_iota(jnp.int32, (patches, count), 0) == held[0][...]
    chosen = chosen.astype(f32).astype(bf16)
    for part, out in ((1, teach_ref), (2, stud_ref)):
        copies[part].wait()
        rows = lax.dot_general(chosen, held[part][...], TN, preferred_element_type=f32)
        square = jnp.sum(rows * rows, axis=1, keepdims=True)
        rows = (rows * lax.rsqrt(square + epsilon)).astype(bf16)
        out[...] = jnp.broadcast_to(rows[None], out.shape) if part == 1 else rows
    for part, out in ((3, teach_protos_ref), (4, stud_protos_ref)):
        copies[part].wait()
        values = held[part][...].astype(f32)
        square = jnp.sum(values * values, axis=0, keepdims=True)
        out[...] = (values * lax.rsqrt(square + epsilon)).astype(bf16)


def prepare(mask, teacher, student, teacher_weight, student_weight, copies):
    sources = (mask, teacher, student, teacher_weight, student_weight)
    count, width = mask.shape[1], teacher.shape[1]
    return pl.pallas_call(
        prepare_kernel,
        in_specs=[IN_HBM] * 5,
        out_specs=(IN_VMEM,) * 4,
        out_shape=(
            jax.ShapeDtypeStruct((copies, count, width), bf16),
            jax.ShapeDtypeStruct((count, width), bf16),
            jax.ShapeDtypeStruct(teacher_weight.shape, bf16),
            jax.ShapeDtypeStruct(student_weight.shape, bf16),
        ),
        scratch_shapes=[pltpu.VMEM(source.shape, source.dtype) for source in sources] + [pltpu.SemaphoreType.DMA((5,))],
        compiler_params=params(),
        name="prepare",
    )(*map(in_hbm, sources))


def pack_piece(block, piece, pieces):
    rows, columns = block.shape
    width = columns // pieces
    part = block[:, piece * width : (piece + 1) * width]
    return jnp.concatenate([part[: rows // 2], part[rows // 2 :]], axis=1)


def spread_cols(total, cols_ref):
    for j in range(cols_ref.shape[1]):
        part = total[:, j * LANES : (j + 1) * LANES]
        cols_ref[:, j, :] = jnp.broadcast_to(part, (cols_ref.shape[0], LANES))


def fetch(source, target, sem):
    copy = pltpu.make_async_copy(source, target, sem)
    copy.start()
    copy.wait()


class Blocks:
    def __init__(self, source, held=None, sems=None):
        self.count = source.shape[0] // CHUNK
        self.block = source if held is None else held
        self.copies = []
        if held is not None:
            for i in range(self.count):
                span = pl.ds(i * CHUNK, CHUNK)
                self.copies.append(pltpu.make_async_copy(source.at[span, :], held.at[span, :], sems.at[i]))
            for copy in self.copies:
                copy.start()

    def ready(self, i):
        if self.copies:
            self.copies[i].wait()


def held_blocks(shape):
    return [pltpu.VMEM(shape, bf16), pltpu.SemaphoreType.DMA((shape[0] // CHUNK,))]


def codes_kernel(rows_ref, protos_ref, codes_ref, cols_ref):
    scores = jnp.dot(rows_ref[...], protos_ref[...], preferred_element_type=f32)
    codes = jnp.exp2(scores * (teacher_scale * LOG2E))
    codes_ref[...] = codes.astype(bf16)
    spread_cols(jnp.sum(codes, axis=0, keepdims=True), cols_ref)


def first_codes(rows, protos, groups):
    count, width = rows.shape
    columns = protos.shape[1]
    return pl.pallas_call(
        codes_kernel,
        in_specs=[IN_VMEM, IN_VMEM],
        out_specs=(IN_VMEM, IN_VMEM),
        out_shape=(
            pltpu.VMEM((count, columns), bf16),
            jax.ShapeDtypeStruct((groups, columns // LANES, LANES), f32),
        ),
        compiler_params=params(),
        cost_estimate=cost(2 * count * width * columns, count * columns, 2 * count * columns),
        name="first_codes",
    )(rows, protos)


def sum_lanes(block):
    ones = jnp.ones((16, LANES), bf16)
    sums = lax.dot_general(ones, block.astype(bf16), NT, preferred_element_type=f32)[0:1]
    lines = block.shape[0] // LANES
    return jnp.concatenate([sums[:, j * LANES : (j + 1) * LANES] for j in range(lines)], axis=0)


def row_pass_kernel(stage, *refs):
    recv_ref, codes_ref = refs[:2]
    norm_ref, refs = (refs[2], refs[3:]) if stage else (None, refs[2:])
    out_ref, held = refs[0], refs[1:]
    blocks = Blocks(codes_ref, *held)
    tiles = recv_ref.shape[1]
    lines = CHUNK // LANES
    scale = lane_row(1.0 / jnp.sum(recv_ref[...], axis=0), 0, tiles)
    for i in range(blocks.count):
        blocks.ready(i)
        part = None
        for j in range(tiles):
            columns = slice(j * LANES, (j + 1) * LANES)
            term = blocks.block[i * CHUNK : (i + 1) * CHUNK, columns].astype(f32) * scale[:, columns]
            part = term if part is None else part + term
        block = jnp.broadcast_to(sum_lanes(part)[None], (out_ref.shape[0], lines, LANES))
        out_ref[:, i * lines : (i + 1) * lines, :] = block.astype(bf16)
    first = blocks.count * lines
    if stage == 1:
        for member in range(out_ref.shape[0]):
            line = norm_ref[member : member + 1, :]
            out_ref[member, first:, :] = jnp.broadcast_to(line, (EXTRA, LANES)).astype(bf16)
    if stage == 2:
        total = jnp.sum(norm_ref[:, first : first + 1, :].astype(f32), axis=0)
        high = total.astype(bf16).astype(f32)
        index = lax.broadcasted_iota(jnp.int32, (EXTRA, LANES), 0)
        extra = jnp.where(index == 0, high, jnp.where(index == 1, total - high, 0.0)).astype(bf16)
        out_ref[:, first:, :] = jnp.broadcast_to(extra[None], (out_ref.shape[0], EXTRA, LANES))


def row_pass(recv, codes, members, stream, norm=None, stage=0):
    count, columns = codes.shape
    lines = count // LANES + (EXTRA if stage else 0)
    return pl.pallas_call(
        functools.partial(row_pass_kernel, stage),
        in_specs=[IN_VMEM, IN_HBM if stream else IN_VMEM] + ([IN_VMEM] if stage else []),
        out_specs=IN_VMEM,
        out_shape=jax.ShapeDtypeStruct((members, lines, LANES), bf16),
        scratch_shapes=held_blocks(codes.shape) if stream else [],
        compiler_params=params(),
        cost_estimate=cost(2 * count * columns, 0, 2 * count * columns),
        name="row_pass",
    )(recv, in_hbm(codes) if stream else codes, *((norm,) if stage else ()))


def col_pass_kernel(recv_ref, codes_ref, cols_ref):
    count, columns = codes_ref.shape
    lines = CHUNK // LANES
    scale = 1.0 / jnp.sum(recv_ref[:, : count // LANES, :].astype(f32), axis=0)
    ones = jnp.ones((16, LANES), bf16)
    first = lax.broadcasted_iota(jnp.int32, (16, CHUNK), 0) == 0
    total = jnp.zeros((16, columns), f32)
    for i in range(count // CHUNK):
        row = jnp.where(first, lane_row(scale, i * lines, lines), 0.0).astype(bf16)
        spread = lax.dot_general(row, ones, TN, preferred_element_type=f32).astype(bf16)
        for g in range(lines):
            parts = []
            for j in range(columns // LANES):
                part = None
                for q in range(LANES // 16):
                    at = g * LANES + q * 16
                    term = codes_ref[i * CHUNK + at : i * CHUNK + at + 16, j * LANES : (j + 1) * LANES]
                    term = term * spread[at : at + 16]
                    part = term if part is None else part + term
                parts.append(part.astype(f32))
            total = total + jnp.concatenate(parts, axis=1)
    spread_cols(jnp.sum(total, axis=0, keepdims=True), cols_ref)


def col_pass(recv, codes, groups):
    count, columns = codes.shape
    return pl.pallas_call(
        col_pass_kernel,
        in_specs=[IN_VMEM, IN_VMEM],
        out_specs=IN_VMEM,
        out_shape=jax.ShapeDtypeStruct((groups, columns // LANES, LANES), f32),
        compiler_params=params(),
        cost_estimate=cost(2 * count * columns, 0, 2 * count * columns),
        name="col_pass",
    )(recv, codes)


def student_kernel(rows_ref, protos_ref, expo_ref, norm_ref, turned_ref, held_ref, sem):
    fetch(rows_ref, held_ref, sem)
    count, columns = expo_ref.shape
    lines = CHUNK // LANES
    for i in range(count // CHUNK):
        span = slice(i * CHUNK, (i + 1) * CHUNK)
        rows = held_ref[span, :]
        scores = jnp.dot(rows, protos_ref[...], preferred_element_type=f32)
        expo = jnp.exp2(scores * (student_scale * LOG2E))
        expo_ref[span, :] = expo.astype(bf16)
        part = expo[:, :LANES]
        for j in range(1, columns // LANES):
            part = part + expo[:, j * LANES : (j + 1) * LANES]
        norm_ref[i * lines : (i + 1) * lines, :] = sum_lanes(part)
        turned_ref[:, span] = rows.T


def student_expo(rows, protos):
    count, width = rows.shape
    columns = protos.shape[1]
    return pl.pallas_call(
        student_kernel,
        in_specs=[IN_HBM, IN_VMEM],
        out_specs=(IN_VMEM, IN_VMEM, IN_VMEM),
        out_shape=(
            jax.ShapeDtypeStruct((count, columns), bf16),
            jax.ShapeDtypeStruct((count // LANES, LANES), f32),
            jax.ShapeDtypeStruct((width, count), bf16),
        ),
        scratch_shapes=[pltpu.VMEM((count, width), bf16), pltpu.SemaphoreType.DMA],
        compiler_params=params(),
        cost_estimate=cost(2 * count * width * columns, count * columns, 2 * count * columns),
        name="student_expo",
    )(in_hbm(rows), protos)


def scaled_product(scale, turned_ref, blocks):
    lines = CHUNK // LANES
    total = None
    for i in range(blocks.count):
        span = slice(i * CHUNK, (i + 1) * CHUNK)
        turned = (turned_ref[:, span].astype(f32) * lane_row(scale, i * lines, lines)).astype(bf16)
        blocks.ready(i)
        term = jnp.dot(turned, blocks.block[span, :], preferred_element_type=f32)
        total = term if total is None else total + term
    return total


def grad_kernel(recv_ref, cols_ref, turned_ref, codes_ref, expo_ref, out_ref, *held):
    stud_blocks = Blocks(expo_ref, *held)
    members = recv_ref.shape[0]
    lines = codes_ref.shape[0] // LANES
    row_scale = 1.0 / jnp.sum(recv_ref[:, :lines, :].astype(f32), axis=0)
    norm = jnp.concatenate(
        [recv_ref[m, lines : lines + 1, :].astype(f32) + recv_ref[m, lines + 1 : lines + 2, :].astype(f32) for m in range(members)],
        axis=0,
    )
    teach = scaled_product(row_scale, turned_ref, Blocks(codes_ref))
    mass = jnp.sum(cols_ref[...], axis=0)
    teach = teach * lane_row(1.0 / mass, 0, cols_ref.shape[1])
    grad = grad_factor * (scaled_product(1.0 / norm, turned_ref, stud_blocks) - teach)
    for piece in range(out_ref.shape[0]):
        out_ref[piece] = pack_piece(grad, piece, out_ref.shape[0]).astype(bf16)


def grad_pieces(recv, cols, turned, codes, expo):
    count, columns = codes.shape
    width = turned.shape[0]
    pieces = cols.shape[0]
    return pl.pallas_call(
        grad_kernel,
        in_specs=[IN_VMEM, IN_VMEM, IN_VMEM, IN_VMEM, IN_HBM],
        out_specs=IN_VMEM,
        out_shape=jax.ShapeDtypeStruct((pieces, width // 2, 2 * columns // pieces), bf16),
        scratch_shapes=held_blocks(expo.shape),
        compiler_params=params(),
        cost_estimate=cost(4 * count * width * columns, 0, 4 * count * columns),
        name="grad_pieces",
    )(recv, cols, turned, codes, in_hbm(expo))


def back_kernel(index_ref, recv_ref, weight_ref, out_ref):
    half = out_ref.shape[1] // 2
    index = index_ref[0]
    block = weight_ref[:, pl.ds(pl.multiple_of(index // 2 * LANES, LANES), LANES)].astype(f32)
    block = jnp.where(index % 2 == 0, block[:, :half], block[:, half:])
    rows = block.shape[0] // 2
    weight = jnp.concatenate([block[:rows], block[rows:]], axis=1)
    grad = jnp.sum(recv_ref[...].astype(f32), axis=0)

    def column_sum(values):
        total = jnp.sum(values, axis=0, keepdims=True)
        return total + jnp.concatenate([total[:, half:], total[:, :half]], axis=1)

    inverse = lax.rsqrt(column_sum(weight * weight) + epsilon)
    along = column_sum(grad * weight)
    out_ref[...] = (grad * inverse - weight * (inverse * inverse * inverse * along)).astype(bf16)


def weight_back(index, recv, weight):
    return pl.pallas_call(
        back_kernel,
        in_specs=[pl.BlockSpec(memory_space=pltpu.SMEM), IN_VMEM, IN_VMEM],
        out_specs=IN_VMEM,
        out_shape=jax.ShapeDtypeStruct(recv.shape[1:], bf16),
        compiler_params=params(),
        name="weight_back",
    )(index, recv, weight)


def join_kernel(pieces_ref, out_ref):
    pieces, rows, lanes = pieces_ref.shape
    half = lanes // 2
    for pair in range(pieces // 2):
        left, right = pieces_ref[2 * pair], pieces_ref[2 * pair + 1]
        columns = pl.ds(pair * lanes, lanes)
        out_ref[:rows, columns] = jnp.concatenate([left[:, :half], right[:, :half]], axis=1)
        out_ref[rows:, columns] = jnp.concatenate([left[:, half:], right[:, half:]], axis=1)


def join_pieces(pieces):
    count, rows, lanes = pieces.shape
    return pl.pallas_call(
        join_kernel,
        out_shape=jax.ShapeDtypeStruct((2 * rows, count * lanes // 2), pieces.dtype),
        compiler_params=params(),
        name="join_pieces",
    )(pieces)


def exchange(values, axes):
    return lax.all_to_all(values, axes, 0, 0, tiled=True)


def shards(groups, members, teacher_patches, student_patches, mask_index, teacher_weight, student_weight):
    along_z, along_x = lax.axis_size("z"), lax.axis_size("x")
    own, stud_own, teach_protos, stud_protos = prepare(
        mask_index.reshape(1, -1), teacher_patches, student_patches, teacher_weight, student_weight, along_z
    )
    width = own.shape[2]
    stud_rows = lax.all_gather(stud_own, ("x", "z"), axis=0, tiled=True)
    line = exchange(own, "z")
    line = jnp.broadcast_to(line.reshape(1, -1, width), (along_x, line.shape[0] * line.shape[1], width))
    teach_rows = exchange(line, "x").reshape(-1, width)

    codes, cols = first_codes(teach_rows, teach_protos, groups)
    cols = exchange(cols, GROUP)
    rows = exchange(row_pass(cols, codes, members, False), MEMBER)
    cols = exchange(col_pass(rows, codes, groups), GROUP)
    expo, norm, turned = student_expo(stud_rows, stud_protos)
    rows = exchange(row_pass(cols, codes, members, True, norm, 1), MEMBER)
    cols = exchange(col_pass(rows, codes, groups), GROUP)
    rows = exchange(row_pass(cols, codes, members, False, rows, 2), MEMBER)
    pieces = exchange(grad_pieces(rows, cols, turned, codes, expo), GROUP)
    index = lax.axis_index(GROUP).reshape(1)
    back = weight_back(index, pieces, student_weight)
    return join_pieces(lax.all_gather(back, GROUP, axis=0))


def solution(mesh):
    groups, members = mesh.devices.shape
    split = Mesh(mesh.devices.reshape(8, 2, 8, 4), GROUP + MEMBER)
    rows = P(GROUP + MEMBER, None)
    columns = P(None, MEMBER)
    return jax.shard_map(
        functools.partial(shards, groups, members),
        mesh=split,
        in_specs=(rows, rows, P(GROUP + MEMBER), columns, columns),
        out_specs=columns,
        check_vma=False,
    )
```

```python
import functools
import math

import jax
import jax.numpy as jnp
from jax import lax
from jax.experimental import pallas as pl
from jax.experimental.pallas import tpu as pltpu
from jax.sharding import Mesh
from jax.sharding import PartitionSpec as P

GROUP = ("y", "core")
MEMBER = ("z", "x")
LANES = 128
CHUNK = 1024
EXTRA = 8
VMEM_LIMIT = 28 * 1024 * 1024
LOG2E = math.log2(math.e)
IN_VMEM = pl.BlockSpec(memory_space=pltpu.VMEM)
IN_HBM = pl.BlockSpec(memory_space=pltpu.HBM)

epsilon = 1e-06
teacher_scale = 1.0 / 0.07
student_scale = 1.0 / 0.1
grad_factor = 256.0 / 0.1
NT = (((1,), (1,)), ((), ()))
TN = (((0,), (0,)), ((), ()))
f32 = jnp.float32
bf16 = jnp.bfloat16


def params():
    return pltpu.CompilerParams(vmem_limit_bytes=VMEM_LIMIT)


def cost(flops, transcendentals, nbytes):
    return pl.CostEstimate(flops=flops, transcendentals=transcendentals, bytes_accessed=nbytes)


def lane_row(block, start, count):
    return jnp.concatenate([block[start + j : start + j + 1, :] for j in range(count)], axis=1)


def in_hbm(values):
    return pltpu.with_memory_space_constraint(values, pltpu.HBM)


def prepare_kernel(*refs):
    sources, (teach_ref, stud_ref, teach_protos_ref, stud_protos_ref), held, sems = refs[:5], refs[5:9], refs[9:14], refs[14]
    copies = [pltpu.make_async_copy(source, to, sems.at[i]) for i, (source, to) in enumerate(zip(sources, held))]
    for copy in copies:
        copy.start()
    copies[0].wait()
    count = held[0].shape[1]
    patches = held[1].shape[0]
    chosen = lax.broadcasted_iota(jnp.int32, (patches, count), 0) == held[0][...]
    chosen = chosen.astype(f32).astype(bf16)
    for part, out in ((1, teach_ref), (2, stud_ref)):
        copies[part].wait()
        rows = lax.dot_general(chosen, held[part][...], TN, preferred_element_type=f32)
        square = jnp.sum(rows * rows, axis=1, keepdims=True)
        rows = (rows * lax.rsqrt(square + epsilon)).astype(bf16)
        out[...] = jnp.broadcast_to(rows[None], out.shape) if part == 1 else rows
    for part, out in ((3, teach_protos_ref), (4, stud_protos_ref)):
        copies[part].wait()
        values = held[part][...].astype(f32)
        square = jnp.sum(values * values, axis=0, keepdims=True)
        out[...] = (values * lax.rsqrt(square + epsilon)).astype(bf16)


def prepare(mask, teacher, student, teacher_weight, student_weight, copies):
    sources = (mask, teacher, student, teacher_weight, student_weight)
    count, width = mask.shape[1], teacher.shape[1]
    return pl.pallas_call(
        prepare_kernel,
        in_specs=[IN_HBM] * 5,
        out_specs=(IN_VMEM,) * 4,
        out_shape=(
            jax.ShapeDtypeStruct((copies, count, width), bf16),
            jax.ShapeDtypeStruct((count, width), bf16),
            jax.ShapeDtypeStruct(teacher_weight.shape, bf16),
            jax.ShapeDtypeStruct(student_weight.shape, bf16),
        ),
        scratch_shapes=[pltpu.VMEM(source.shape, source.dtype) for source in sources] + [pltpu.SemaphoreType.DMA((5,))],
        compiler_params=params(),
        name="prepare",
    )(*map(in_hbm, sources))


def pack_piece(block, piece, pieces):
    rows, columns = block.shape
    width = columns // pieces
    part = block[:, piece * width : (piece + 1) * width]
    return jnp.concatenate([part[: rows // 2], part[rows // 2 :]], axis=1)


def spread_cols(total, cols_ref):
    for j in range(cols_ref.shape[1]):
        part = total[:, j * LANES : (j + 1) * LANES]
        cols_ref[:, j, :] = jnp.broadcast_to(part, (cols_ref.shape[0], LANES)).astype(bf16)


class Blocks:
    def __init__(self, source, held=None, sems=None):
        self.count = source.shape[0] // CHUNK
        self.block = source if held is None else held
        self.copies = []
        if held is not None:
            for i in range(self.count):
                span = pl.ds(i * CHUNK, CHUNK)
                self.copies.append(pltpu.make_async_copy(source.at[span, :], held.at[span, :], sems.at[i]))
            for copy in self.copies:
                copy.start()

    def ready(self, i):
        if self.copies:
            self.copies[i].wait()


def held_blocks(shape):
    return [pltpu.VMEM(shape, bf16), pltpu.SemaphoreType.DMA((shape[0] // CHUNK,))]


def codes_kernel(rows_ref, protos_ref, codes_ref, cols_ref):
    scores = jnp.dot(rows_ref[...], protos_ref[...], preferred_element_type=f32)
    codes = jnp.exp2(scores * (teacher_scale * LOG2E))
    codes_ref[...] = codes.astype(bf16)
    spread_cols(jnp.sum(codes, axis=0, keepdims=True), cols_ref)


def first_codes(rows, protos, groups):
    count, width = rows.shape
    columns = protos.shape[1]
    return pl.pallas_call(
        codes_kernel,
        in_specs=[IN_VMEM, IN_VMEM],
        out_specs=(IN_VMEM, IN_VMEM),
        out_shape=(
            pltpu.VMEM((count, columns), bf16),
            jax.ShapeDtypeStruct((groups, columns // LANES, LANES), bf16),
        ),
        compiler_params=params(),
        cost_estimate=cost(2 * count * width * columns, count * columns, 2 * count * columns),
        name="first_codes",
    )(rows, protos)


def sum_lanes(block):
    ones = jnp.ones((16, LANES), bf16)
    sums = lax.dot_general(ones, block.astype(bf16), NT, preferred_element_type=f32)[0:1]
    lines = block.shape[0] // LANES
    return jnp.concatenate([sums[:, j * LANES : (j + 1) * LANES] for j in range(lines)], axis=0)


def row_pass_kernel(stage, *refs):
    recv_ref, codes_ref = refs[:2]
    norm_ref, refs = (refs[2], refs[3:]) if stage else (None, refs[2:])
    out_ref, held = refs[0], refs[1:]
    blocks = Blocks(codes_ref, *held)
    tiles = recv_ref.shape[1]
    lines = CHUNK // LANES
    scale = lane_row(1.0 / jnp.sum(recv_ref[...].astype(f32), axis=0), 0, tiles)
    for i in range(blocks.count):
        blocks.ready(i)
        part = None
        for j in range(tiles):
            columns = slice(j * LANES, (j + 1) * LANES)
            term = blocks.block[i * CHUNK : (i + 1) * CHUNK, columns].astype(f32) * scale[:, columns]
            part = term if part is None else part + term
        block = jnp.broadcast_to(sum_lanes(part)[None], (out_ref.shape[0], lines, LANES))
        out_ref[:, i * lines : (i + 1) * lines, :] = block.astype(bf16)
    first = blocks.count * lines
    if stage == 1:
        for member in range(out_ref.shape[0]):
            line = norm_ref[member : member + 1, :]
            out_ref[member, first:, :] = jnp.broadcast_to(line, (EXTRA, LANES)).astype(bf16)
    if stage == 2:
        total = jnp.sum(norm_ref[:, first : first + 1, :].astype(f32), axis=0)
        high = total.astype(bf16).astype(f32)
        index = lax.broadcasted_iota(jnp.int32, (EXTRA, LANES), 0)
        extra = jnp.where(index == 0, high, jnp.where(index == 1, total - high, 0.0)).astype(bf16)
        out_ref[:, first:, :] = jnp.broadcast_to(extra[None], (out_ref.shape[0], EXTRA, LANES))


def row_pass(recv, codes, members, stream, norm=None, stage=0):
    count, columns = codes.shape
    lines = count // LANES + (EXTRA if stage else 0)
    return pl.pallas_call(
        functools.partial(row_pass_kernel, stage),
        in_specs=[IN_VMEM, IN_HBM if stream else IN_VMEM] + ([IN_VMEM] if stage else []),
        out_specs=IN_VMEM,
        out_shape=jax.ShapeDtypeStruct((members, lines, LANES), bf16),
        scratch_shapes=held_blocks(codes.shape) if stream else [],
        compiler_params=params(),
        cost_estimate=cost(2 * count * columns, 0, 2 * count * columns),
        name="row_pass",
    )(recv, in_hbm(codes) if stream else codes, *((norm,) if stage else ()))


def col_pass_kernel(recv_ref, codes_ref, cols_ref):
    count, columns = codes_ref.shape
    lines = CHUNK // LANES
    scale = 1.0 / jnp.sum(recv_ref[:, : count // LANES, :].astype(f32), axis=0)
    ones = jnp.ones((16, LANES), bf16)
    first = lax.broadcasted_iota(jnp.int32, (16, CHUNK), 0) == 0
    total = jnp.zeros((16, columns), f32)
    for i in range(count // CHUNK):
        row = jnp.where(first, lane_row(scale, i * lines, lines), 0.0).astype(bf16)
        spread = lax.dot_general(row, ones, TN, preferred_element_type=f32).astype(bf16)
        for g in range(lines):
            parts = []
            for j in range(columns // LANES):
                part = None
                for q in range(LANES // 16):
                    at = g * LANES + q * 16
                    term = codes_ref[i * CHUNK + at : i * CHUNK + at + 16, j * LANES : (j + 1) * LANES]
                    term = term * spread[at : at + 16]
                    part = term if part is None else part + term
                parts.append(part.astype(f32))
            total = total + jnp.concatenate(parts, axis=1)
    spread_cols(jnp.sum(total, axis=0, keepdims=True), cols_ref)


def col_pass(recv, codes, groups):
    count, columns = codes.shape
    return pl.pallas_call(
        col_pass_kernel,
        in_specs=[IN_VMEM, IN_VMEM],
        out_specs=IN_VMEM,
        out_shape=jax.ShapeDtypeStruct((groups, columns // LANES, LANES), bf16),
        compiler_params=params(),
        cost_estimate=cost(2 * count * columns, 0, 2 * count * columns),
        name="col_pass",
    )(recv, codes)


def student_kernel(rows_ref, protos_ref, expo_ref, norm_ref, turned_ref, held, made, turned, in_sems, out_sems):
    count, columns = expo_ref.shape
    lines = CHUNK // LANES
    spans = [pl.ds(i * CHUNK, CHUNK) for i in range(count // CHUNK)]
    fetches = [pltpu.make_async_copy(rows_ref.at[span, :], held.at[span, :], in_sems.at[i]) for i, span in enumerate(spans)]
    for fetch in fetches:
        fetch.start()
    sends = []
    for i, span in enumerate(spans):
        fetches[i].wait()
        rows = held[span, :]
        scores = jnp.dot(rows, protos_ref[...], preferred_element_type=f32)
        expo = jnp.exp2(scores * (student_scale * LOG2E))
        made[span, :] = expo.astype(bf16)
        sends.append(pltpu.make_async_copy(made.at[span, :], expo_ref.at[span, :], out_sems.at[2 * i]))
        sends[-1].start()
        part = expo[:, :LANES]
        for j in range(1, columns // LANES):
            part = part + expo[:, j * LANES : (j + 1) * LANES]
        norm_ref[i * lines : (i + 1) * lines, :] = sum_lanes(part)
        turned[:, span] = rows.T
        sends.append(pltpu.make_async_copy(turned.at[:, span], turned_ref.at[:, span], out_sems.at[2 * i + 1]))
        sends[-1].start()
    for send in sends:
        send.wait()


def student_expo(rows, protos):
    count, width = rows.shape
    columns = protos.shape[1]
    return pl.pallas_call(
        student_kernel,
        in_specs=[IN_HBM, IN_VMEM],
        out_specs=(IN_HBM, IN_VMEM, IN_HBM),
        out_shape=(
            pltpu.HBM((count, columns), bf16),
            jax.ShapeDtypeStruct((count // LANES, LANES), f32),
            pltpu.HBM((width, count), bf16),
        ),
        scratch_shapes=[
            pltpu.VMEM((count, width), bf16),
            pltpu.VMEM((count, columns), bf16),
            pltpu.VMEM((width, count), bf16),
            pltpu.SemaphoreType.DMA((count // CHUNK,)),
            pltpu.SemaphoreType.DMA((2 * count // CHUNK,)),
        ],
        compiler_params=params(),
        cost_estimate=cost(2 * count * width * columns, count * columns, 2 * count * columns),
        name="student_expo",
    )(in_hbm(rows), protos)


def scaled_product(scale, turned_ref, codes_ref):
    turned = (turned_ref[...].astype(f32) * lane_row(scale, 0, scale.shape[0])).astype(bf16)
    return jnp.dot(turned, codes_ref[...], preferred_element_type=f32)


def grad_kernel(recv_ref, cols_ref, turned_ref, codes_ref, expo_ref, out_ref):
    members = recv_ref.shape[0]
    lines = codes_ref.shape[0] // LANES
    row_scale = 1.0 / jnp.sum(recv_ref[:, :lines, :].astype(f32), axis=0)
    norm = jnp.concatenate(
        [recv_ref[m, lines : lines + 1, :].astype(f32) + recv_ref[m, lines + 1 : lines + 2, :].astype(f32) for m in range(members)],
        axis=0,
    )
    mass = jnp.sum(cols_ref[...].astype(f32), axis=0)
    teach = scaled_product(row_scale, turned_ref, codes_ref) * lane_row(1.0 / mass, 0, cols_ref.shape[1])
    grad = grad_factor * (scaled_product(1.0 / norm, turned_ref, expo_ref) - teach)
    for piece in range(out_ref.shape[0]):
        out_ref[piece] = pack_piece(grad, piece, out_ref.shape[0]).astype(bf16)


def grad_pieces(recv, cols, turned, codes, expo):
    count, columns = codes.shape
    width = turned.shape[0]
    pieces = cols.shape[0]
    return pl.pallas_call(
        grad_kernel,
        in_specs=[IN_VMEM] * 5,
        out_specs=IN_VMEM,
        out_shape=jax.ShapeDtypeStruct((pieces, width // 2, 2 * columns // pieces), bf16),
        compiler_params=params(),
        cost_estimate=cost(4 * count * width * columns, 0, 4 * count * columns),
        name="grad_pieces",
    )(recv, cols, turned, codes, expo)


def back_kernel(index_ref, recv_ref, weight_ref, out_ref):
    half = out_ref.shape[1] // 2
    index = index_ref[0]
    block = weight_ref[:, pl.ds(pl.multiple_of(index // 2 * LANES, LANES), LANES)].astype(f32)
    block = jnp.where(index % 2 == 0, block[:, :half], block[:, half:])
    rows = block.shape[0] // 2
    weight = jnp.concatenate([block[:rows], block[rows:]], axis=1)
    grad = jnp.sum(recv_ref[...].astype(f32), axis=0)

    def column_sum(values):
        total = jnp.sum(values, axis=0, keepdims=True)
        return total + jnp.concatenate([total[:, half:], total[:, :half]], axis=1)

    inverse = lax.rsqrt(column_sum(weight * weight) + epsilon)
    along = column_sum(grad * weight)
    out_ref[...] = (grad * inverse - weight * (inverse * inverse * inverse * along)).astype(bf16)


def weight_back(index, recv, weight):
    return pl.pallas_call(
        back_kernel,
        in_specs=[pl.BlockSpec(memory_space=pltpu.SMEM), IN_VMEM, IN_VMEM],
        out_specs=IN_VMEM,
        out_shape=jax.ShapeDtypeStruct(recv.shape[1:], bf16),
        compiler_params=params(),
        name="weight_back",
    )(index, recv, weight)


def join_kernel(pieces_ref, out_ref):
    pieces, rows, lanes = pieces_ref.shape
    half = lanes // 2
    for pair in range(pieces // 2):
        left, right = pieces_ref[2 * pair], pieces_ref[2 * pair + 1]
        columns = pl.ds(pair * lanes, lanes)
        out_ref[:rows, columns] = jnp.concatenate([left[:, :half], right[:, :half]], axis=1)
        out_ref[rows:, columns] = jnp.concatenate([left[:, half:], right[:, half:]], axis=1)


def join_pieces(pieces):
    count, rows, lanes = pieces.shape
    return pl.pallas_call(
        join_kernel,
        out_shape=jax.ShapeDtypeStruct((2 * rows, count * lanes // 2), pieces.dtype),
        compiler_params=params(),
        name="join_pieces",
    )(pieces)


def exchange(values, axes):
    return lax.all_to_all(values, axes, 0, 0, tiled=True)


def shards(groups, members, teacher_patches, student_patches, mask_index, teacher_weight, student_weight):
    along_z, along_x = lax.axis_size("z"), lax.axis_size("x")
    own, stud_own, teach_protos, stud_protos = prepare(
        mask_index.reshape(1, -1), teacher_patches, student_patches, teacher_weight, student_weight, along_z
    )
    width = own.shape[2]
    stud_rows = lax.all_gather(stud_own, ("x", "z"), axis=0, tiled=True)
    line = exchange(own, "z")
    line = jnp.broadcast_to(line.reshape(1, -1, width), (along_x, line.shape[0] * line.shape[1], width))
    teach_rows = exchange(line, "x").reshape(-1, width)

    codes, cols = first_codes(teach_rows, teach_protos, groups)
    cols = exchange(cols, GROUP)
    rows = exchange(row_pass(cols, codes, members, False), MEMBER)
    cols = exchange(col_pass(rows, codes, groups), GROUP)
    expo, norm, turned = student_expo(stud_rows, stud_protos)
    rows = exchange(row_pass(cols, codes, members, True, norm, 1), MEMBER)
    cols = exchange(col_pass(rows, codes, groups), GROUP)
    rows = exchange(row_pass(cols, codes, members, False, rows, 2), MEMBER)
    pieces = exchange(grad_pieces(rows, cols, turned, codes, expo), GROUP)
    index = lax.axis_index(GROUP).reshape(1)
    back = weight_back(index, pieces, student_weight)
    return join_pieces(lax.all_gather(back, GROUP, axis=0))


def solution(mesh):
    groups, members = mesh.devices.shape
    split = Mesh(mesh.devices.reshape(8, 2, 8, 4), GROUP + MEMBER)
    rows = P(GROUP + MEMBER, None)
    columns = P(None, MEMBER)
    return jax.shard_map(
        functools.partial(shards, groups, members),
        mesh=split,
        in_specs=(rows, rows, P(GROUP + MEMBER), columns, columns),
        out_specs=columns,
        check_vma=False,
    )
```

```python
import functools
import math

import jax
import jax.numpy as jnp
from jax import lax
from jax.experimental import pallas as pl
from jax.experimental.pallas import tpu as pltpu
from jax.sharding import Mesh
from jax.sharding import PartitionSpec as P

ALL = ("y", "core", "z", "xhi", "xlo")
SHARD = ("z", "xhi", "xlo")
COLUMN_PEERS = ("y", "xhi", "xlo")
ROW_PEERS = ("core", "z")
PIECE_PEERS = ("xlo", "xhi", "y")
SHARD_PEERS = ("xhi", "y")
LANES = 128
CHUNK = 1024
EXTRA = 8
VMEM_LIMIT = 20 * 1024 * 1024
LOG2E = math.log2(math.e)
IN_VMEM = pl.BlockSpec(memory_space=pltpu.VMEM)
IN_HBM = pl.BlockSpec(memory_space=pltpu.HBM)
IN_SMEM = pl.BlockSpec(memory_space=pltpu.SMEM)

epsilon = 1e-06
teacher_scale = 1.0 / 0.07
student_scale = 1.0 / 0.1
grad_factor = 256.0 / 0.1
NT = (((1,), (1,)), ((), ()))
TN = (((0,), (0,)), ((), ()))
f32 = jnp.float32
bf16 = jnp.bfloat16


def params():
    return pltpu.CompilerParams(vmem_limit_bytes=VMEM_LIMIT)


def cost(flops, transcendentals, nbytes):
    return pl.CostEstimate(flops=flops, transcendentals=transcendentals, bytes_accessed=nbytes)


def lane_row(block, start, count):
    return jnp.concatenate([block[start + j : start + j + 1, :] for j in range(count)], axis=1)


def in_hbm(values):
    return pltpu.with_memory_space_constraint(values, pltpu.HBM)


def rows_kernel(mask_ref, teacher_ref, student_ref, out_ref, index_ref, held_ref, sems):
    copies = [
        pltpu.make_async_copy(mask_ref, index_ref, sems.at[0]),
        pltpu.make_async_copy(teacher_ref, held_ref.at[0], sems.at[1]),
        pltpu.make_async_copy(student_ref, held_ref.at[1], sems.at[2]),
    ]
    for copy in copies:
        copy.start()
    copies[0].wait()
    patches = teacher_ref.shape[0]
    count = mask_ref.shape[1]
    chosen = lax.broadcasted_iota(jnp.int32, (patches, count), 0) == index_ref[...]
    chosen = chosen.astype(f32).astype(bf16)
    for part in range(2):
        copies[1 + part].wait()
        rows = lax.dot_general(chosen, held_ref[part], TN, preferred_element_type=f32)
        square = jnp.sum(rows * rows, axis=1, keepdims=True)
        rows = (rows * lax.rsqrt(square + epsilon)).astype(bf16)
        out_ref[:, part * count : (part + 1) * count, :] = jnp.broadcast_to(rows[None], (out_ref.shape[0],) + rows.shape)


def masked_rows(mask, teacher, student, copies):
    count, width = mask.shape[1], teacher.shape[1]
    return pl.pallas_call(
        rows_kernel,
        in_specs=[IN_HBM] * 3,
        out_specs=IN_VMEM,
        out_shape=jax.ShapeDtypeStruct((copies, 2 * count, width), bf16),
        scratch_shapes=[
            pltpu.VMEM(mask.shape, jnp.int32),
            pltpu.VMEM((2,) + teacher.shape, bf16),
            pltpu.SemaphoreType.DMA((3,)),
        ],
        compiler_params=params(),
        name="masked_rows",
    )(in_hbm(mask), in_hbm(teacher), in_hbm(student))


def two_shards(flags_ref, own_ref, near_ref, far_ref, act):
    @pl.when(flags_ref[2] == 1)
    def _():
        act(own_ref, near_ref)

    @pl.when(flags_ref[2] == 0)
    def _():
        act(near_ref, far_ref)


def protos_kernel(flags_ref, own_ref, near_ref, far_ref, teach_ref, stud_ref, held_ref, sems):
    def bring(first, second):
        copies = [
            pltpu.make_async_copy(first, held_ref.at[0], sems.at[0]),
            pltpu.make_async_copy(second, held_ref.at[1], sems.at[1]),
        ]
        for copy in copies:
            copy.start()
        for copy in copies:
            copy.wait()

    two_shards(flags_ref, own_ref, near_ref, far_ref, bring)
    columns = own_ref.shape[2]
    xlo = flags_ref[1]
    for net, out_ref in enumerate((teach_ref, stud_ref)):
        for part, place in ((0, xlo), (1, 1 - xlo)):
            values = held_ref[part, net].astype(f32)
            square = jnp.sum(values * values, axis=0, keepdims=True)
            at = pl.multiple_of(place * columns, columns)
            out_ref[:, pl.ds(at, columns)] = (values * lax.rsqrt(square + epsilon)).astype(bf16)


def prototypes(flags, own, near, far):
    nets, rows, columns = own.shape
    like = jax.ShapeDtypeStruct((rows, 2 * columns), bf16)
    return pl.pallas_call(
        protos_kernel,
        in_specs=[IN_SMEM] + [IN_HBM] * 3,
        out_specs=(IN_VMEM, IN_VMEM),
        out_shape=(like, like),
        scratch_shapes=[pltpu.VMEM((2,) + own.shape, bf16), pltpu.SemaphoreType.DMA((2,))],
        compiler_params=params(),
        name="prototypes",
    )(flags, in_hbm(own), in_hbm(near), in_hbm(far))


def pack_piece(block, piece, pieces):
    rows, columns = block.shape
    width = columns // pieces
    part = block[:, piece * width : (piece + 1) * width]
    return jnp.concatenate([part[: rows // 2], part[rows // 2 :]], axis=1)


def own_piece_kernel(pieces, flags_ref, own_ref, near_ref, out_ref, held_ref, sem):
    index = flags_ref[3]
    columns = pl.ds(pl.multiple_of(index // 2 * LANES, LANES), LANES)

    def bring(first, _):
        copy = pltpu.make_async_copy(first.at[1, :, columns], held_ref, sem)
        copy.start()
        copy.wait()

    two_shards(flags_ref, own_ref, near_ref, near_ref, bring)
    half = own_ref.shape[2] // pieces
    block = held_ref[...].astype(f32)
    block = jnp.where(index % 2 == 0, block[:, :half], block[:, half:])
    rows = block.shape[0] // 2
    out_ref[...] = jnp.concatenate([block[:rows], block[rows:]], axis=1)


def own_piece(flags, own, near, pieces):
    _, rows, columns = own.shape
    return pl.pallas_call(
        functools.partial(own_piece_kernel, pieces),
        in_specs=[IN_SMEM, IN_HBM, IN_HBM],
        out_specs=IN_VMEM,
        out_shape=jax.ShapeDtypeStruct((rows // 2, 2 * columns // pieces), f32),
        scratch_shapes=[pltpu.VMEM((rows, LANES), bf16), pltpu.SemaphoreType.DMA],
        compiler_params=params(),
        name="own_piece",
    )(flags, in_hbm(own), in_hbm(near))


def spread_cols(total, cols_ref):
    for j in range(cols_ref.shape[1]):
        part = total[:, j * LANES : (j + 1) * LANES]
        cols_ref[:, j, :] = jnp.broadcast_to(part, (cols_ref.shape[0], LANES)).astype(bf16)


def net_rows(ref, net):
    blocks, both, width = ref.shape
    count = both // 2
    return ref[:, net * count : (net + 1) * count, :].reshape(blocks * count, width)


def codes_kernel(flags_ref, own_ref, other_ref, protos_ref, codes_ref, cols_ref):
    core = flags_ref[0]
    count = codes_ref.shape[0] // 2
    total = None
    for ref, place in ((own_ref, core), (other_ref, 1 - core)):
        scores = jnp.dot(net_rows(ref, 0), protos_ref[...], preferred_element_type=f32)
        codes = jnp.exp2(scores * (teacher_scale * LOG2E))
        codes_ref[pl.ds(pl.multiple_of(place * count, count), count), :] = codes.astype(bf16)
        sums = jnp.sum(codes, axis=0, keepdims=True)
        total = sums if total is None else total + sums
    spread_cols(total, cols_ref)


def first_codes(flags, own, other, protos, groups):
    blocks, both, width = own.shape
    count = blocks * both
    columns = protos.shape[1]
    return pl.pallas_call(
        codes_kernel,
        in_specs=[IN_SMEM] + [IN_VMEM] * 3,
        out_specs=(IN_VMEM, IN_VMEM),
        out_shape=(
            pltpu.VMEM((count, columns), bf16),
            jax.ShapeDtypeStruct((groups, columns // LANES, LANES), bf16),
        ),
        compiler_params=params(),
        cost_estimate=cost(2 * count * width * columns, count * columns, 2 * count * columns),
        name="first_codes",
    )(flags, own, other, protos)


def sum_lanes(block):
    ones = jnp.ones((16, LANES), bf16)
    sums = lax.dot_general(ones, block.astype(bf16), NT, preferred_element_type=f32)[0:1]
    lines = block.shape[0] // LANES
    return jnp.concatenate([sums[:, j * LANES : (j + 1) * LANES] for j in range(lines)], axis=0)


def row_pass_kernel(stage, *refs):
    recv_ref, codes_ref = refs[:2]
    norm_ref, out_ref = refs[2] if stage else None, refs[-1]
    count = codes_ref.shape[0]
    tiles = recv_ref.shape[1]
    lines = CHUNK // LANES
    scale = lane_row(1.0 / jnp.sum(recv_ref[...].astype(f32), axis=0), 0, tiles)
    for i in range(count // CHUNK):
        part = None
        for j in range(tiles):
            columns = slice(j * LANES, (j + 1) * LANES)
            term = codes_ref[i * CHUNK : (i + 1) * CHUNK, columns].astype(f32) * scale[:, columns]
            part = term if part is None else part + term
        block = jnp.broadcast_to(sum_lanes(part)[None], (out_ref.shape[0], lines, LANES))
        out_ref[:, i * lines : (i + 1) * lines, :] = block.astype(bf16)
    first = count // LANES
    if stage == 1:
        for member in range(out_ref.shape[0]):
            line = norm_ref[member : member + 1, :]
            out_ref[member, first:, :] = jnp.broadcast_to(line, (EXTRA, LANES)).astype(bf16)
    if stage == 2:
        total = jnp.sum(norm_ref[:, first : first + 1, :].astype(f32), axis=0)
        high = total.astype(bf16).astype(f32)
        index = lax.broadcasted_iota(jnp.int32, (EXTRA, LANES), 0)
        extra = jnp.where(index == 0, high, jnp.where(index == 1, total - high, 0.0)).astype(bf16)
        out_ref[:, first:, :] = jnp.broadcast_to(extra[None], (out_ref.shape[0], EXTRA, LANES))


def row_pass(recv, codes, members, norm=None, stage=0):
    count, columns = codes.shape
    lines = count // LANES + (EXTRA if stage else 0)
    return pl.pallas_call(
        functools.partial(row_pass_kernel, stage),
        in_specs=[IN_VMEM] * (3 if stage else 2),
        out_specs=IN_VMEM,
        out_shape=jax.ShapeDtypeStruct((members, lines, LANES), bf16),
        compiler_params=params(),
        cost_estimate=cost(2 * count * columns, 0, 2 * count * columns),
        name="row_pass",
    )(recv, codes, *((norm,) if stage else ()))


def col_pass_kernel(recv_ref, codes_ref, cols_ref):
    count, columns = codes_ref.shape
    lines = CHUNK // LANES
    scale = 1.0 / jnp.sum(recv_ref[:, : count // LANES, :].astype(f32), axis=0)
    ones = jnp.ones((16, LANES), bf16)
    first = lax.broadcasted_iota(jnp.int32, (16, CHUNK), 0) == 0
    spreads = []
    for i in range(count // CHUNK):
        row = jnp.where(first, lane_row(scale, i * lines, lines), 0.0).astype(bf16)
        spreads.append(lax.dot_general(row, ones, TN, preferred_element_type=f32).astype(bf16))
    width = 8 * LANES
    for h in range(columns // width):
        total = jnp.zeros((16, width), f32)
        for i, spread in enumerate(spreads):
            for g in range(lines):
                parts = []
                for j in range(width // LANES):
                    part = None
                    for q in range(LANES // 16):
                        at = g * LANES + q * 16
                        lane = h * width + j * LANES
                        term = codes_ref[i * CHUNK + at : i * CHUNK + at + 16, lane : lane + LANES]
                        term = term * spread[at : at + 16]
                        part = term if part is None else part + term
                    parts.append(part.astype(f32))
                total = total + jnp.concatenate(parts, axis=1)
        total = jnp.sum(total, axis=0, keepdims=True)
        for j in range(width // LANES):
            part = jnp.broadcast_to(total[:, j * LANES : (j + 1) * LANES], (cols_ref.shape[0], LANES))
            cols_ref[:, h * (width // LANES) + j, :] = part.astype(bf16)


def col_pass(recv, codes, groups):
    count, columns = codes.shape
    return pl.pallas_call(
        col_pass_kernel,
        in_specs=[IN_VMEM, IN_VMEM],
        out_specs=IN_VMEM,
        out_shape=jax.ShapeDtypeStruct((groups, columns // LANES, LANES), bf16),
        compiler_params=params(),
        cost_estimate=cost(2 * count * columns, 0, 2 * count * columns),
        name="col_pass",
    )(recv, codes)


def student_kernel(flags_ref, own_ref, other_ref, protos_ref, expo_ref, norm_ref, turned_ref):
    core = flags_ref[0]
    columns = protos_ref.shape[1]
    count = expo_ref.shape[0] // 2
    lines = count // LANES
    for half in range(2):
        rows = jnp.where(core == half, net_rows(own_ref, 1), net_rows(other_ref, 1))
        span = slice(half * count, (half + 1) * count)
        scores = jnp.dot(rows, protos_ref[...], preferred_element_type=f32)
        expo = jnp.exp2(scores * (student_scale * LOG2E))
        expo_ref[span, :] = expo.astype(bf16)
        part = expo[:, :LANES]
        for j in range(1, columns // LANES):
            part = part + expo[:, j * LANES : (j + 1) * LANES]
        norm_ref[half * lines : (half + 1) * lines, :] = sum_lanes(part)
        turned_ref[:, span] = rows.T


def student_expo(flags, own, other, protos):
    blocks, both, width = own.shape
    count = blocks * both
    columns = protos.shape[1]
    return pl.pallas_call(
        student_kernel,
        in_specs=[IN_SMEM] + [IN_VMEM] * 3,
        out_specs=(IN_VMEM,) * 3,
        out_shape=(
            pltpu.VMEM((count, columns), bf16),
            jax.ShapeDtypeStruct((count // LANES, LANES), f32),
            pltpu.VMEM((width, count), bf16),
        ),
        compiler_params=params(),
        cost_estimate=cost(2 * count * width * columns, count * columns, 2 * count * columns),
        name="student_expo",
    )(flags, own, other, protos)


def scaled_product(scale, turned_ref, codes_ref):
    turned = (turned_ref[...].astype(f32) * lane_row(scale, 0, scale.shape[0])).astype(bf16)
    return jnp.dot(turned, codes_ref[...], preferred_element_type=f32)


def grad_kernel(recv_ref, norm_ref, cols_ref, turned_ref, codes_ref, expo_ref, out_ref):
    members = recv_ref.shape[0]
    lines = codes_ref.shape[0] // LANES
    row_scale = 1.0 / jnp.sum(recv_ref[:, :lines, :].astype(f32), axis=0)
    norm = jnp.concatenate(
        [norm_ref[m, lines : lines + 1, :].astype(f32) + norm_ref[m, lines + 1 : lines + 2, :].astype(f32) for m in range(members)],
        axis=0,
    )
    mass = jnp.sum(cols_ref[...].astype(f32), axis=0)
    teach = scaled_product(row_scale, turned_ref, codes_ref) * lane_row(1.0 / mass, 0, cols_ref.shape[1])
    grad = grad_factor * (scaled_product(1.0 / norm, turned_ref, expo_ref) - teach)
    for piece in range(out_ref.shape[0]):
        out_ref[piece] = pack_piece(grad, piece, out_ref.shape[0]).astype(bf16)


def grad_pieces(recv, norm, cols, turned, codes, expo, pieces):
    count, columns = codes.shape
    width = turned.shape[0]
    return pl.pallas_call(
        grad_kernel,
        in_specs=[IN_VMEM] * 6,
        out_specs=IN_VMEM,
        out_shape=jax.ShapeDtypeStruct((pieces, width // 2, 2 * columns // pieces), bf16),
        compiler_params=params(),
        cost_estimate=cost(4 * count * width * columns, 0, 4 * count * columns),
        name="grad_pieces",
    )(recv, norm, cols, turned, codes, expo)


def back_kernel(recv_ref, weight_ref, out_ref):
    grad = jnp.sum(recv_ref[...].astype(f32), axis=0)
    weight = weight_ref[...]
    half = weight.shape[1] // 2

    def column_sum(values):
        total = jnp.sum(values, axis=0, keepdims=True)
        return total + jnp.concatenate([total[:, half:], total[:, :half]], axis=1)

    inverse = lax.rsqrt(column_sum(weight * weight) + epsilon)
    along = column_sum(grad * weight)
    back = (grad * inverse - weight * (inverse * inverse * inverse * along)).astype(bf16)
    out_ref[...] = jnp.broadcast_to(back[None], out_ref.shape)


def weight_back(recv, weight, copies):
    return pl.pallas_call(
        back_kernel,
        in_specs=[IN_VMEM, IN_VMEM],
        out_specs=IN_VMEM,
        out_shape=jax.ShapeDtypeStruct((copies,) + weight.shape, bf16),
        compiler_params=params(),
        name="weight_back",
    )(recv, weight)


def join_kernel(flags_ref, mine_ref, other_ref, out_ref):
    pieces, rows, lanes = mine_ref.shape
    half = lanes // 2

    def join(ref):
        for pair in range(pieces // 2):
            left, right = ref[2 * pair], ref[2 * pair + 1]
            columns = pl.ds(pair * lanes, lanes)
            out_ref[:rows, columns] = jnp.concatenate([left[:, :half], right[:, :half]], axis=1)
            out_ref[rows:, columns] = jnp.concatenate([left[:, half:], right[:, half:]], axis=1)

    @pl.when(flags_ref[2] == 1)
    def _():
        join(mine_ref)

    @pl.when(flags_ref[2] == 0)
    def _():
        join(other_ref)


def join_pieces(flags, mine, other):
    count, rows, lanes = mine.shape
    return pl.pallas_call(
        join_kernel,
        in_specs=[IN_SMEM, IN_VMEM, IN_VMEM],
        out_specs=IN_VMEM,
        out_shape=jax.ShapeDtypeStruct((2 * rows, count * lanes // 2), mine.dtype),
        compiler_params=params(),
        name="join_pieces",
    )(flags, mine, other)


def exchange(values, axes):
    return lax.all_to_all(values, axes, 0, 0, tiled=True)


def shard_permutes(weight):
    axes = ("core", "xhi", "xlo")
    near, far = [], []
    for core in range(2):
        for xhi in range(2):
            for xlo in range(2):
                here = core * 4 + xhi * 2 + xlo
                if xhi == core:
                    near.append((core * 4 + xhi * 2 + 1 - xlo, here))
                else:
                    near.append(((1 - core) * 4 + core * 2 + xlo, here))
                    far.append((core * 4 + core * 2 + 1 - xlo, here))
    return lax.ppermute(weight, axes, near), lax.ppermute(weight, axes, far)


def shards(teacher_patches, student_patches, mask_index, teacher_weight, student_weight):
    size = lax.axis_size
    column_peers, row_peers = size(COLUMN_PEERS), size(ROW_PEERS)
    shard_pieces = size(SHARD_PEERS)
    core, xhi, xlo = lax.axis_index("core"), lax.axis_index("xhi"), lax.axis_index("xlo")
    matched = (core == xhi).astype(jnp.int32)
    flags = jnp.stack([core, xlo, matched, lax.axis_index(SHARD_PEERS)]).astype(jnp.int32)

    weights = jnp.stack([teacher_weight, student_weight])
    near, far = shard_permutes(weights)
    teach_protos, stud_protos = prototypes(flags, weights, near, far)
    line = masked_rows(mask_index.reshape(1, -1), teacher_patches, student_patches, size("z"))
    line = exchange(line, "z")
    line, teach_protos, stud_protos = lax.optimization_barrier((line, teach_protos, stud_protos))
    other = lax.ppermute(line, "core", [(0, 1), (1, 0)])

    codes, cols = first_codes(flags, line, other, teach_protos, column_peers)
    expo, norm, turned = student_expo(flags, line, other, stud_protos)
    cols, expo, norm, turned = lax.optimization_barrier((cols, expo, norm, turned))
    cols = exchange(cols, COLUMN_PEERS)
    rows = exchange(row_pass(cols, codes, row_peers, norm, 1), ROW_PEERS)
    cols = exchange(col_pass(rows, codes, column_peers), COLUMN_PEERS)
    rows = exchange(row_pass(cols, codes, row_peers, rows, 2), ROW_PEERS)
    norm = rows
    cols = exchange(col_pass(rows, codes, column_peers), COLUMN_PEERS)
    rows = exchange(row_pass(cols, codes, row_peers), ROW_PEERS)
    pieces = exchange(grad_pieces(rows, norm, cols, turned, codes, expo, 2 * shard_pieces), PIECE_PEERS)
    weight = own_piece(flags, weights, near, shard_pieces)
    mine = exchange(weight_back(pieces, weight, shard_pieces), SHARD_PEERS)
    other = lax.ppermute(mine, ("core", "xhi"), [(0, 2), (3, 1)])
    return join_pieces(flags, mine, other)


def solution(mesh):
    split = Mesh(mesh.devices.reshape(8, 2, 8, 2, 2), ALL)
    rows = P(ALL, None)
    columns = P(None, SHARD)
    return jax.shard_map(
        shards,
        mesh=split,
        in_specs=(rows, rows, P(ALL), columns, columns),
        out_specs=columns,
        check_vma=False,
    )
```

```python
import functools
import math

import jax
import jax.numpy as jnp
from jax import lax
from jax.experimental import pallas as pl
from jax.experimental.pallas import tpu as pltpu
from jax.sharding import Mesh
from jax.sharding import PartitionSpec as P

ALL = ("y", "core", "z", "xhi", "xlo")
SHARD = ("z", "xhi", "xlo")
COLUMN_PEERS = ("y", "xhi", "xlo")
ROW_PEERS = ("core", "z")
PIECE_PEERS = ("xlo", "xhi", "y")
SHARD_PEERS = ("xhi", "y")
LANES = 128
CHUNK = 1024
EXTRA = 8
VMEM_LIMIT = 20 * 1024 * 1024
LOG2E = math.log2(math.e)
IN_VMEM = pl.BlockSpec(memory_space=pltpu.VMEM)
IN_HBM = pl.BlockSpec(memory_space=pltpu.HBM)
IN_SMEM = pl.BlockSpec(memory_space=pltpu.SMEM)

epsilon = 1e-06
teacher_scale = 1.0 / 0.07
student_scale = 1.0 / 0.1
grad_factor = 256.0 / 0.1
NT = (((1,), (1,)), ((), ()))
TN = (((0,), (0,)), ((), ()))
f32 = jnp.float32
bf16 = jnp.bfloat16


def params():
    return pltpu.CompilerParams(vmem_limit_bytes=VMEM_LIMIT)


def cost(flops, transcendentals, nbytes):
    return pl.CostEstimate(flops=flops, transcendentals=transcendentals, bytes_accessed=nbytes)


def lane_row(block, start, count):
    return jnp.concatenate([block[start + j : start + j + 1, :] for j in range(count)], axis=1)


def in_hbm(values):
    return pltpu.with_memory_space_constraint(values, pltpu.HBM)


def rows_kernel(mask_ref, teacher_ref, student_ref, out_ref, index_ref, held_ref, sems):
    copies = [
        pltpu.make_async_copy(mask_ref, index_ref, sems.at[0]),
        pltpu.make_async_copy(teacher_ref, held_ref.at[0], sems.at[1]),
        pltpu.make_async_copy(student_ref, held_ref.at[1], sems.at[2]),
    ]
    for copy in copies:
        copy.start()
    copies[0].wait()
    patches = teacher_ref.shape[0]
    count = mask_ref.shape[1]
    chosen = lax.broadcasted_iota(jnp.int32, (patches, count), 0) == index_ref[...]
    chosen = chosen.astype(f32).astype(bf16)
    for part in range(2):
        copies[1 + part].wait()
        rows = lax.dot_general(chosen, held_ref[part], TN, preferred_element_type=f32)
        square = jnp.sum(rows * rows, axis=1, keepdims=True)
        rows = (rows * lax.rsqrt(square + epsilon)).astype(bf16)
        out_ref[:, part * count : (part + 1) * count, :] = jnp.broadcast_to(rows[None], (out_ref.shape[0],) + rows.shape)


def masked_rows(mask, teacher, student, copies):
    count, width = mask.shape[1], teacher.shape[1]
    return pl.pallas_call(
        rows_kernel,
        in_specs=[IN_HBM] * 3,
        out_specs=IN_VMEM,
        out_shape=jax.ShapeDtypeStruct((copies, 2 * count, width), bf16),
        scratch_shapes=[
            pltpu.VMEM(mask.shape, jnp.int32),
            pltpu.VMEM((2,) + teacher.shape, bf16),
            pltpu.SemaphoreType.DMA((3,)),
        ],
        compiler_params=params(),
        name="masked_rows",
    )(in_hbm(mask), in_hbm(teacher), in_hbm(student))


def two_shards(flags_ref, own_ref, near_ref, far_ref, act):
    @pl.when(flags_ref[2] == 1)
    def _():
        act(own_ref, near_ref)

    @pl.when(flags_ref[2] == 0)
    def _():
        act(near_ref, far_ref)


def protos_kernel(pieces, flags_ref, own_ref, near_ref, far_ref, out_ref, *piece_ref):
    columns = own_ref.shape[1]
    xlo = flags_ref[1]

    def scaled(first, second):
        for ref, place in ((first, xlo), (second, 1 - xlo)):
            values = ref[...].astype(f32)
            square = jnp.sum(values * values, axis=0, keepdims=True)
            at = pl.multiple_of(place * columns, columns)
            out_ref[:, pl.ds(at, columns)] = (values * lax.rsqrt(square + epsilon)).astype(bf16)
        if pieces:
            index = flags_ref[3]
            half = columns // pieces
            block = first[:, pl.ds(pl.multiple_of(index // 2 * LANES, LANES), LANES)].astype(f32)
            block = jnp.where(index % 2 == 0, block[:, :half], block[:, half:])
            rows = block.shape[0] // 2
            piece_ref[0][...] = jnp.concatenate([block[:rows], block[rows:]], axis=1)

    two_shards(flags_ref, own_ref, near_ref, far_ref, scaled)


def prototypes(flags, own, near, far, pieces=0):
    rows, columns = own.shape
    shapes = [jax.ShapeDtypeStruct((rows, 2 * columns), bf16)]
    if pieces:
        shapes.append(jax.ShapeDtypeStruct((rows // 2, 2 * columns // pieces), f32))
    return pl.pallas_call(
        functools.partial(protos_kernel, pieces),
        in_specs=[IN_SMEM] + [IN_VMEM] * 3,
        out_specs=[IN_VMEM] * len(shapes),
        out_shape=shapes,
        compiler_params=params(),
        cost_estimate=cost(4 * rows * columns, 0, 8 * rows * columns),
        name="prototypes",
    )(flags, own, near, far)


def pack_piece(block, piece, pieces):
    rows, columns = block.shape
    width = columns // pieces
    part = block[:, piece * width : (piece + 1) * width]
    return jnp.concatenate([part[: rows // 2], part[rows // 2 :]], axis=1)


def spread_cols(total, cols_ref):
    for j in range(cols_ref.shape[1]):
        part = total[:, j * LANES : (j + 1) * LANES]
        cols_ref[:, j, :] = jnp.broadcast_to(part, (cols_ref.shape[0], LANES)).astype(bf16)


def net_rows(ref, net):
    blocks, both, width = ref.shape
    count = both // 2
    return ref[:, net * count : (net + 1) * count, :].reshape(blocks * count, width)


def codes_kernel(flags_ref, own_ref, other_ref, protos_ref, codes_ref, cols_ref):
    core = flags_ref[0]
    count = codes_ref.shape[0] // 2
    total = None
    for ref, place in ((own_ref, core), (other_ref, 1 - core)):
        scores = jnp.dot(net_rows(ref, 0), protos_ref[...], preferred_element_type=f32)
        codes = jnp.exp2(scores * (teacher_scale * LOG2E))
        codes_ref[pl.ds(pl.multiple_of(place * count, count), count), :] = codes.astype(bf16)
        sums = jnp.sum(codes, axis=0, keepdims=True)
        total = sums if total is None else total + sums
    spread_cols(total, cols_ref)


def first_codes(flags, own, other, protos, groups):
    blocks, both, width = own.shape
    count = blocks * both
    columns = protos.shape[1]
    return pl.pallas_call(
        codes_kernel,
        in_specs=[IN_SMEM] + [IN_VMEM] * 3,
        out_specs=(IN_VMEM, IN_VMEM),
        out_shape=(
            pltpu.VMEM((count, columns), bf16),
            jax.ShapeDtypeStruct((groups, columns // LANES, LANES), bf16),
        ),
        compiler_params=params(),
        cost_estimate=cost(2 * count * width * columns, count * columns, 2 * count * columns),
        name="first_codes",
    )(flags, own, other, protos)


def sum_lanes(block):
    ones = jnp.ones((16, LANES), bf16)
    sums = lax.dot_general(ones, block.astype(bf16), NT, preferred_element_type=f32)[0:1]
    lines = block.shape[0] // LANES
    return jnp.concatenate([sums[:, j * LANES : (j + 1) * LANES] for j in range(lines)], axis=0)


def row_pass_kernel(stage, *refs):
    recv_ref, codes_ref = refs[:2]
    norm_ref, out_ref = refs[2] if stage else None, refs[-1]
    count = codes_ref.shape[0]
    tiles = recv_ref.shape[1]
    lines = CHUNK // LANES
    scale = lane_row(1.0 / jnp.sum(recv_ref[...].astype(f32), axis=0), 0, tiles)
    for i in range(count // CHUNK):
        blocks = []
        for k in range(lines):
            at = i * CHUNK + k * LANES
            part = None
            for j in range(tiles):
                columns = slice(j * LANES, (j + 1) * LANES)
                term = codes_ref[at : at + LANES, columns].astype(f32) * scale[:, columns]
                part = term if part is None else part + term
            blocks.append(part.astype(bf16))
        block = jnp.broadcast_to(sum_lanes(jnp.concatenate(blocks, axis=0))[None], (out_ref.shape[0], lines, LANES))
        out_ref[:, i * lines : (i + 1) * lines, :] = block.astype(bf16)
    first = count // LANES
    if stage == 1:
        for member in range(out_ref.shape[0]):
            line = norm_ref[member : member + 1, :]
            out_ref[member, first:, :] = jnp.broadcast_to(line, (EXTRA, LANES)).astype(bf16)
    if stage == 2:
        total = jnp.sum(norm_ref[:, first : first + 1, :].astype(f32), axis=0)
        high = total.astype(bf16).astype(f32)
        index = lax.broadcasted_iota(jnp.int32, (EXTRA, LANES), 0)
        extra = jnp.where(index == 0, high, jnp.where(index == 1, total - high, 0.0)).astype(bf16)
        out_ref[:, first:, :] = jnp.broadcast_to(extra[None], (out_ref.shape[0], EXTRA, LANES))


def row_pass(recv, codes, members, norm=None, stage=0):
    count, columns = codes.shape
    lines = count // LANES + (EXTRA if stage else 0)
    return pl.pallas_call(
        functools.partial(row_pass_kernel, stage),
        in_specs=[IN_VMEM] * (3 if stage else 2),
        out_specs=IN_VMEM,
        out_shape=jax.ShapeDtypeStruct((members, lines, LANES), bf16),
        compiler_params=params(),
        cost_estimate=cost(2 * count * columns, 0, 2 * count * columns),
        name="row_pass",
    )(recv, codes, *((norm,) if stage else ()))


def col_pass_kernel(recv_ref, codes_ref, cols_ref):
    count, columns = codes_ref.shape
    lines = CHUNK // LANES
    scale = 1.0 / jnp.sum(recv_ref[:, : count // LANES, :].astype(f32), axis=0)
    ones = jnp.ones((16, LANES), bf16)
    first = lax.broadcasted_iota(jnp.int32, (16, CHUNK), 0) == 0
    spreads = []
    for i in range(count // CHUNK):
        row = jnp.where(first, lane_row(scale, i * lines, lines), 0.0).astype(bf16)
        spreads.append(lax.dot_general(row, ones, TN, preferred_element_type=f32).astype(bf16))
    width = 8 * LANES
    for h in range(columns // width):
        total = jnp.zeros((16, width), f32)
        for i, spread in enumerate(spreads):
            for g in range(lines):
                parts = []
                for j in range(width // LANES):
                    part = None
                    for q in range(LANES // 16):
                        at = g * LANES + q * 16
                        lane = h * width + j * LANES
                        term = codes_ref[i * CHUNK + at : i * CHUNK + at + 16, lane : lane + LANES]
                        term = term * spread[at : at + 16]
                        part = term if part is None else part + term
                    parts.append(part.astype(f32))
                total = total + jnp.concatenate(parts, axis=1)
        total = jnp.sum(total, axis=0, keepdims=True)
        for j in range(width // LANES):
            part = jnp.broadcast_to(total[:, j * LANES : (j + 1) * LANES], (cols_ref.shape[0], LANES))
            cols_ref[:, h * (width // LANES) + j, :] = part.astype(bf16)


def col_pass(recv, codes, groups):
    count, columns = codes.shape
    return pl.pallas_call(
        col_pass_kernel,
        in_specs=[IN_VMEM, IN_VMEM],
        out_specs=IN_VMEM,
        out_shape=jax.ShapeDtypeStruct((groups, columns // LANES, LANES), bf16),
        compiler_params=params(),
        cost_estimate=cost(2 * count * columns, 0, 2 * count * columns),
        name="col_pass",
    )(recv, codes)


def student_kernel(flags_ref, own_ref, other_ref, protos_ref, expo_ref, norm_ref, turned_ref):
    core = flags_ref[0]
    columns = protos_ref.shape[1]
    count = expo_ref.shape[0] // 2
    lines = count // LANES
    for half in range(2):
        rows = jnp.where(core == half, net_rows(own_ref, 1), net_rows(other_ref, 1))
        span = slice(half * count, (half + 1) * count)
        scores = jnp.dot(rows, protos_ref[...], preferred_element_type=f32)
        expo = jnp.exp2(scores * (student_scale * LOG2E))
        expo_ref[span, :] = expo.astype(bf16)
        part = expo[:, :LANES]
        for j in range(1, columns // LANES):
            part = part + expo[:, j * LANES : (j + 1) * LANES]
        norm_ref[half * lines : (half + 1) * lines, :] = sum_lanes(part)
        turned_ref[:, span] = rows.T


def student_expo(flags, own, other, protos):
    blocks, both, width = own.shape
    count = blocks * both
    columns = protos.shape[1]
    return pl.pallas_call(
        student_kernel,
        in_specs=[IN_SMEM] + [IN_VMEM] * 3,
        out_specs=(IN_VMEM,) * 3,
        out_shape=(
            pltpu.VMEM((count, columns), bf16),
            jax.ShapeDtypeStruct((count // LANES, LANES), f32),
            pltpu.VMEM((width, count), bf16),
        ),
        compiler_params=params(),
        cost_estimate=cost(2 * count * width * columns, count * columns, 2 * count * columns),
        name="student_expo",
    )(flags, own, other, protos)


def scaled_product(scale, turned_ref, codes_ref):
    turned = (turned_ref[...].astype(f32) * lane_row(scale, 0, scale.shape[0])).astype(bf16)
    return jnp.dot(turned, codes_ref[...], preferred_element_type=f32)


def grad_kernel(recv_ref, norm_ref, cols_ref, turned_ref, codes_ref, expo_ref, out_ref):
    members = recv_ref.shape[0]
    lines = codes_ref.shape[0] // LANES
    row_scale = 1.0 / jnp.sum(recv_ref[:, :lines, :].astype(f32), axis=0)
    norm = jnp.concatenate(
        [norm_ref[m, lines : lines + 1, :].astype(f32) + norm_ref[m, lines + 1 : lines + 2, :].astype(f32) for m in range(members)],
        axis=0,
    )
    mass = jnp.sum(cols_ref[...].astype(f32), axis=0)
    teach = scaled_product(row_scale, turned_ref, codes_ref) * lane_row(1.0 / mass, 0, cols_ref.shape[1])
    grad = grad_factor * (scaled_product(1.0 / norm, turned_ref, expo_ref) - teach)
    for piece in range(out_ref.shape[0]):
        out_ref[piece] = pack_piece(grad, piece, out_ref.shape[0]).astype(bf16)


def grad_pieces(recv, norm, cols, turned, codes, expo, pieces):
    count, columns = codes.shape
    width = turned.shape[0]
    return pl.pallas_call(
        grad_kernel,
        in_specs=[IN_VMEM] * 6,
        out_specs=IN_VMEM,
        out_shape=jax.ShapeDtypeStruct((pieces, width // 2, 2 * columns // pieces), bf16),
        compiler_params=params(),
        cost_estimate=cost(4 * count * width * columns, 0, 4 * count * columns),
        name="grad_pieces",
    )(recv, norm, cols, turned, codes, expo)


def back_kernel(recv_ref, weight_ref, out_ref):
    grad = jnp.sum(recv_ref[...].astype(f32), axis=0)
    weight = weight_ref[...]
    half = weight.shape[1] // 2

    def column_sum(values):
        total = jnp.sum(values, axis=0, keepdims=True)
        return total + jnp.concatenate([total[:, half:], total[:, :half]], axis=1)

    inverse = lax.rsqrt(column_sum(weight * weight) + epsilon)
    along = column_sum(grad * weight)
    back = (grad * inverse - weight * (inverse * inverse * inverse * along)).astype(bf16)
    out_ref[...] = jnp.broadcast_to(back[None], out_ref.shape)


def weight_back(recv, weight, copies):
    return pl.pallas_call(
        back_kernel,
        in_specs=[IN_VMEM, IN_VMEM],
        out_specs=IN_VMEM,
        out_shape=jax.ShapeDtypeStruct((copies,) + weight.shape, bf16),
        compiler_params=params(),
        name="weight_back",
    )(recv, weight)


def join_kernel(flags_ref, mine_ref, other_ref, out_ref):
    pieces, rows, lanes = mine_ref.shape
    half = lanes // 2

    def join(ref):
        for pair in range(pieces // 2):
            left, right = ref[2 * pair], ref[2 * pair + 1]
            columns = pl.ds(pair * lanes, lanes)
            out_ref[:rows, columns] = jnp.concatenate([left[:, :half], right[:, :half]], axis=1)
            out_ref[rows:, columns] = jnp.concatenate([left[:, half:], right[:, half:]], axis=1)

    @pl.when(flags_ref[2] == 1)
    def _():
        join(mine_ref)

    @pl.when(flags_ref[2] == 0)
    def _():
        join(other_ref)


def join_pieces(flags, mine, other):
    count, rows, lanes = mine.shape
    return pl.pallas_call(
        join_kernel,
        in_specs=[IN_SMEM, IN_VMEM, IN_VMEM],
        out_specs=IN_VMEM,
        out_shape=jax.ShapeDtypeStruct((2 * rows, count * lanes // 2), mine.dtype),
        compiler_params=params(),
        name="join_pieces",
    )(flags, mine, other)


def exchange(values, axes):
    return lax.all_to_all(values, axes, 0, 0, tiled=True)


def shard_permutes(weight):
    axes = ("core", "xhi", "xlo")
    near, far = [], []
    for core in range(2):
        for xhi in range(2):
            for xlo in range(2):
                here = core * 4 + xhi * 2 + xlo
                if xhi == core:
                    near.append((core * 4 + xhi * 2 + 1 - xlo, here))
                else:
                    near.append(((1 - core) * 4 + core * 2 + xlo, here))
                    far.append((core * 4 + core * 2 + 1 - xlo, here))
    return lax.ppermute(weight, axes, near), lax.ppermute(weight, axes, far)


def shards(teacher_patches, student_patches, mask_index, teacher_weight, student_weight):
    size = lax.axis_size
    column_peers, row_peers = size(COLUMN_PEERS), size(ROW_PEERS)
    shard_pieces = size(SHARD_PEERS)
    core, xhi, xlo = lax.axis_index("core"), lax.axis_index("xhi"), lax.axis_index("xlo")
    matched = (core == xhi).astype(jnp.int32)
    flags = jnp.stack([core, xlo, matched, lax.axis_index(SHARD_PEERS)]).astype(jnp.int32)

    teach_near, teach_far = shard_permutes(teacher_weight)
    stud_near, stud_far = shard_permutes(student_weight)
    (teach_protos,) = prototypes(flags, teacher_weight, teach_near, teach_far)
    line = masked_rows(mask_index.reshape(1, -1), teacher_patches, student_patches, size("z"))
    line = exchange(line, "z")
    line, teach_protos, stud_near, stud_far = lax.optimization_barrier((line, teach_protos, stud_near, stud_far))
    other = lax.ppermute(line, "core", [(0, 1), (1, 0)])
    stud_protos, weight = prototypes(flags, student_weight, stud_near, stud_far, shard_pieces)
    other, stud_protos, weight = lax.optimization_barrier((other, stud_protos, weight))

    codes, cols = first_codes(flags, line, other, teach_protos, column_peers)
    expo, norm, turned = student_expo(flags, line, other, stud_protos)
    cols, expo, norm, turned = lax.optimization_barrier((cols, expo, norm, turned))
    cols = exchange(cols, COLUMN_PEERS)
    rows = exchange(row_pass(cols, codes, row_peers, norm, 1), ROW_PEERS)
    cols = exchange(col_pass(rows, codes, column_peers), COLUMN_PEERS)
    rows = exchange(row_pass(cols, codes, row_peers, rows, 2), ROW_PEERS)
    norm = rows
    cols = exchange(col_pass(rows, codes, column_peers), COLUMN_PEERS)
    rows = exchange(row_pass(cols, codes, row_peers), ROW_PEERS)
    pieces = exchange(grad_pieces(rows, norm, cols, turned, codes, expo, 2 * shard_pieces), PIECE_PEERS)
    mine = exchange(weight_back(pieces, weight, shard_pieces), SHARD_PEERS)
    other = lax.ppermute(mine, ("core", "xhi"), [(0, 2), (3, 1)])
    return join_pieces(flags, mine, other)


def solution(mesh):
    split = Mesh(mesh.devices.reshape(8, 2, 8, 2, 2), ALL)
    rows = P(ALL, None)
    columns = P(None, SHARD)
    return jax.shard_map(
        shards,
        mesh=split,
        in_specs=(rows, rows, P(ALL), columns, columns),
        out_specs=columns,
        check_vma=False,
    )
```

```python
import functools
import math

import jax
import jax.numpy as jnp
from jax import lax
from jax.experimental import pallas as pl
from jax.experimental.pallas import tpu as pltpu
from jax.sharding import Mesh
from jax.sharding import PartitionSpec as P

ALL = ("y", "core", "z", "xhi", "xlo")
SHARD = ("z", "xhi", "xlo")
COLUMN_PEERS = ("y", "xhi", "xlo")
ROW_PEERS = ("core", "z")
PIECE_PEERS = ("xlo", "xhi", "y")
SHARD_PEERS = ("xhi", "y")
LANES = 128
CHUNK = 1024
EXTRA = 8
VMEM_LIMIT = 20 * 1024 * 1024
LOG2E = math.log2(math.e)
IN_VMEM = pl.BlockSpec(memory_space=pltpu.VMEM)
IN_HBM = pl.BlockSpec(memory_space=pltpu.HBM)
IN_SMEM = pl.BlockSpec(memory_space=pltpu.SMEM)

epsilon = 1e-06
teacher_scale = 1.0 / 0.07
student_scale = 1.0 / 0.1
grad_factor = 256.0 / 0.1
NT = (((1,), (1,)), ((), ()))
TN = (((0,), (0,)), ((), ()))
f32 = jnp.float32
bf16 = jnp.bfloat16


def params():
    return pltpu.CompilerParams(vmem_limit_bytes=VMEM_LIMIT)


def cost(flops, transcendentals, nbytes):
    return pl.CostEstimate(flops=flops, transcendentals=transcendentals, bytes_accessed=nbytes)


def lane_row(block, start, count):
    return jnp.concatenate([block[start + j : start + j + 1, :] for j in range(count)], axis=1)


def in_hbm(values):
    return pltpu.with_memory_space_constraint(values, pltpu.HBM)


def rows_kernel(
    mask_ref, teacher_ref, student_ref, teacher_weight_ref, student_weight_ref, out_ref, weights_ref, index_ref, held_ref, made_ref, sems
):
    copies = [
        pltpu.make_async_copy(mask_ref, index_ref, sems.at[0]),
        pltpu.make_async_copy(teacher_ref, held_ref.at[0], sems.at[1]),
        pltpu.make_async_copy(student_ref, held_ref.at[1], sems.at[2]),
        pltpu.make_async_copy(teacher_weight_ref, weights_ref.at[0], sems.at[3]),
        pltpu.make_async_copy(student_weight_ref, weights_ref.at[1], sems.at[4]),
    ]
    for copy in copies:
        copy.start()
    copies[0].wait()
    patches = teacher_ref.shape[0]
    count = mask_ref.shape[1]
    chosen = lax.broadcasted_iota(jnp.int32, (patches, count), 0) == index_ref[...]
    chosen = chosen.astype(f32).astype(bf16)
    for part in range(2):
        copies[1 + part].wait()
        rows = lax.dot_general(chosen, held_ref[part], TN, preferred_element_type=f32)
        square = jnp.sum(rows * rows, axis=1, keepdims=True)
        made_ref[part * count : (part + 1) * count, :] = (rows * lax.rsqrt(square + epsilon)).astype(bf16)
    sends = [pltpu.make_async_copy(made_ref, out_ref.at[i], sems.at[5 + i]) for i in range(out_ref.shape[0])]
    for send in sends:
        send.start()
    for copy in copies[3:] + sends:
        copy.wait()


def masked_rows(mask, teacher, student, teacher_weight, student_weight, copies):
    count, width = mask.shape[1], teacher.shape[1]
    sources = (mask, teacher, student, teacher_weight, student_weight)
    return pl.pallas_call(
        rows_kernel,
        in_specs=[IN_HBM] * 5,
        out_specs=(IN_HBM, IN_HBM),
        out_shape=(
            pltpu.HBM((copies, 2 * count, width), bf16),
            pltpu.HBM((2,) + teacher_weight.shape, bf16),
        ),
        scratch_shapes=[
            pltpu.VMEM(mask.shape, jnp.int32),
            pltpu.VMEM((2,) + teacher.shape, bf16),
            pltpu.VMEM((2 * count, width), bf16),
            pltpu.SemaphoreType.DMA((5 + copies,)),
        ],
        compiler_params=params(),
        name="masked_rows",
    )(*map(in_hbm, sources))


def two_shards(flags_ref, own_ref, near_ref, far_ref, act):
    @pl.when(flags_ref[2] == 1)
    def _():
        act(own_ref, near_ref)

    @pl.when(flags_ref[2] == 0)
    def _():
        act(near_ref, far_ref)


def protos_kernel(pieces, flags_ref, own_ref, near_ref, far_ref, teach_ref, stud_ref, piece_ref, held_ref, sems):
    def bring(first, second):
        copies = [
            pltpu.make_async_copy(first, held_ref.at[0], sems.at[0]),
            pltpu.make_async_copy(second, held_ref.at[1], sems.at[1]),
        ]
        for copy in copies:
            copy.start()
        for copy in copies:
            copy.wait()

    two_shards(flags_ref, own_ref, near_ref, far_ref, bring)
    columns = own_ref.shape[2]
    xlo, index = flags_ref[1], flags_ref[3]
    for net, out_ref in enumerate((teach_ref, stud_ref)):
        for part, place in ((0, xlo), (1, 1 - xlo)):
            values = held_ref[part, net].astype(f32)
            square = jnp.sum(values * values, axis=0, keepdims=True)
            at = pl.multiple_of(place * columns, columns)
            out_ref[:, pl.ds(at, columns)] = (values * lax.rsqrt(square + epsilon)).astype(bf16)
    half = columns // pieces
    block = held_ref[0, 1, :, pl.ds(pl.multiple_of(index // 2 * LANES, LANES), LANES)].astype(f32)
    block = jnp.where(index % 2 == 0, block[:, :half], block[:, half:])
    rows = block.shape[0] // 2
    piece_ref[...] = jnp.concatenate([block[:rows], block[rows:]], axis=1)


def prototypes(flags, own, near, far, pieces):
    nets, rows, columns = own.shape
    like = jax.ShapeDtypeStruct((rows, 2 * columns), bf16)
    return pl.pallas_call(
        functools.partial(protos_kernel, pieces),
        in_specs=[IN_SMEM] + [IN_HBM] * 3,
        out_specs=[IN_VMEM] * 3,
        out_shape=(like, like, jax.ShapeDtypeStruct((rows // 2, 2 * columns // pieces), f32)),
        scratch_shapes=[pltpu.VMEM((2,) + own.shape, bf16), pltpu.SemaphoreType.DMA((2,))],
        compiler_params=params(),
        cost_estimate=cost(8 * rows * columns, 0, 16 * rows * columns),
        name="prototypes",
    )(flags, in_hbm(own), in_hbm(near), in_hbm(far))


def pack_piece(block, piece, pieces):
    rows, columns = block.shape
    width = columns // pieces
    part = block[:, piece * width : (piece + 1) * width]
    return jnp.concatenate([part[: rows // 2], part[rows // 2 :]], axis=1)


def spread_cols(total, cols_ref):
    lines = cols_ref.shape[1]
    block = jnp.concatenate([total[:, j * LANES : (j + 1) * LANES] for j in range(lines)], axis=0)
    cols_ref[...] = jnp.broadcast_to(block[None], cols_ref.shape).astype(bf16)


def net_rows(ref, net):
    blocks, both, width = ref.shape
    count = both // 2
    return ref[:, net * count : (net + 1) * count, :].reshape(blocks * count, width)


def codes_kernel(flags_ref, own_ref, other_ref, protos_ref, codes_ref, cols_ref):
    core = flags_ref[0]
    count = codes_ref.shape[0] // 2
    total = None
    for ref, place in ((own_ref, core), (other_ref, 1 - core)):
        scores = jnp.dot(net_rows(ref, 0), protos_ref[...], preferred_element_type=f32)
        codes = jnp.exp2(scores * (teacher_scale * LOG2E))
        codes_ref[pl.ds(pl.multiple_of(place * count, count), count), :] = codes.astype(bf16)
        sums = jnp.sum(codes, axis=0, keepdims=True)
        total = sums if total is None else total + sums
    spread_cols(total, cols_ref)


def first_codes(flags, own, other, protos, groups):
    blocks, both, width = own.shape
    count = blocks * both
    columns = protos.shape[1]
    return pl.pallas_call(
        codes_kernel,
        in_specs=[IN_SMEM] + [IN_VMEM] * 3,
        out_specs=(IN_VMEM, IN_VMEM),
        out_shape=(
            pltpu.VMEM((count, columns), bf16),
            jax.ShapeDtypeStruct((groups, columns // LANES, LANES), bf16),
        ),
        compiler_params=params(),
        cost_estimate=cost(2 * count * width * columns, count * columns, 2 * count * columns),
        name="first_codes",
    )(flags, own, other, protos)


def sum_lanes(block):
    ones = jnp.ones((16, LANES), bf16)
    sums = lax.dot_general(ones, block.astype(bf16), NT, preferred_element_type=f32)[0:1]
    lines = block.shape[0] // LANES
    return jnp.concatenate([sums[:, j * LANES : (j + 1) * LANES] for j in range(lines)], axis=0)


def row_pass_kernel(stage, *refs):
    recv_ref, codes_ref = refs[:2]
    norm_ref, out_ref = refs[2] if stage else None, refs[-1]
    count = codes_ref.shape[0]
    tiles = recv_ref.shape[1]
    lines = CHUNK // LANES
    scale = lane_row(1.0 / jnp.sum(recv_ref[...].astype(f32), axis=0), 0, tiles).astype(bf16)
    for i in range(count // CHUNK):
        blocks = []
        for k in range(lines):
            at = i * CHUNK + k * LANES
            total = None
            for g in range(0, tiles, 8):
                part = None
                for j in range(g, g + 8):
                    columns = slice(j * LANES, (j + 1) * LANES)
                    term = codes_ref[at : at + LANES, columns] * scale[:, columns]
                    part = term if part is None else part + term
                part = part.astype(f32)
                total = part if total is None else total + part
            blocks.append(total.astype(bf16))
        block = jnp.broadcast_to(sum_lanes(jnp.concatenate(blocks, axis=0))[None], (out_ref.shape[0], lines, LANES))
        out_ref[:, i * lines : (i + 1) * lines, :] = block.astype(bf16)
    first = count // LANES
    if stage == 1:
        for member in range(out_ref.shape[0]):
            line = norm_ref[member : member + 1, :]
            out_ref[member, first:, :] = jnp.broadcast_to(line, (EXTRA, LANES)).astype(bf16)
    if stage == 2:
        total = jnp.sum(norm_ref[:, first : first + 1, :].astype(f32), axis=0)
        high = total.astype(bf16).astype(f32)
        index = lax.broadcasted_iota(jnp.int32, (EXTRA, LANES), 0)
        extra = jnp.where(index == 0, high, jnp.where(index == 1, total - high, 0.0)).astype(bf16)
        out_ref[:, first:, :] = jnp.broadcast_to(extra[None], (out_ref.shape[0], EXTRA, LANES))


def row_pass(recv, codes, members, norm=None, stage=0):
    count, columns = codes.shape
    lines = count // LANES + (EXTRA if stage else 0)
    return pl.pallas_call(
        functools.partial(row_pass_kernel, stage),
        in_specs=[IN_VMEM] * (3 if stage else 2),
        out_specs=IN_VMEM,
        out_shape=jax.ShapeDtypeStruct((members, lines, LANES), bf16),
        compiler_params=params(),
        cost_estimate=cost(2 * count * columns, 0, 2 * count * columns),
        name="row_pass",
    )(recv, codes, *((norm,) if stage else ()))


def col_pass_kernel(recv_ref, codes_ref, cols_ref):
    count, columns = codes_ref.shape
    lines = CHUNK // LANES
    scale = 1.0 / jnp.sum(recv_ref[:, : count // LANES, :].astype(f32), axis=0)
    ones = jnp.ones((16, LANES), bf16)
    first = lax.broadcasted_iota(jnp.int32, (16, CHUNK), 0) == 0
    spreads = []
    for i in range(count // CHUNK):
        row = jnp.where(first, lane_row(scale, i * lines, lines), 0.0).astype(bf16)
        spreads.append(lax.dot_general(row, ones, TN, preferred_element_type=f32).astype(bf16))
    width = 8 * LANES
    totals = []
    for h in range(columns // width):
        total = jnp.zeros((16, width), f32)
        for i, spread in enumerate(spreads):
            for g in range(lines):
                parts = []
                for j in range(width // LANES):
                    part = None
                    for q in range(LANES // 16):
                        at = g * LANES + q * 16
                        lane = h * width + j * LANES
                        term = codes_ref[i * CHUNK + at : i * CHUNK + at + 16, lane : lane + LANES]
                        term = term * spread[at : at + 16]
                        part = term if part is None else part + term
                    parts.append(part.astype(f32))
                total = total + jnp.concatenate(parts, axis=1)
        totals.append(jnp.sum(total, axis=0, keepdims=True))
    spread_cols(jnp.concatenate(totals, axis=1), cols_ref)


def col_pass(recv, codes, groups):
    count, columns = codes.shape
    return pl.pallas_call(
        col_pass_kernel,
        in_specs=[IN_VMEM, IN_VMEM],
        out_specs=IN_VMEM,
        out_shape=jax.ShapeDtypeStruct((groups, columns // LANES, LANES), bf16),
        compiler_params=params(),
        cost_estimate=cost(2 * count * columns, 0, 2 * count * columns),
        name="col_pass",
    )(recv, codes)


def student_kernel(flags_ref, own_ref, other_ref, protos_ref, expo_ref, norm_ref, turned_ref):
    core = flags_ref[0]
    columns = protos_ref.shape[1]
    count = expo_ref.shape[0] // 2
    lines = count // LANES
    for half in range(2):
        rows = jnp.where(core == half, net_rows(own_ref, 1), net_rows(other_ref, 1))
        span = slice(half * count, (half + 1) * count)
        scores = jnp.dot(rows, protos_ref[...], preferred_element_type=f32)
        expo = jnp.exp2(scores * (student_scale * LOG2E))
        expo_ref[span, :] = expo.astype(bf16)
        part = expo[:, :LANES]
        for j in range(1, columns // LANES):
            part = part + expo[:, j * LANES : (j + 1) * LANES]
        norm_ref[half * lines : (half + 1) * lines, :] = sum_lanes(part)
        turned_ref[:, span] = rows.T


def student_expo(flags, own, other, protos):
    blocks, both, width = own.shape
    count = blocks * both
    columns = protos.shape[1]
    return pl.pallas_call(
        student_kernel,
        in_specs=[IN_SMEM] + [IN_VMEM] * 3,
        out_specs=(IN_VMEM,) * 3,
        out_shape=(
            pltpu.VMEM((count, columns), bf16),
            jax.ShapeDtypeStruct((count // LANES, LANES), f32),
            pltpu.VMEM((width, count), bf16),
        ),
        compiler_params=params(),
        cost_estimate=cost(2 * count * width * columns, count * columns, 2 * count * columns),
        name="student_expo",
    )(flags, own, other, protos)


def scaled_product(scale, turned_ref, codes_ref):
    turned = (turned_ref[...].astype(f32) * lane_row(scale, 0, scale.shape[0])).astype(bf16)
    return jnp.dot(turned, codes_ref[...], preferred_element_type=f32)


def grad_kernel(recv_ref, norm_ref, cols_ref, turned_ref, codes_ref, expo_ref, out_ref):
    members = recv_ref.shape[0]
    lines = codes_ref.shape[0] // LANES
    row_scale = 1.0 / jnp.sum(recv_ref[:, :lines, :].astype(f32), axis=0)
    norm = jnp.concatenate(
        [norm_ref[m, lines : lines + 1, :].astype(f32) + norm_ref[m, lines + 1 : lines + 2, :].astype(f32) for m in range(members)],
        axis=0,
    )
    mass = jnp.sum(cols_ref[...].astype(f32), axis=0)
    teach = scaled_product(row_scale, turned_ref, codes_ref) * lane_row(1.0 / mass, 0, cols_ref.shape[1])
    grad = grad_factor * (scaled_product(1.0 / norm, turned_ref, expo_ref) - teach)
    for piece in range(out_ref.shape[0]):
        out_ref[piece] = pack_piece(grad, piece, out_ref.shape[0]).astype(bf16)


def grad_pieces(recv, norm, cols, turned, codes, expo, pieces):
    count, columns = codes.shape
    width = turned.shape[0]
    return pl.pallas_call(
        grad_kernel,
        in_specs=[IN_VMEM] * 6,
        out_specs=IN_VMEM,
        out_shape=jax.ShapeDtypeStruct((pieces, width // 2, 2 * columns // pieces), bf16),
        compiler_params=params(),
        cost_estimate=cost(4 * count * width * columns, 0, 4 * count * columns),
        name="grad_pieces",
    )(recv, norm, cols, turned, codes, expo)


def back_kernel(recv_ref, weight_ref, out_ref):
    grad = jnp.sum(recv_ref[...].astype(f32), axis=0)
    weight = weight_ref[...]
    half = weight.shape[1] // 2

    def column_sum(values):
        total = jnp.sum(values, axis=0, keepdims=True)
        return total + jnp.concatenate([total[:, half:], total[:, :half]], axis=1)

    inverse = lax.rsqrt(column_sum(weight * weight) + epsilon)
    along = column_sum(grad * weight)
    back = (grad * inverse - weight * (inverse * inverse * inverse * along)).astype(bf16)
    out_ref[...] = jnp.broadcast_to(back[None], out_ref.shape)


def weight_back(recv, weight, copies):
    return pl.pallas_call(
        back_kernel,
        in_specs=[IN_VMEM, IN_VMEM],
        out_specs=IN_VMEM,
        out_shape=jax.ShapeDtypeStruct((copies,) + weight.shape, bf16),
        compiler_params=params(),
        name="weight_back",
    )(recv, weight)


def join_kernel(flags_ref, mine_ref, other_ref, out_ref):
    pieces, rows, lanes = mine_ref.shape
    half = lanes // 2

    def join(ref):
        for pair in range(pieces // 2):
            left, right = ref[2 * pair], ref[2 * pair + 1]
            columns = pl.ds(pair * lanes, lanes)
            out_ref[:rows, columns] = jnp.concatenate([left[:, :half], right[:, :half]], axis=1)
            out_ref[rows:, columns] = jnp.concatenate([left[:, half:], right[:, half:]], axis=1)

    @pl.when(flags_ref[2] == 1)
    def _():
        join(mine_ref)

    @pl.when(flags_ref[2] == 0)
    def _():
        join(other_ref)


def join_pieces(flags, mine, other):
    count, rows, lanes = mine.shape
    return pl.pallas_call(
        join_kernel,
        in_specs=[IN_SMEM, IN_VMEM, IN_VMEM],
        out_specs=IN_VMEM,
        out_shape=jax.ShapeDtypeStruct((2 * rows, count * lanes // 2), mine.dtype),
        compiler_params=params(),
        name="join_pieces",
    )(flags, mine, other)


def exchange(values, axes):
    return lax.all_to_all(values, axes, 0, 0, tiled=True)


def shard_permutes(weight):
    axes = ("core", "xhi", "xlo")
    near, far = [], []
    for core in range(2):
        for xhi in range(2):
            for xlo in range(2):
                here = core * 4 + xhi * 2 + xlo
                if xhi == core:
                    near.append((core * 4 + xhi * 2 + 1 - xlo, here))
                else:
                    near.append(((1 - core) * 4 + core * 2 + xlo, here))
                    far.append((core * 4 + core * 2 + 1 - xlo, here))
    return lax.ppermute(weight, axes, near), lax.ppermute(weight, axes, far)


def shards(teacher_patches, student_patches, mask_index, teacher_weight, student_weight):
    size = lax.axis_size
    column_peers, row_peers = size(COLUMN_PEERS), size(ROW_PEERS)
    shard_pieces = size(SHARD_PEERS)
    core, xhi, xlo = lax.axis_index("core"), lax.axis_index("xhi"), lax.axis_index("xlo")
    matched = (core == xhi).astype(jnp.int32)
    flags = jnp.stack([core, xlo, matched, lax.axis_index(SHARD_PEERS)]).astype(jnp.int32)

    line, weights = masked_rows(
        mask_index.reshape(1, -1), teacher_patches, student_patches, teacher_weight, student_weight, size("z")
    )
    near, far = shard_permutes(weights)
    line = exchange(line, "z")
    line, near, far = lax.optimization_barrier((line, near, far))
    other = lax.ppermute(line, "core", [(0, 1), (1, 0)])
    teach_protos, stud_protos, weight = prototypes(flags, weights, near, far, shard_pieces)
    other, teach_protos, stud_protos, weight = lax.optimization_barrier((other, teach_protos, stud_protos, weight))

    codes, cols = first_codes(flags, line, other, teach_protos, column_peers)
    expo, norm, turned = student_expo(flags, line, other, stud_protos)
    cols, expo, norm, turned = lax.optimization_barrier((cols, expo, norm, turned))
    cols = exchange(cols, COLUMN_PEERS)
    rows = exchange(row_pass(cols, codes, row_peers, norm, 1), ROW_PEERS)
    cols = exchange(col_pass(rows, codes, column_peers), COLUMN_PEERS)
    rows = exchange(row_pass(cols, codes, row_peers, rows, 2), ROW_PEERS)
    norm = rows
    cols = exchange(col_pass(rows, codes, column_peers), COLUMN_PEERS)
    rows = exchange(row_pass(cols, codes, row_peers), ROW_PEERS)
    pieces = exchange(grad_pieces(rows, norm, cols, turned, codes, expo, 2 * shard_pieces), PIECE_PEERS)
    mine = exchange(weight_back(pieces, weight, shard_pieces), SHARD_PEERS)
    other = lax.ppermute(mine, ("core", "xhi"), [(0, 2), (3, 1)])
    return join_pieces(flags, mine, other)


def solution(mesh):
    split = Mesh(mesh.devices.reshape(8, 2, 8, 2, 2), ALL)
    rows = P(ALL, None)
    columns = P(None, SHARD)
    return jax.shard_map(
        shards,
        mesh=split,
        in_specs=(rows, rows, P(ALL), columns, columns),
        out_specs=columns,
        check_vma=False,
    )
```

```python
import functools
import math

import jax
import jax.numpy as jnp
from jax import lax
from jax.experimental import pallas as pl
from jax.experimental.pallas import tpu as pltpu
from jax.sharding import Mesh
from jax.sharding import PartitionSpec as P

ALL = ("y", "core", "z", "xhi", "xlo")
SHARD = ("z", "xhi", "xlo")
COLUMN_PEERS = ("y", "xhi", "xlo")
ROW_PEERS = ("core", "z")
PIECE_PEERS = ("xlo", "xhi", "y")
SHARD_PEERS = ("xhi", "y")
LANES = 128
CHUNK = 1024
EXTRA = 8
VMEM_LIMIT = 20 * 1024 * 1024
LOG2E = math.log2(math.e)
IN_VMEM = pl.BlockSpec(memory_space=pltpu.VMEM)
IN_HBM = pl.BlockSpec(memory_space=pltpu.HBM)
IN_SMEM = pl.BlockSpec(memory_space=pltpu.SMEM)

epsilon = 1e-06
teacher_scale = 1.0 / 0.07
student_scale = 1.0 / 0.1
grad_factor = 256.0 / 0.1
NT = (((1,), (1,)), ((), ()))
TN = (((0,), (0,)), ((), ()))
f32 = jnp.float32
bf16 = jnp.bfloat16


def params():
    return pltpu.CompilerParams(vmem_limit_bytes=VMEM_LIMIT)


def cost(flops, transcendentals, nbytes):
    return pl.CostEstimate(flops=flops, transcendentals=transcendentals, bytes_accessed=nbytes)


def lane_row(block, start, count):
    return jnp.concatenate([block[start + j : start + j + 1, :] for j in range(count)], axis=1)


def in_hbm(values):
    return pltpu.with_memory_space_constraint(values, pltpu.HBM)


def rows_kernel(mask_ref, teacher_ref, student_ref, out_ref, index_ref, held_ref, made_ref, sems):
    copies = [
        pltpu.make_async_copy(mask_ref, index_ref, sems.at[0]),
        pltpu.make_async_copy(teacher_ref, held_ref.at[0], sems.at[1]),
        pltpu.make_async_copy(student_ref, held_ref.at[1], sems.at[2]),
    ]
    for copy in copies:
        copy.start()
    copies[0].wait()
    patches = teacher_ref.shape[0]
    count = mask_ref.shape[1]
    chosen = lax.broadcasted_iota(jnp.int32, (patches, count), 0) == index_ref[...]
    chosen = chosen.astype(f32).astype(bf16)
    for part in range(2):
        copies[1 + part].wait()
        rows = lax.dot_general(chosen, held_ref[part], TN, preferred_element_type=f32)
        square = jnp.sum(rows * rows, axis=1, keepdims=True)
        made_ref[part * count : (part + 1) * count, :] = (rows * lax.rsqrt(square + epsilon)).astype(bf16)
    sends = [pltpu.make_async_copy(made_ref, out_ref.at[i], sems.at[3 + i]) for i in range(out_ref.shape[0])]
    for send in sends:
        send.start()
    for send in sends:
        send.wait()


def masked_rows(mask, teacher, student, copies):
    count, width = mask.shape[1], teacher.shape[1]
    return pl.pallas_call(
        rows_kernel,
        in_specs=[IN_HBM] * 3,
        out_specs=IN_HBM,
        out_shape=pltpu.HBM((copies, 2 * count, width), bf16),
        scratch_shapes=[
            pltpu.VMEM(mask.shape, jnp.int32),
            pltpu.VMEM((2,) + teacher.shape, bf16),
            pltpu.VMEM((2 * count, width), bf16),
            pltpu.SemaphoreType.DMA((3 + copies,)),
        ],
        compiler_params=params(),
        name="masked_rows",
    )(in_hbm(mask), in_hbm(teacher), in_hbm(student))


def two_shards(flags_ref, own_ref, first_ref, second_ref, act):
    @pl.when(flags_ref[2] == 1)
    def _():
        act(own_ref, first_ref)

    @pl.when(flags_ref[2] == 0)
    def _():
        act(second_ref, first_ref)


def protos_kernel(pieces, flags_ref, own_ref, first_in_ref, second_in_ref, out_ref, *piece_ref):
    columns = own_ref.shape[1]
    xlo = flags_ref[1]

    def scaled(first, second):
        for ref, place in ((first, xlo), (second, 1 - xlo)):
            values = ref[...].astype(f32)
            square = jnp.sum(values * values, axis=0, keepdims=True)
            at = pl.multiple_of(place * columns, columns)
            out_ref[:, pl.ds(at, columns)] = (values * lax.rsqrt(square + epsilon)).astype(bf16)
        if pieces:
            index = flags_ref[3]
            half = columns // pieces
            block = first[:, pl.ds(pl.multiple_of(index // 2 * LANES, LANES), LANES)].astype(f32)
            block = jnp.where(index % 2 == 0, block[:, :half], block[:, half:])
            rows = block.shape[0] // 2
            piece_ref[0][...] = jnp.concatenate([block[:rows], block[rows:]], axis=1)

    two_shards(flags_ref, own_ref, first_in_ref, second_in_ref, scaled)


def prototypes(flags, own, first_in, second_in, pieces=0):
    rows, columns = own.shape
    shapes = [jax.ShapeDtypeStruct((rows, 2 * columns), bf16)]
    if pieces:
        shapes.append(jax.ShapeDtypeStruct((rows // 2, 2 * columns // pieces), f32))
    return pl.pallas_call(
        functools.partial(protos_kernel, pieces),
        in_specs=[IN_SMEM] + [IN_VMEM] * 3,
        out_specs=[IN_VMEM] * len(shapes),
        out_shape=shapes,
        compiler_params=params(),
        cost_estimate=cost(4 * rows * columns, 0, 8 * rows * columns),
        name="prototypes",
    )(flags, own, first_in, second_in)


def pack_piece(block, piece, pieces):
    rows, columns = block.shape
    width = columns // pieces
    part = block[:, piece * width : (piece + 1) * width]
    return jnp.concatenate([part[: rows // 2], part[rows // 2 :]], axis=1)


def spread_cols(total, cols_ref):
    lines = cols_ref.shape[1]
    block = jnp.concatenate([total[:, j * LANES : (j + 1) * LANES] for j in range(lines)], axis=0)
    cols_ref[...] = jnp.broadcast_to(block[None], cols_ref.shape).astype(bf16)


def net_rows(ref, net):
    blocks, both, width = ref.shape
    count = both // 2
    return ref[:, net * count : (net + 1) * count, :].reshape(blocks * count, width)


def codes_kernel(flags_ref, own_ref, other_ref, protos_ref, codes_ref, cols_ref):
    core = flags_ref[0]
    count = codes_ref.shape[0] // 2
    total = None
    for ref, place in ((own_ref, core), (other_ref, 1 - core)):
        scores = jnp.dot(net_rows(ref, 0), protos_ref[...], preferred_element_type=f32)
        codes = jnp.exp2(scores * (teacher_scale * LOG2E))
        codes_ref[pl.ds(pl.multiple_of(place * count, count), count), :] = codes.astype(bf16)
        sums = jnp.sum(codes, axis=0, keepdims=True)
        total = sums if total is None else total + sums
    spread_cols(total, cols_ref)


def first_codes(flags, own, other, protos, groups):
    blocks, both, width = own.shape
    count = blocks * both
    columns = protos.shape[1]
    return pl.pallas_call(
        codes_kernel,
        in_specs=[IN_SMEM] + [IN_VMEM] * 3,
        out_specs=(IN_VMEM, IN_VMEM),
        out_shape=(
            pltpu.VMEM((count, columns), bf16),
            jax.ShapeDtypeStruct((groups, columns // LANES, LANES), bf16),
        ),
        compiler_params=params(),
        cost_estimate=cost(2 * count * width * columns, count * columns, 2 * count * columns),
        name="first_codes",
    )(flags, own, other, protos)


def sum_lanes(block):
    ones = jnp.ones((16, LANES), bf16)
    sums = lax.dot_general(ones, block.astype(bf16), NT, preferred_element_type=f32)[0:1]
    lines = block.shape[0] // LANES
    return jnp.concatenate([sums[:, j * LANES : (j + 1) * LANES] for j in range(lines)], axis=0)


def row_pass_kernel(stage, *refs):
    recv_ref, codes_ref = refs[:2]
    norm_ref, out_ref = refs[2] if stage else None, refs[-1]
    count = codes_ref.shape[0]
    tiles = recv_ref.shape[1]
    lines = CHUNK // LANES
    scale = lane_row(1.0 / jnp.sum(recv_ref[...].astype(f32), axis=0), 0, tiles).astype(bf16)
    for i in range(count // CHUNK):
        blocks = []
        for k in range(lines):
            at = i * CHUNK + k * LANES
            total = None
            for g in range(0, tiles, 8):
                part = None
                for j in range(g, g + 8):
                    columns = slice(j * LANES, (j + 1) * LANES)
                    term = codes_ref[at : at + LANES, columns] * scale[:, columns]
                    part = term if part is None else part + term
                part = part.astype(f32)
                total = part if total is None else total + part
            blocks.append(total.astype(bf16))
        block = jnp.broadcast_to(sum_lanes(jnp.concatenate(blocks, axis=0))[None], (out_ref.shape[0], lines, LANES))
        out_ref[:, i * lines : (i + 1) * lines, :] = block.astype(bf16)
    first = count // LANES
    if stage == 1:
        for member in range(out_ref.shape[0]):
            line = norm_ref[member : member + 1, :]
            out_ref[member, first:, :] = jnp.broadcast_to(line, (EXTRA, LANES)).astype(bf16)
    if stage == 2:
        total = jnp.sum(norm_ref[:, first : first + 1, :].astype(f32), axis=0)
        high = total.astype(bf16).astype(f32)
        index = lax.broadcasted_iota(jnp.int32, (EXTRA, LANES), 0)
        extra = jnp.where(index == 0, high, jnp.where(index == 1, total - high, 0.0)).astype(bf16)
        out_ref[:, first:, :] = jnp.broadcast_to(extra[None], (out_ref.shape[0], EXTRA, LANES))


def row_pass(recv, codes, members, norm=None, stage=0):
    count, columns = codes.shape
    lines = count // LANES + (EXTRA if stage else 0)
    return pl.pallas_call(
        functools.partial(row_pass_kernel, stage),
        in_specs=[IN_VMEM] * (3 if stage else 2),
        out_specs=IN_VMEM,
        out_shape=jax.ShapeDtypeStruct((members, lines, LANES), bf16),
        compiler_params=params(),
        cost_estimate=cost(2 * count * columns, 0, 2 * count * columns),
        name="row_pass",
    )(recv, codes, *((norm,) if stage else ()))


def col_pass_kernel(recv_ref, codes_ref, cols_ref):
    count, columns = codes_ref.shape
    lines = CHUNK // LANES
    scale = 1.0 / jnp.sum(recv_ref[:, : count // LANES, :].astype(f32), axis=0)
    ones = jnp.ones((16, LANES), bf16)
    first = lax.broadcasted_iota(jnp.int32, (16, CHUNK), 0) == 0
    spreads = []
    for i in range(count // CHUNK):
        row = jnp.where(first, lane_row(scale, i * lines, lines), 0.0).astype(bf16)
        spreads.append(lax.dot_general(row, ones, TN, preferred_element_type=f32).astype(bf16))
    width = 8 * LANES
    totals = []
    for h in range(columns // width):
        total = jnp.zeros((16, width), f32)
        for i, spread in enumerate(spreads):
            for g in range(lines):
                parts = []
                for j in range(width // LANES):
                    part = None
                    for q in range(LANES // 16):
                        at = g * LANES + q * 16
                        lane = h * width + j * LANES
                        term = codes_ref[i * CHUNK + at : i * CHUNK + at + 16, lane : lane + LANES]
                        term = term * spread[at : at + 16]
                        part = term if part is None else part + term
                    parts.append(part.astype(f32))
                total = total + jnp.concatenate(parts, axis=1)
        totals.append(jnp.sum(total, axis=0, keepdims=True))
    spread_cols(jnp.concatenate(totals, axis=1), cols_ref)


def col_pass(recv, codes, groups):
    count, columns = codes.shape
    return pl.pallas_call(
        col_pass_kernel,
        in_specs=[IN_VMEM, IN_VMEM],
        out_specs=IN_VMEM,
        out_shape=jax.ShapeDtypeStruct((groups, columns // LANES, LANES), bf16),
        compiler_params=params(),
        cost_estimate=cost(2 * count * columns, 0, 2 * count * columns),
        name="col_pass",
    )(recv, codes)


def student_kernel(flags_ref, own_ref, other_ref, protos_ref, expo_ref, norm_ref, turned_ref):
    core = flags_ref[0]
    columns = protos_ref.shape[1]
    count = expo_ref.shape[0] // 2
    lines = count // LANES
    for half in range(2):
        rows = jnp.where(core == half, net_rows(own_ref, 1), net_rows(other_ref, 1))
        span = slice(half * count, (half + 1) * count)
        scores = jnp.dot(rows, protos_ref[...], preferred_element_type=f32)
        expo = jnp.exp2(scores * (student_scale * LOG2E))
        expo_ref[span, :] = expo.astype(bf16)
        part = expo[:, :LANES]
        for j in range(1, columns // LANES):
            part = part + expo[:, j * LANES : (j + 1) * LANES]
        norm_ref[half * lines : (half + 1) * lines, :] = sum_lanes(part)
        turned_ref[:, span] = rows.T


def student_expo(flags, own, other, protos):
    blocks, both, width = own.shape
    count = blocks * both
    columns = protos.shape[1]
    return pl.pallas_call(
        student_kernel,
        in_specs=[IN_SMEM] + [IN_VMEM] * 3,
        out_specs=(IN_VMEM,) * 3,
        out_shape=(
            pltpu.VMEM((count, columns), bf16),
            jax.ShapeDtypeStruct((count // LANES, LANES), f32),
            pltpu.VMEM((width, count), bf16),
        ),
        compiler_params=params(),
        cost_estimate=cost(2 * count * width * columns, count * columns, 2 * count * columns),
        name="student_expo",
    )(flags, own, other, protos)


def scaled_product(scale, turned_ref, codes_ref):
    turned = (turned_ref[...].astype(f32) * lane_row(scale, 0, scale.shape[0])).astype(bf16)
    return jnp.dot(turned, codes_ref[...], preferred_element_type=f32)


def grad_kernel(recv_ref, norm_ref, cols_ref, turned_ref, codes_ref, expo_ref, out_ref):
    members = recv_ref.shape[0]
    lines = codes_ref.shape[0] // LANES
    row_scale = 1.0 / jnp.sum(recv_ref[:, :lines, :].astype(f32), axis=0)
    norm = jnp.concatenate(
        [norm_ref[m, lines : lines + 1, :].astype(f32) + norm_ref[m, lines + 1 : lines + 2, :].astype(f32) for m in range(members)],
        axis=0,
    )
    mass = jnp.sum(cols_ref[...].astype(f32), axis=0)
    teach = scaled_product(row_scale, turned_ref, codes_ref) * lane_row(1.0 / mass, 0, cols_ref.shape[1])
    grad = grad_factor * (scaled_product(1.0 / norm, turned_ref, expo_ref) - teach)
    for piece in range(out_ref.shape[0]):
        out_ref[piece] = pack_piece(grad, piece, out_ref.shape[0]).astype(bf16)


def grad_pieces(recv, norm, cols, turned, codes, expo, pieces):
    count, columns = codes.shape
    width = turned.shape[0]
    return pl.pallas_call(
        grad_kernel,
        in_specs=[IN_VMEM] * 6,
        out_specs=IN_VMEM,
        out_shape=jax.ShapeDtypeStruct((pieces, width // 2, 2 * columns // pieces), bf16),
        compiler_params=params(),
        cost_estimate=cost(4 * count * width * columns, 0, 4 * count * columns),
        name="grad_pieces",
    )(recv, norm, cols, turned, codes, expo)


def back_kernel(recv_ref, weight_ref, out_ref):
    grad = jnp.sum(recv_ref[...].astype(f32), axis=0)
    weight = weight_ref[...]
    half = weight.shape[1] // 2

    def column_sum(values):
        total = jnp.sum(values, axis=0, keepdims=True)
        return total + jnp.concatenate([total[:, half:], total[:, :half]], axis=1)

    inverse = lax.rsqrt(column_sum(weight * weight) + epsilon)
    along = column_sum(grad * weight)
    back = (grad * inverse - weight * (inverse * inverse * inverse * along)).astype(bf16)
    out_ref[...] = jnp.broadcast_to(back[None], out_ref.shape)


def weight_back(recv, weight, copies):
    return pl.pallas_call(
        back_kernel,
        in_specs=[IN_VMEM, IN_VMEM],
        out_specs=IN_VMEM,
        out_shape=jax.ShapeDtypeStruct((copies,) + weight.shape, bf16),
        compiler_params=params(),
        name="weight_back",
    )(recv, weight)


def join_kernel(flags_ref, mine_ref, other_ref, out_ref):
    pieces, rows, lanes = mine_ref.shape
    half = lanes // 2

    def join(ref):
        for pair in range(pieces // 2):
            left, right = ref[2 * pair], ref[2 * pair + 1]
            columns = pl.ds(pair * lanes, lanes)
            out_ref[:rows, columns] = jnp.concatenate([left[:, :half], right[:, :half]], axis=1)
            out_ref[rows:, columns] = jnp.concatenate([left[:, half:], right[:, half:]], axis=1)

    @pl.when(flags_ref[2] == 1)
    def _():
        join(mine_ref)

    @pl.when(flags_ref[2] == 0)
    def _():
        join(other_ref)


def join_pieces(flags, mine, other):
    count, rows, lanes = mine.shape
    return pl.pallas_call(
        join_kernel,
        in_specs=[IN_SMEM, IN_VMEM, IN_VMEM],
        out_specs=IN_VMEM,
        out_shape=jax.ShapeDtypeStruct((2 * rows, count * lanes // 2), mine.dtype),
        compiler_params=params(),
        name="join_pieces",
    )(flags, mine, other)


def exchange(values, axes):
    return lax.all_to_all(values, axes, 0, 0, tiled=True)


def shard_permutes(weight, pair):
    axes = ("core", "xhi", "xlo")
    first, second = [], []
    for core in range(2):
        for xhi in range(2):
            for xlo in range(2):
                here = core * 4 + xhi * 2 + xlo
                if xhi == core:
                    first.append((core * 4 + xhi * 2 + 1 - xlo, here))
                else:
                    first.append(((1 - core) * 4 + core * 2 + 1 - xlo, here))
                    second.append((core * 4 + (xhi if pair else core) * 2 + 1 - xlo, here))
    once = lax.ppermute(weight, axes, first)
    return once, lax.ppermute(once, axes, second)


def shards(teacher_patches, student_patches, mask_index, teacher_weight, student_weight):
    size = lax.axis_size
    column_peers, row_peers = size(COLUMN_PEERS), size(ROW_PEERS)
    shard_pieces = size(SHARD_PEERS)
    core, xhi, xlo = lax.axis_index("core"), lax.axis_index("xhi"), lax.axis_index("xlo")
    matched = (core == xhi).astype(jnp.int32)
    flags = jnp.stack([core, xlo, matched, lax.axis_index(SHARD_PEERS)]).astype(jnp.int32)

    teach_first, teach_second = shard_permutes(teacher_weight, True)
    stud_first, stud_second = shard_permutes(student_weight, False)
    (teach_protos,) = prototypes(flags, teacher_weight, teach_first, teach_second)
    line = masked_rows(mask_index.reshape(1, -1), teacher_patches, student_patches, size("z"))
    line = exchange(line, "z")
    line, teach_protos, stud_first, stud_second = lax.optimization_barrier((line, teach_protos, stud_first, stud_second))
    other = lax.ppermute(line, "core", [(0, 1), (1, 0)])
    stud_protos, weight = prototypes(flags, student_weight, stud_first, stud_second, shard_pieces)
    other, stud_protos, weight = lax.optimization_barrier((other, stud_protos, weight))

    codes, cols = first_codes(flags, line, other, teach_protos, column_peers)
    expo, norm, turned = student_expo(flags, line, other, stud_protos)
    cols, expo, norm, turned = lax.optimization_barrier((cols, expo, norm, turned))
    cols = exchange(cols, COLUMN_PEERS)
    rows = exchange(row_pass(cols, codes, row_peers, norm, 1), ROW_PEERS)
    cols = exchange(col_pass(rows, codes, column_peers), COLUMN_PEERS)
    rows = exchange(row_pass(cols, codes, row_peers, rows, 2), ROW_PEERS)
    norm = rows
    cols = exchange(col_pass(rows, codes, column_peers), COLUMN_PEERS)
    rows = exchange(row_pass(cols, codes, row_peers), ROW_PEERS)
    pieces = exchange(grad_pieces(rows, norm, cols, turned, codes, expo, 2 * shard_pieces), PIECE_PEERS)
    mine = exchange(weight_back(pieces, weight, shard_pieces), SHARD_PEERS)
    other = lax.ppermute(mine, ("core", "xhi"), [(0, 2), (3, 1)])
    return join_pieces(flags, mine, other)


def solution(mesh):
    split = Mesh(mesh.devices.reshape(8, 2, 8, 2, 2), ALL)
    rows = P(ALL, None)
    columns = P(None, SHARD)
    return jax.shard_map(
        shards,
        mesh=split,
        in_specs=(rows, rows, P(ALL), columns, columns),
        out_specs=columns,
        check_vma=False,
    )
```

```python
import functools
import math

import jax
import jax.numpy as jnp
from jax import lax
from jax.experimental import pallas as pl
from jax.experimental.pallas import tpu as pltpu
from jax.sharding import Mesh
from jax.sharding import PartitionSpec as P

ALL = ("y", "core", "z", "xhi", "xlo")
SHARD = ("z", "xhi", "xlo")
COLUMN_PEERS = ("y", "xhi", "xlo")
ROW_PEERS = ("core", "z")
PIECE_PEERS = ("xlo", "xhi", "y")
SHARD_PEERS = ("xhi", "y")
LANES = 128
CHUNK = 1024
EXTRA = 8
VMEM_LIMIT = 20 * 1024 * 1024
LOG2E = math.log2(math.e)
IN_VMEM = pl.BlockSpec(memory_space=pltpu.VMEM)
IN_HBM = pl.BlockSpec(memory_space=pltpu.HBM)
IN_SMEM = pl.BlockSpec(memory_space=pltpu.SMEM)

epsilon = 1e-06
teacher_scale = 1.0 / 0.07
student_scale = 1.0 / 0.1
grad_factor = 256.0 / 0.1
NT = (((1,), (1,)), ((), ()))
TN = (((0,), (0,)), ((), ()))
f32 = jnp.float32
bf16 = jnp.bfloat16


def params():
    return pltpu.CompilerParams(vmem_limit_bytes=VMEM_LIMIT)


def cost(flops, transcendentals, nbytes):
    return pl.CostEstimate(flops=flops, transcendentals=transcendentals, bytes_accessed=nbytes)


def lane_row(block, start, count):
    return jnp.concatenate([block[start + j : start + j + 1, :] for j in range(count)], axis=1)


def in_hbm(values):
    return pltpu.with_memory_space_constraint(values, pltpu.HBM)


def rows_kernel(mask_ref, teacher_ref, student_ref, out_ref, index_ref, held_ref, made_ref, sems):
    copies = [
        pltpu.make_async_copy(mask_ref, index_ref, sems.at[0]),
        pltpu.make_async_copy(teacher_ref, held_ref.at[0], sems.at[1]),
        pltpu.make_async_copy(student_ref, held_ref.at[1], sems.at[2]),
    ]
    for copy in copies:
        copy.start()
    copies[0].wait()
    patches = teacher_ref.shape[0]
    count = mask_ref.shape[1]
    chosen = lax.broadcasted_iota(jnp.int32, (patches, count), 0) == index_ref[...]
    chosen = chosen.astype(f32).astype(bf16)
    for part in range(2):
        copies[1 + part].wait()
        rows = lax.dot_general(chosen, held_ref[part], TN, preferred_element_type=f32)
        square = jnp.sum(rows * rows, axis=1, keepdims=True)
        made_ref[part * count : (part + 1) * count, :] = (rows * lax.rsqrt(square + epsilon)).astype(bf16)
    sends = [pltpu.make_async_copy(made_ref, out_ref.at[i], sems.at[3 + i]) for i in range(out_ref.shape[0])]
    for send in sends:
        send.start()
    for send in sends:
        send.wait()


def masked_rows(mask, teacher, student, copies):
    count, width = mask.shape[1], teacher.shape[1]
    return pl.pallas_call(
        rows_kernel,
        in_specs=[IN_HBM] * 3,
        out_specs=IN_HBM,
        out_shape=pltpu.HBM((copies, 2 * count, width), bf16),
        scratch_shapes=[
            pltpu.VMEM(mask.shape, jnp.int32),
            pltpu.VMEM((2,) + teacher.shape, bf16),
            pltpu.VMEM((2 * count, width), bf16),
            pltpu.SemaphoreType.DMA((3 + copies,)),
        ],
        compiler_params=params(),
        name="masked_rows",
    )(in_hbm(mask), in_hbm(teacher), in_hbm(student))


def two_shards(flags_ref, own_ref, first_ref, second_ref, act):
    @pl.when(flags_ref[2] == 1)
    def _():
        act(own_ref, first_ref)

    @pl.when(flags_ref[2] == 0)
    def _():
        act(second_ref, first_ref)


def protos_kernel(pieces, flags_ref, own_ref, first_ref, second_ref, out_ref, *rest):
    piece_ref, held_ref, sems = rest if pieces else (None,) + rest

    def bring(one, other):
        copies = [
            pltpu.make_async_copy(one, held_ref.at[0], sems.at[0]),
            pltpu.make_async_copy(other, held_ref.at[1], sems.at[1]),
        ]
        for copy in copies:
            copy.start()
        for copy in copies:
            copy.wait()

    two_shards(flags_ref, own_ref, first_ref, second_ref, bring)
    columns = own_ref.shape[1]
    xlo = flags_ref[1]
    for part, place in ((0, xlo), (1, 1 - xlo)):
        values = held_ref[part].astype(f32)
        square = jnp.sum(values * values, axis=0, keepdims=True)
        at = pl.multiple_of(place * columns, columns)
        out_ref[:, pl.ds(at, columns)] = (values * lax.rsqrt(square + epsilon)).astype(bf16)
    if pieces:
        index = flags_ref[3]
        half = columns // pieces
        block = held_ref[0, :, pl.ds(pl.multiple_of(index // 2 * LANES, LANES), LANES)].astype(f32)
        block = jnp.where(index % 2 == 0, block[:, :half], block[:, half:])
        rows = block.shape[0] // 2
        piece_ref[...] = jnp.concatenate([block[:rows], block[rows:]], axis=1)


def prototypes(flags, own, first, second, pieces=0):
    rows, columns = own.shape
    shapes = [jax.ShapeDtypeStruct((rows, 2 * columns), bf16)]
    if pieces:
        shapes.append(jax.ShapeDtypeStruct((rows // 2, 2 * columns // pieces), f32))
    return pl.pallas_call(
        functools.partial(protos_kernel, pieces),
        in_specs=[IN_SMEM] + [IN_HBM] * 3,
        out_specs=[IN_VMEM] * len(shapes),
        out_shape=shapes,
        scratch_shapes=[pltpu.VMEM((2, rows, columns), bf16), pltpu.SemaphoreType.DMA((2,))],
        compiler_params=params(),
        cost_estimate=cost(4 * rows * columns, 0, 8 * rows * columns),
        name="prototypes",
    )(flags, in_hbm(own), in_hbm(first), in_hbm(second))


def pack_piece(block, piece, pieces):
    rows, columns = block.shape
    width = columns // pieces
    part = block[:, piece * width : (piece + 1) * width]
    return jnp.concatenate([part[: rows // 2], part[rows // 2 :]], axis=1)


def spread_cols(total, cols_ref):
    lines = cols_ref.shape[1]
    block = jnp.concatenate([total[:, j * LANES : (j + 1) * LANES] for j in range(lines)], axis=0)
    cols_ref[...] = jnp.broadcast_to(block[None], cols_ref.shape).astype(bf16)


def net_rows(ref, net):
    blocks, both, width = ref.shape
    count = both // 2
    return ref[:, net * count : (net + 1) * count, :].reshape(blocks * count, width)


def codes_kernel(flags_ref, own_ref, other_ref, protos_ref, codes_ref, cols_ref):
    core = flags_ref[0]
    count = codes_ref.shape[0] // 2
    total = None
    for ref, place in ((own_ref, core), (other_ref, 1 - core)):
        scores = jnp.dot(net_rows(ref, 0), protos_ref[...], preferred_element_type=f32)
        codes = jnp.exp2(scores * (teacher_scale * LOG2E))
        codes_ref[pl.ds(pl.multiple_of(place * count, count), count), :] = codes.astype(bf16)
        sums = jnp.sum(codes, axis=0, keepdims=True)
        total = sums if total is None else total + sums
    spread_cols(total, cols_ref)


def first_codes(flags, own, other, protos, groups):
    blocks, both, width = own.shape
    count = blocks * both
    columns = protos.shape[1]
    return pl.pallas_call(
        codes_kernel,
        in_specs=[IN_SMEM] + [IN_VMEM] * 3,
        out_specs=(IN_VMEM, IN_VMEM),
        out_shape=(
            pltpu.VMEM((count, columns), bf16),
            jax.ShapeDtypeStruct((groups, columns // LANES, LANES), bf16),
        ),
        compiler_params=params(),
        cost_estimate=cost(2 * count * width * columns, count * columns, 2 * count * columns),
        name="first_codes",
    )(flags, own, other, protos)


def sum_lanes(block):
    ones = jnp.ones((16, LANES), bf16)
    sums = lax.dot_general(ones, block.astype(bf16), NT, preferred_element_type=f32)[0:1]
    lines = block.shape[0] // LANES
    return jnp.concatenate([sums[:, j * LANES : (j + 1) * LANES] for j in range(lines)], axis=0)


def row_pass_kernel(stage, *refs):
    recv_ref, codes_ref = refs[:2]
    norm_ref, out_ref = refs[2] if stage else None, refs[-1]
    count = codes_ref.shape[0]
    tiles = recv_ref.shape[1]
    lines = CHUNK // LANES
    scale = lane_row(1.0 / jnp.sum(recv_ref[...].astype(f32), axis=0), 0, tiles).astype(bf16)
    for i in range(count // CHUNK):
        blocks = []
        for k in range(lines):
            at = i * CHUNK + k * LANES
            total = None
            for g in range(0, tiles, 8):
                part = None
                for j in range(g, g + 8):
                    columns = slice(j * LANES, (j + 1) * LANES)
                    term = codes_ref[at : at + LANES, columns] * scale[:, columns]
                    part = term if part is None else part + term
                part = part.astype(f32)
                total = part if total is None else total + part
            blocks.append(total.astype(bf16))
        block = jnp.broadcast_to(sum_lanes(jnp.concatenate(blocks, axis=0))[None], (out_ref.shape[0], lines, LANES))
        out_ref[:, i * lines : (i + 1) * lines, :] = block.astype(bf16)
    first = count // LANES
    if stage == 1:
        for member in range(out_ref.shape[0]):
            line = norm_ref[member : member + 1, :]
            out_ref[member, first:, :] = jnp.broadcast_to(line, (EXTRA, LANES)).astype(bf16)
    if stage == 2:
        total = jnp.sum(norm_ref[:, first : first + 1, :].astype(f32), axis=0)
        high = total.astype(bf16).astype(f32)
        index = lax.broadcasted_iota(jnp.int32, (EXTRA, LANES), 0)
        extra = jnp.where(index == 0, high, jnp.where(index == 1, total - high, 0.0)).astype(bf16)
        out_ref[:, first:, :] = jnp.broadcast_to(extra[None], (out_ref.shape[0], EXTRA, LANES))


def row_pass(recv, codes, members, norm=None, stage=0):
    count, columns = codes.shape
    lines = count // LANES + (EXTRA if stage else 0)
    return pl.pallas_call(
        functools.partial(row_pass_kernel, stage),
        in_specs=[IN_VMEM] * (3 if stage else 2),
        out_specs=IN_VMEM,
        out_shape=jax.ShapeDtypeStruct((members, lines, LANES), bf16),
        compiler_params=params(),
        cost_estimate=cost(2 * count * columns, 0, 2 * count * columns),
        name="row_pass",
    )(recv, codes, *((norm,) if stage else ()))


def col_pass_kernel(recv_ref, codes_ref, cols_ref):
    count, columns = codes_ref.shape
    lines = CHUNK // LANES
    scale = 1.0 / jnp.sum(recv_ref[:, : count // LANES, :].astype(f32), axis=0)
    ones = jnp.ones((16, LANES), bf16)
    first = lax.broadcasted_iota(jnp.int32, (16, CHUNK), 0) == 0
    spreads = []
    for i in range(count // CHUNK):
        row = jnp.where(first, lane_row(scale, i * lines, lines), 0.0).astype(bf16)
        spreads.append(lax.dot_general(row, ones, TN, preferred_element_type=f32).astype(bf16))
    width = 8 * LANES
    totals = []
    for h in range(columns // width):
        total = jnp.zeros((16, width), f32)
        for i, spread in enumerate(spreads):
            for g in range(lines):
                parts = []
                for j in range(width // LANES):
                    part = None
                    for q in range(LANES // 16):
                        at = g * LANES + q * 16
                        lane = h * width + j * LANES
                        term = codes_ref[i * CHUNK + at : i * CHUNK + at + 16, lane : lane + LANES]
                        term = term * spread[at : at + 16]
                        part = term if part is None else part + term
                    parts.append(part.astype(f32))
                total = total + jnp.concatenate(parts, axis=1)
        totals.append(jnp.sum(total, axis=0, keepdims=True))
    spread_cols(jnp.concatenate(totals, axis=1), cols_ref)


def col_pass(recv, codes, groups):
    count, columns = codes.shape
    return pl.pallas_call(
        col_pass_kernel,
        in_specs=[IN_VMEM, IN_VMEM],
        out_specs=IN_VMEM,
        out_shape=jax.ShapeDtypeStruct((groups, columns // LANES, LANES), bf16),
        compiler_params=params(),
        cost_estimate=cost(2 * count * columns, 0, 2 * count * columns),
        name="col_pass",
    )(recv, codes)


def student_kernel(flags_ref, own_ref, other_ref, protos_ref, expo_ref, norm_ref, turned_ref):
    core = flags_ref[0]
    columns = protos_ref.shape[1]
    count = expo_ref.shape[0] // 2
    lines = count // LANES
    for half in range(2):
        rows = jnp.where(core == half, net_rows(own_ref, 1), net_rows(other_ref, 1))
        span = slice(half * count, (half + 1) * count)
        scores = jnp.dot(rows, protos_ref[...], preferred_element_type=f32)
        expo = jnp.exp2(scores * (student_scale * LOG2E))
        expo_ref[span, :] = expo.astype(bf16)
        part = expo[:, :LANES]
        for j in range(1, columns // LANES):
            part = part + expo[:, j * LANES : (j + 1) * LANES]
        norm_ref[half * lines : (half + 1) * lines, :] = sum_lanes(part)
        turned_ref[:, span] = rows.T


def student_expo(flags, own, other, protos):
    blocks, both, width = own.shape
    count = blocks * both
    columns = protos.shape[1]
    return pl.pallas_call(
        student_kernel,
        in_specs=[IN_SMEM] + [IN_VMEM] * 3,
        out_specs=(IN_VMEM,) * 3,
        out_shape=(
            pltpu.VMEM((count, columns), bf16),
            jax.ShapeDtypeStruct((count // LANES, LANES), f32),
            pltpu.VMEM((width, count), bf16),
        ),
        compiler_params=params(),
        cost_estimate=cost(2 * count * width * columns, count * columns, 2 * count * columns),
        name="student_expo",
    )(flags, own, other, protos)


def scaled_product(scale, turned_ref, codes_ref):
    turned = (turned_ref[...].astype(f32) * lane_row(scale, 0, scale.shape[0])).astype(bf16)
    return jnp.dot(turned, codes_ref[...], preferred_element_type=f32)


def grad_kernel(recv_ref, norm_ref, cols_ref, turned_ref, codes_ref, expo_ref, out_ref):
    members = recv_ref.shape[0]
    lines = codes_ref.shape[0] // LANES
    row_scale = 1.0 / jnp.sum(recv_ref[:, :lines, :].astype(f32), axis=0)
    norm = jnp.concatenate(
        [norm_ref[m, lines : lines + 1, :].astype(f32) + norm_ref[m, lines + 1 : lines + 2, :].astype(f32) for m in range(members)],
        axis=0,
    )
    mass = jnp.sum(cols_ref[...].astype(f32), axis=0)
    teach = scaled_product(row_scale, turned_ref, codes_ref) * lane_row(1.0 / mass, 0, cols_ref.shape[1])
    grad = grad_factor * (scaled_product(1.0 / norm, turned_ref, expo_ref) - teach)
    for piece in range(out_ref.shape[0]):
        out_ref[piece] = pack_piece(grad, piece, out_ref.shape[0]).astype(bf16)


def grad_pieces(recv, norm, cols, turned, codes, expo, pieces):
    count, columns = codes.shape
    width = turned.shape[0]
    return pl.pallas_call(
        grad_kernel,
        in_specs=[IN_VMEM] * 6,
        out_specs=IN_VMEM,
        out_shape=jax.ShapeDtypeStruct((pieces, width // 2, 2 * columns // pieces), bf16),
        compiler_params=params(),
        cost_estimate=cost(4 * count * width * columns, 0, 4 * count * columns),
        name="grad_pieces",
    )(recv, norm, cols, turned, codes, expo)


def back_kernel(recv_ref, weight_ref, out_ref):
    grad = jnp.sum(recv_ref[...].astype(f32), axis=0)
    weight = weight_ref[...]
    half = weight.shape[1] // 2

    def column_sum(values):
        total = jnp.sum(values, axis=0, keepdims=True)
        return total + jnp.concatenate([total[:, half:], total[:, :half]], axis=1)

    inverse = lax.rsqrt(column_sum(weight * weight) + epsilon)
    along = column_sum(grad * weight)
    back = (grad * inverse - weight * (inverse * inverse * inverse * along)).astype(bf16)
    out_ref[...] = back


def weight_back(recv, weight):
    return pl.pallas_call(
        back_kernel,
        in_specs=[IN_VMEM, IN_VMEM],
        out_specs=IN_VMEM,
        out_shape=jax.ShapeDtypeStruct(weight.shape, bf16),
        compiler_params=params(),
        name="weight_back",
    )(recv, weight)


def join_kernel(pieces_ref, out_ref):
    pieces, rows, lanes = pieces_ref.shape
    half = lanes // 2
    for pair in range(pieces // 2):
        at = [2 * (index % (pieces // 2)) + index // (pieces // 2) for index in (2 * pair, 2 * pair + 1)]
        left, right = pieces_ref[at[0]], pieces_ref[at[1]]
        columns = pl.ds(pair * lanes, lanes)
        out_ref[:rows, columns] = jnp.concatenate([left[:, :half], right[:, :half]], axis=1)
        out_ref[rows:, columns] = jnp.concatenate([left[:, half:], right[:, half:]], axis=1)


def join_pieces(pieces):
    count, rows, lanes = pieces.shape
    return pl.pallas_call(
        join_kernel,
        in_specs=[IN_VMEM],
        out_specs=IN_VMEM,
        out_shape=jax.ShapeDtypeStruct((2 * rows, count * lanes // 2), pieces.dtype),
        compiler_params=params(),
        name="join_pieces",
    )(pieces)


def exchange(values, axes):
    return lax.all_to_all(values, axes, 0, 0, tiled=True)


def shard_permutes(weight, pair):
    axes = ("core", "xhi", "xlo")
    first, second = [], []
    for core in range(2):
        for xhi in range(2):
            for xlo in range(2):
                here = core * 4 + xhi * 2 + xlo
                if xhi == core:
                    first.append((core * 4 + xhi * 2 + 1 - xlo, here))
                else:
                    first.append(((1 - core) * 4 + core * 2 + 1 - xlo, here))
                    second.append((core * 4 + (xhi if pair else core) * 2 + 1 - xlo, here))
    once = lax.ppermute(weight, axes, first)
    return once, lax.ppermute(once, axes, second)


def shards(teacher_patches, student_patches, mask_index, teacher_weight, student_weight):
    size = lax.axis_size
    column_peers, row_peers = size(COLUMN_PEERS), size(ROW_PEERS)
    shard_pieces = size(SHARD_PEERS)
    core, xhi, xlo = lax.axis_index("core"), lax.axis_index("xhi"), lax.axis_index("xlo")
    matched = (core == xhi).astype(jnp.int32)
    flags = jnp.stack([core, xlo, matched, lax.axis_index(SHARD_PEERS)]).astype(jnp.int32)

    teach_first, teach_second = shard_permutes(teacher_weight, True)
    stud_first, stud_second = shard_permutes(student_weight, False)
    line = masked_rows(mask_index.reshape(1, -1), teacher_patches, student_patches, size("z"))
    line = exchange(line, "z")
    line, teach_first, teach_second, stud_first, stud_second = lax.optimization_barrier(
        (line, teach_first, teach_second, stud_first, stud_second)
    )
    other = lax.ppermute(line, "core", [(0, 1), (1, 0)])
    (teach_protos,) = prototypes(flags, teacher_weight, teach_first, teach_second)
    stud_protos, weight = prototypes(flags, student_weight, stud_first, stud_second, shard_pieces)
    other, teach_protos, stud_protos, weight = lax.optimization_barrier((other, teach_protos, stud_protos, weight))

    codes, cols = first_codes(flags, line, other, teach_protos, column_peers)
    expo, norm, turned = student_expo(flags, line, other, stud_protos)
    cols, expo, norm, turned = lax.optimization_barrier((cols, expo, norm, turned))
    cols = exchange(cols, COLUMN_PEERS)
    rows = exchange(row_pass(cols, codes, row_peers, norm, 1), ROW_PEERS)
    cols = exchange(col_pass(rows, codes, column_peers), COLUMN_PEERS)
    rows = exchange(row_pass(cols, codes, row_peers, rows, 2), ROW_PEERS)
    norm = rows
    cols = exchange(col_pass(rows, codes, column_peers), COLUMN_PEERS)
    rows = exchange(row_pass(cols, codes, row_peers), ROW_PEERS)
    pieces = exchange(grad_pieces(rows, norm, cols, turned, codes, expo, 2 * shard_pieces), PIECE_PEERS)
    mine = weight_back(pieces, weight)
    other = lax.ppermute(mine, ("core", "xhi"), [(1, 2), (2, 1)])
    piece = jnp.where(matched == 1, mine, other)
    return join_pieces(lax.all_gather(piece, ("y", "core"), axis=0))


def solution(mesh):
    split = Mesh(mesh.devices.reshape(8, 2, 8, 2, 2), ALL)
    rows = P(ALL, None)
    columns = P(None, SHARD)
    return jax.shard_map(
        shards,
        mesh=split,
        in_specs=(rows, rows, P(ALL), columns, columns),
        out_specs=columns,
        check_vma=False,
    )
```

```python
import functools
import math

import jax
import jax.numpy as jnp
from jax import lax
from jax.experimental import pallas as pl
from jax.experimental.pallas import tpu as pltpu
from jax.sharding import Mesh
from jax.sharding import PartitionSpec as P

ALL = ("y", "core", "z", "xhi", "xlo")
SHARD = ("z", "xhi", "xlo")
COLUMN_PEERS = ("y", "xhi", "xlo")
ROW_PEERS = ("core", "z")
PIECE_PEERS = ("xlo", "xhi", "y")
SHARD_PEERS = ("xhi", "y")
LANES = 128
CHUNK = 1024
EXTRA = 8
VMEM_LIMIT = 20 * 1024 * 1024
LOG2E = math.log2(math.e)
IN_VMEM = pl.BlockSpec(memory_space=pltpu.VMEM)
IN_HBM = pl.BlockSpec(memory_space=pltpu.HBM)
IN_SMEM = pl.BlockSpec(memory_space=pltpu.SMEM)

epsilon = 1e-06
teacher_scale = 1.0 / 0.07
student_scale = 1.0 / 0.1
grad_factor = 256.0 / 0.1
NT = (((1,), (1,)), ((), ()))
TN = (((0,), (0,)), ((), ()))
f32 = jnp.float32
bf16 = jnp.bfloat16


def params():
    return pltpu.CompilerParams(vmem_limit_bytes=VMEM_LIMIT)


def cost(flops, transcendentals, nbytes):
    return pl.CostEstimate(flops=flops, transcendentals=transcendentals, bytes_accessed=nbytes)


def lane_row(block, start, count):
    return jnp.concatenate([block[start + j : start + j + 1, :] for j in range(count)], axis=1)


def in_hbm(values):
    return pltpu.with_memory_space_constraint(values, pltpu.HBM)


def rows_kernel(mask_ref, teacher_ref, student_ref, out_ref, index_ref, held_ref, made_ref, sems):
    copies = [
        pltpu.make_async_copy(mask_ref, index_ref, sems.at[0]),
        pltpu.make_async_copy(teacher_ref, held_ref.at[0], sems.at[1]),
        pltpu.make_async_copy(student_ref, held_ref.at[1], sems.at[2]),
    ]
    for copy in copies:
        copy.start()
    copies[0].wait()
    patches = teacher_ref.shape[0]
    count = mask_ref.shape[1]
    chosen = lax.broadcasted_iota(jnp.int32, (patches, count), 0) == index_ref[...]
    chosen = chosen.astype(f32).astype(bf16)
    for part in range(2):
        copies[1 + part].wait()
        rows = lax.dot_general(chosen, held_ref[part], TN, preferred_element_type=f32)
        square = jnp.sum(rows * rows, axis=1, keepdims=True)
        made_ref[part * count : (part + 1) * count, :] = (rows * lax.rsqrt(square + epsilon)).astype(bf16)
    sends = [pltpu.make_async_copy(made_ref, out_ref.at[i], sems.at[3 + i]) for i in range(out_ref.shape[0])]
    for send in sends:
        send.start()
    for send in sends:
        send.wait()


def masked_rows(mask, teacher, student, copies):
    count, width = mask.shape[1], teacher.shape[1]
    return pl.pallas_call(
        rows_kernel,
        in_specs=[IN_HBM] * 3,
        out_specs=IN_HBM,
        out_shape=pltpu.HBM((copies, 2 * count, width), bf16),
        scratch_shapes=[
            pltpu.VMEM(mask.shape, jnp.int32),
            pltpu.VMEM((2,) + teacher.shape, bf16),
            pltpu.VMEM((2 * count, width), bf16),
            pltpu.SemaphoreType.DMA((3 + copies,)),
        ],
        compiler_params=params(),
        name="masked_rows",
    )(in_hbm(mask), in_hbm(teacher), in_hbm(student))


def two_shards(flags_ref, own_ref, first_ref, second_ref, act):
    @pl.when(flags_ref[2] == 1)
    def _():
        act(own_ref, first_ref)

    @pl.when(flags_ref[2] == 0)
    def _():
        act(second_ref, first_ref)


def protos_kernel(pieces, flags_ref, own_ref, first_ref, second_ref, out_ref, *rest):
    piece_ref, held_ref, sems = rest if pieces else (None,) + rest

    def bring(one, other):
        copies = [
            pltpu.make_async_copy(one, held_ref.at[0], sems.at[0]),
            pltpu.make_async_copy(other, held_ref.at[1], sems.at[1]),
        ]
        for copy in copies:
            copy.start()
        for copy in copies:
            copy.wait()

    two_shards(flags_ref, own_ref, first_ref, second_ref, bring)
    columns = own_ref.shape[1]
    xlo = flags_ref[1]
    for part, place in ((0, xlo), (1, 1 - xlo)):
        values = held_ref[part].astype(f32)
        square = jnp.sum(values * values, axis=0, keepdims=True)
        at = pl.multiple_of(place * columns, columns)
        out_ref[:, pl.ds(at, columns)] = (values * lax.rsqrt(square + epsilon)).astype(bf16)
    if pieces:
        index = flags_ref[3]
        half = columns // pieces
        block = held_ref[0, :, pl.ds(pl.multiple_of(index // 2 * LANES, LANES), LANES)].astype(f32)
        block = jnp.where(index % 2 == 0, block[:, :half], block[:, half:])
        rows = block.shape[0] // 2
        piece_ref[...] = jnp.concatenate([block[:rows], block[rows:]], axis=1)


def prototypes(flags, own, first, second, pieces=0):
    rows, columns = own.shape
    shapes = [jax.ShapeDtypeStruct((rows, 2 * columns), bf16)]
    if pieces:
        shapes.append(jax.ShapeDtypeStruct((rows // 2, 2 * columns // pieces), f32))
    return pl.pallas_call(
        functools.partial(protos_kernel, pieces),
        in_specs=[IN_SMEM] + [IN_HBM] * 3,
        out_specs=[IN_VMEM] * len(shapes),
        out_shape=shapes,
        scratch_shapes=[pltpu.VMEM((2, rows, columns), bf16), pltpu.SemaphoreType.DMA((2,))],
        compiler_params=params(),
        cost_estimate=cost(4 * rows * columns, 0, 8 * rows * columns),
        name="prototypes",
    )(flags, in_hbm(own), in_hbm(first), in_hbm(second))


def pack_piece(block, piece, pieces):
    rows, columns = block.shape
    width = columns // pieces
    part = block[:, piece * width : (piece + 1) * width]
    return jnp.concatenate([part[: rows // 2], part[rows // 2 :]], axis=1)


def spread_cols(total, cols_ref):
    lines = cols_ref.shape[1]
    block = jnp.concatenate([total[:, j * LANES : (j + 1) * LANES] for j in range(lines)], axis=0)
    cols_ref[...] = jnp.broadcast_to(block[None], cols_ref.shape).astype(bf16)


def net_rows(ref, net):
    blocks, both, width = ref.shape
    count = both // 2
    return ref[:, net * count : (net + 1) * count, :].reshape(blocks * count, width)


def codes_kernel(flags_ref, own_ref, other_ref, protos_ref, codes_ref, cols_ref):
    core = flags_ref[0]
    count = codes_ref.shape[0] // 2
    total = None
    for ref, place in ((own_ref, core), (other_ref, 1 - core)):
        scores = jnp.dot(net_rows(ref, 0), protos_ref[...], preferred_element_type=f32)
        codes = jnp.exp2(scores * (teacher_scale * LOG2E))
        codes_ref[pl.ds(pl.multiple_of(place * count, count), count), :] = codes.astype(bf16)
        sums = jnp.sum(codes, axis=0, keepdims=True)
        total = sums if total is None else total + sums
    spread_cols(total, cols_ref)


def first_codes(flags, own, other, protos, groups):
    blocks, both, width = own.shape
    count = blocks * both
    columns = protos.shape[1]
    return pl.pallas_call(
        codes_kernel,
        in_specs=[IN_SMEM] + [IN_VMEM] * 3,
        out_specs=(IN_VMEM, IN_VMEM),
        out_shape=(
            pltpu.VMEM((count, columns), bf16),
            jax.ShapeDtypeStruct((groups, columns // LANES, LANES), bf16),
        ),
        compiler_params=params(),
        cost_estimate=cost(2 * count * width * columns, count * columns, 2 * count * columns),
        name="first_codes",
    )(flags, own, other, protos)


def sum_lanes(block):
    ones = jnp.ones((16, LANES), bf16)
    sums = lax.dot_general(ones, block.astype(bf16), NT, preferred_element_type=f32)[0:1]
    lines = block.shape[0] // LANES
    return jnp.concatenate([sums[:, j * LANES : (j + 1) * LANES] for j in range(lines)], axis=0)


def row_pass_kernel(stage, *refs):
    recv_ref, codes_ref = refs[:2]
    norm_ref, out_ref = refs[2] if stage else None, refs[-1]
    count = codes_ref.shape[0]
    tiles = recv_ref.shape[1]
    lines = CHUNK // LANES
    scale = lane_row(1.0 / jnp.sum(recv_ref[...].astype(f32), axis=0), 0, tiles).astype(bf16)
    for i in range(count // CHUNK):
        blocks = []
        for k in range(lines):
            at = i * CHUNK + k * LANES
            total = None
            for g in range(0, tiles, 8):
                part = None
                for j in range(g, g + 8):
                    columns = slice(j * LANES, (j + 1) * LANES)
                    term = codes_ref[at : at + LANES, columns] * scale[:, columns]
                    part = term if part is None else part + term
                part = part.astype(f32)
                total = part if total is None else total + part
            blocks.append(total.astype(bf16))
        block = jnp.broadcast_to(sum_lanes(jnp.concatenate(blocks, axis=0))[None], (out_ref.shape[0], lines, LANES))
        out_ref[:, i * lines : (i + 1) * lines, :] = block.astype(bf16)
    first = count // LANES
    if stage == 1:
        for member in range(out_ref.shape[0]):
            line = norm_ref[member : member + 1, :]
            out_ref[member, first:, :] = jnp.broadcast_to(line, (EXTRA, LANES)).astype(bf16)
    if stage == 2:
        total = jnp.sum(norm_ref[:, first : first + 1, :].astype(f32), axis=0)
        high = total.astype(bf16).astype(f32)
        index = lax.broadcasted_iota(jnp.int32, (EXTRA, LANES), 0)
        extra = jnp.where(index == 0, high, jnp.where(index == 1, total - high, 0.0)).astype(bf16)
        out_ref[:, first:, :] = jnp.broadcast_to(extra[None], (out_ref.shape[0], EXTRA, LANES))


def row_pass(recv, codes, members, norm=None, stage=0):
    count, columns = codes.shape
    lines = count // LANES + (EXTRA if stage else 0)
    return pl.pallas_call(
        functools.partial(row_pass_kernel, stage),
        in_specs=[IN_VMEM] * (3 if stage else 2),
        out_specs=IN_VMEM,
        out_shape=jax.ShapeDtypeStruct((members, lines, LANES), bf16),
        compiler_params=params(),
        cost_estimate=cost(2 * count * columns, 0, 2 * count * columns),
        name="row_pass",
    )(recv, codes, *((norm,) if stage else ()))


def col_pass_kernel(recv_ref, codes_ref, cols_ref):
    count, columns = codes_ref.shape
    lines = CHUNK // LANES
    scale = 1.0 / jnp.sum(recv_ref[:, : count // LANES, :].astype(f32), axis=0)
    ones = jnp.ones((16, LANES), bf16)
    first = lax.broadcasted_iota(jnp.int32, (16, CHUNK), 0) == 0
    spreads = []
    for i in range(count // CHUNK):
        row = jnp.where(first, lane_row(scale, i * lines, lines), 0.0).astype(bf16)
        spreads.append(lax.dot_general(row, ones, TN, preferred_element_type=f32).astype(bf16))
    width = 8 * LANES
    totals = []
    for h in range(columns // width):
        total = jnp.zeros((16, width), f32)
        for i, spread in enumerate(spreads):
            for g in range(lines):
                parts = []
                for j in range(width // LANES):
                    part = None
                    for q in range(LANES // 16):
                        at = g * LANES + q * 16
                        lane = h * width + j * LANES
                        term = codes_ref[i * CHUNK + at : i * CHUNK + at + 16, lane : lane + LANES]
                        term = term * spread[at : at + 16]
                        part = term if part is None else part + term
                    parts.append(part.astype(f32))
                total = total + jnp.concatenate(parts, axis=1)
        totals.append(jnp.sum(total, axis=0, keepdims=True))
    spread_cols(jnp.concatenate(totals, axis=1), cols_ref)


def col_pass(recv, codes, groups):
    count, columns = codes.shape
    return pl.pallas_call(
        col_pass_kernel,
        in_specs=[IN_VMEM, IN_VMEM],
        out_specs=IN_VMEM,
        out_shape=jax.ShapeDtypeStruct((groups, columns // LANES, LANES), bf16),
        compiler_params=params(),
        cost_estimate=cost(2 * count * columns, 0, 2 * count * columns),
        name="col_pass",
    )(recv, codes)


def student_kernel(flags_ref, own_ref, other_ref, protos_ref, expo_ref, norm_ref, turned_ref):
    core = flags_ref[0]
    columns = protos_ref.shape[1]
    count = expo_ref.shape[0] // 2
    lines = count // LANES
    for half in range(2):
        rows = jnp.where(core == half, net_rows(own_ref, 1), net_rows(other_ref, 1))
        span = slice(half * count, (half + 1) * count)
        scores = jnp.dot(rows, protos_ref[...], preferred_element_type=f32)
        expo = jnp.exp2(scores * (student_scale * LOG2E))
        expo_ref[span, :] = expo.astype(bf16)
        part = expo[:, :LANES]
        for j in range(1, columns // LANES):
            part = part + expo[:, j * LANES : (j + 1) * LANES]
        norm_ref[half * lines : (half + 1) * lines, :] = sum_lanes(part)
        turned_ref[:, span] = rows.T


def student_expo(flags, own, other, protos):
    blocks, both, width = own.shape
    count = blocks * both
    columns = protos.shape[1]
    return pl.pallas_call(
        student_kernel,
        in_specs=[IN_SMEM] + [IN_VMEM] * 3,
        out_specs=(IN_VMEM,) * 3,
        out_shape=(
            pltpu.VMEM((count, columns), bf16),
            jax.ShapeDtypeStruct((count // LANES, LANES), f32),
            pltpu.VMEM((width, count), bf16),
        ),
        compiler_params=params(),
        cost_estimate=cost(2 * count * width * columns, count * columns, 2 * count * columns),
        name="student_expo",
    )(flags, own, other, protos)


def scaled_product(scale, turned_ref, codes_ref):
    turned = (turned_ref[...].astype(f32) * lane_row(scale, 0, scale.shape[0])).astype(bf16)
    return jnp.dot(turned, codes_ref[...], preferred_element_type=f32)


def grad_kernel(recv_ref, norm_ref, cols_ref, turned_ref, codes_ref, expo_ref, out_ref):
    members = recv_ref.shape[0]
    lines = codes_ref.shape[0] // LANES
    row_scale = 1.0 / jnp.sum(recv_ref[:, :lines, :].astype(f32), axis=0)
    norm = jnp.concatenate(
        [norm_ref[m, lines : lines + 1, :].astype(f32) + norm_ref[m, lines + 1 : lines + 2, :].astype(f32) for m in range(members)],
        axis=0,
    )
    mass = jnp.sum(cols_ref[...].astype(f32), axis=0)
    teach = scaled_product(row_scale, turned_ref, codes_ref) * lane_row(1.0 / mass, 0, cols_ref.shape[1])
    grad = grad_factor * (scaled_product(1.0 / norm, turned_ref, expo_ref) - teach)
    for piece in range(out_ref.shape[0]):
        out_ref[piece] = pack_piece(grad, piece, out_ref.shape[0]).astype(bf16)


def grad_pieces(recv, norm, cols, turned, codes, expo, pieces):
    count, columns = codes.shape
    width = turned.shape[0]
    return pl.pallas_call(
        grad_kernel,
        in_specs=[IN_VMEM] * 6,
        out_specs=IN_VMEM,
        out_shape=jax.ShapeDtypeStruct((pieces, width // 2, 2 * columns // pieces), bf16),
        compiler_params=params(),
        cost_estimate=cost(4 * count * width * columns, 0, 4 * count * columns),
        name="grad_pieces",
    )(recv, norm, cols, turned, codes, expo)


def back_kernel(recv_ref, weight_ref, out_ref):
    grad = jnp.sum(recv_ref[...].astype(f32), axis=0)
    weight = weight_ref[...]
    half = weight.shape[1] // 2

    def column_sum(values):
        total = jnp.sum(values, axis=0, keepdims=True)
        return total + jnp.concatenate([total[:, half:], total[:, :half]], axis=1)

    inverse = lax.rsqrt(column_sum(weight * weight) + epsilon)
    along = column_sum(grad * weight)
    back = (grad * inverse - weight * (inverse * inverse * inverse * along)).astype(bf16)
    out_ref[...] = back


def weight_back(recv, weight):
    return pl.pallas_call(
        back_kernel,
        in_specs=[IN_VMEM, IN_VMEM],
        out_specs=IN_VMEM,
        out_shape=jax.ShapeDtypeStruct(weight.shape, bf16),
        compiler_params=params(),
        name="weight_back",
    )(recv, weight)


def join_kernel(pieces_ref, out_ref):
    pieces, rows, lanes = pieces_ref.shape
    half = lanes // 2
    for pair in range(pieces // 2):
        at = [2 * (index % (pieces // 2)) + index // (pieces // 2) for index in (2 * pair, 2 * pair + 1)]
        left, right = pieces_ref[at[0]], pieces_ref[at[1]]
        columns = pl.ds(pair * lanes, lanes)
        out_ref[:rows, columns] = jnp.concatenate([left[:, :half], right[:, :half]], axis=1)
        out_ref[rows:, columns] = jnp.concatenate([left[:, half:], right[:, half:]], axis=1)


def join_pieces(pieces):
    count, rows, lanes = pieces.shape
    return pl.pallas_call(
        join_kernel,
        in_specs=[IN_VMEM],
        out_specs=IN_VMEM,
        out_shape=jax.ShapeDtypeStruct((2 * rows, count * lanes // 2), pieces.dtype),
        compiler_params=params(),
        name="join_pieces",
    )(pieces)


def exchange(values, axes):
    return lax.all_to_all(values, axes, 0, 0, tiled=True)


def shard_permutes(weight, pair):
    axes = ("core", "xhi", "xlo")
    first, second = [], []
    for core in range(2):
        for xhi in range(2):
            for xlo in range(2):
                here = core * 4 + xhi * 2 + xlo
                if xhi == core:
                    first.append((core * 4 + xhi * 2 + 1 - xlo, here))
                else:
                    first.append(((1 - core) * 4 + core * 2 + 1 - xlo, here))
                    second.append((core * 4 + (xhi if pair else core) * 2 + 1 - xlo, here))
    once = lax.ppermute(weight, axes, first)
    return once, lax.ppermute(once, axes, second)


def shards(teacher_patches, student_patches, mask_index, teacher_weight, student_weight):
    size = lax.axis_size
    column_peers, row_peers = size(COLUMN_PEERS), size(ROW_PEERS)
    shard_pieces = size(SHARD_PEERS)
    core, xhi, xlo = lax.axis_index("core"), lax.axis_index("xhi"), lax.axis_index("xlo")
    matched = (core == xhi).astype(jnp.int32)
    flags = jnp.stack([core, xlo, matched, lax.axis_index(SHARD_PEERS)]).astype(jnp.int32)

    teach_first, teach_second = shard_permutes(teacher_weight, True)
    stud_first, stud_second = shard_permutes(student_weight, False)
    line = masked_rows(mask_index.reshape(1, -1), teacher_patches, student_patches, size("z"))
    line = exchange(line, "z")
    (teach_protos,) = prototypes(flags, teacher_weight, teach_first, teach_second)
    line, teach_protos, stud_first, stud_second = lax.optimization_barrier((line, teach_protos, stud_first, stud_second))
    other = lax.ppermute(line, "core", [(0, 1), (1, 0)])
    stud_protos, weight = prototypes(flags, student_weight, stud_first, stud_second, shard_pieces)
    other, teach_protos, stud_protos, weight = lax.optimization_barrier((other, teach_protos, stud_protos, weight))

    codes, cols = first_codes(flags, line, other, teach_protos, column_peers)
    expo, norm, turned = student_expo(flags, line, other, stud_protos)
    cols, expo, norm, turned = lax.optimization_barrier((cols, expo, norm, turned))
    cols = exchange(cols, COLUMN_PEERS)
    rows = exchange(row_pass(cols, codes, row_peers, norm, 1), ROW_PEERS)
    cols = exchange(col_pass(rows, codes, column_peers), COLUMN_PEERS)
    rows = exchange(row_pass(cols, codes, row_peers, rows, 2), ROW_PEERS)
    norm = rows
    cols = exchange(col_pass(rows, codes, column_peers), COLUMN_PEERS)
    rows = exchange(row_pass(cols, codes, row_peers), ROW_PEERS)
    pieces = exchange(grad_pieces(rows, norm, cols, turned, codes, expo, 2 * shard_pieces), PIECE_PEERS)
    mine = weight_back(pieces, weight)
    other = lax.ppermute(mine, ("core", "xhi"), [(1, 2), (2, 1)])
    piece = jnp.where(matched == 1, mine, other)
    return join_pieces(lax.all_gather(piece, ("y", "core"), axis=0))


def solution(mesh):
    split = Mesh(mesh.devices.reshape(8, 2, 8, 2, 2), ALL)
    rows = P(ALL, None)
    columns = P(None, SHARD)
    return jax.shard_map(
        shards,
        mesh=split,
        in_specs=(rows, rows, P(ALL), columns, columns),
        out_specs=columns,
        check_vma=False,
    )
```

```python
import functools
import math

import jax
import jax.numpy as jnp
from jax import lax
from jax.experimental import pallas as pl
from jax.experimental.pallas import tpu as pltpu
from jax.sharding import Mesh
from jax.sharding import PartitionSpec as P

ALL = ("y", "core", "z", "xhi", "xlo")
SHARD = ("z", "xhi", "xlo")
COLUMN_PEERS = ("y", "xhi", "xlo")
ROW_PEERS = ("core", "z")
LINE_PEERS = ("xlo", "xhi")
SHARD_PEERS = ("xhi", "y")
LANES = 128
CHUNK = 1024
EXTRA = 8
VMEM_LIMIT = 20 * 1024 * 1024
LOG2E = math.log2(math.e)
IN_VMEM = pl.BlockSpec(memory_space=pltpu.VMEM)
IN_HBM = pl.BlockSpec(memory_space=pltpu.HBM)
IN_SMEM = pl.BlockSpec(memory_space=pltpu.SMEM)

epsilon = 1e-06
teacher_scale = 1.0 / 0.07
student_scale = 1.0 / 0.1
grad_factor = 256.0 / 0.1
NT = (((1,), (1,)), ((), ()))
TN = (((0,), (0,)), ((), ()))
f32 = jnp.float32
bf16 = jnp.bfloat16


def params():
    return pltpu.CompilerParams(vmem_limit_bytes=VMEM_LIMIT)


def cost(flops, transcendentals, nbytes):
    return pl.CostEstimate(flops=flops, transcendentals=transcendentals, bytes_accessed=nbytes)


def lane_row(block, start, count):
    return jnp.concatenate([block[start + j : start + j + 1, :] for j in range(count)], axis=1)


def in_hbm(values):
    return pltpu.with_memory_space_constraint(values, pltpu.HBM)


def rows_kernel(mask_ref, teacher_ref, student_ref, out_ref, index_ref, held_ref, made_ref, sems):
    copies = [
        pltpu.make_async_copy(mask_ref, index_ref, sems.at[0]),
        pltpu.make_async_copy(teacher_ref, held_ref.at[0], sems.at[1]),
        pltpu.make_async_copy(student_ref, held_ref.at[1], sems.at[2]),
    ]
    for copy in copies:
        copy.start()
    copies[0].wait()
    patches = teacher_ref.shape[0]
    count = mask_ref.shape[1]
    chosen = lax.broadcasted_iota(jnp.int32, (patches, count), 0) == index_ref[...]
    chosen = chosen.astype(f32).astype(bf16)
    for part in range(2):
        copies[1 + part].wait()
        rows = lax.dot_general(chosen, held_ref[part], TN, preferred_element_type=f32)
        square = jnp.sum(rows * rows, axis=1, keepdims=True)
        made_ref[part * count : (part + 1) * count, :] = (rows * lax.rsqrt(square + epsilon)).astype(bf16)
    sends = [pltpu.make_async_copy(made_ref, out_ref.at[i], sems.at[3 + i]) for i in range(out_ref.shape[0])]
    for send in sends:
        send.start()
    for send in sends:
        send.wait()


def masked_rows(mask, teacher, student, copies):
    count, width = mask.shape[1], teacher.shape[1]
    return pl.pallas_call(
        rows_kernel,
        in_specs=[IN_HBM] * 3,
        out_specs=IN_HBM,
        out_shape=pltpu.HBM((copies, 2 * count, width), bf16),
        scratch_shapes=[
            pltpu.VMEM(mask.shape, jnp.int32),
            pltpu.VMEM((2,) + teacher.shape, bf16),
            pltpu.VMEM((2 * count, width), bf16),
            pltpu.SemaphoreType.DMA((3 + copies,)),
        ],
        compiler_params=params(),
        name="masked_rows",
    )(in_hbm(mask), in_hbm(teacher), in_hbm(student))


def two_shards(flags_ref, own_ref, first_ref, second_ref, act):
    @pl.when(flags_ref[2] == 1)
    def _():
        act(own_ref, first_ref)

    @pl.when(flags_ref[2] == 0)
    def _():
        act(second_ref, first_ref)


def protos_kernel(pieces, flags_ref, own_ref, first_ref, second_ref, out_ref, *rest):
    piece_ref, held_ref, sems = rest if pieces else (None,) + rest

    def bring(one, other):
        copies = [
            pltpu.make_async_copy(one, held_ref.at[0], sems.at[0]),
            pltpu.make_async_copy(other, held_ref.at[1], sems.at[1]),
        ]
        for copy in copies:
            copy.start()
        for copy in copies:
            copy.wait()

    two_shards(flags_ref, own_ref, first_ref, second_ref, bring)
    columns = own_ref.shape[1]
    xlo = flags_ref[1]
    for part, place in ((0, xlo), (1, 1 - xlo)):
        values = held_ref[part].astype(f32)
        square = jnp.sum(values * values, axis=0, keepdims=True)
        at = pl.multiple_of(place * columns, columns)
        out_ref[:, pl.ds(at, columns)] = (values * lax.rsqrt(square + epsilon)).astype(bf16)
    if pieces:
        index = flags_ref[3]
        half = columns // pieces
        block = held_ref[0, :, pl.ds(pl.multiple_of(index // 2 * LANES, LANES), LANES)].astype(f32)
        block = jnp.where(index % 2 == 0, block[:, :half], block[:, half:])
        rows = block.shape[0] // 2
        piece_ref[...] = jnp.concatenate([block[:rows], block[rows:]], axis=1)


def prototypes(flags, own, first, second, pieces=0):
    rows, columns = own.shape
    shapes = [jax.ShapeDtypeStruct((rows, 2 * columns), bf16)]
    if pieces:
        shapes.append(jax.ShapeDtypeStruct((rows // 2, 2 * columns // pieces), f32))
    return pl.pallas_call(
        functools.partial(protos_kernel, pieces),
        in_specs=[IN_SMEM] + [IN_HBM] * 3,
        out_specs=[IN_VMEM] * len(shapes),
        out_shape=shapes,
        scratch_shapes=[pltpu.VMEM((2, rows, columns), bf16), pltpu.SemaphoreType.DMA((2,))],
        compiler_params=params(),
        cost_estimate=cost(4 * rows * columns, 0, 8 * rows * columns),
        name="prototypes",
    )(flags, in_hbm(own), in_hbm(first), in_hbm(second))


def pack_piece(block, piece, pieces):
    rows, columns = block.shape
    width = columns // pieces
    part = block[:, piece * width : (piece + 1) * width]
    return jnp.concatenate([part[: rows // 2], part[rows // 2 :]], axis=1)


def spread_cols(total, cols_ref):
    lines = cols_ref.shape[1]
    block = jnp.concatenate([total[:, j * LANES : (j + 1) * LANES] for j in range(lines)], axis=0)
    cols_ref[...] = jnp.broadcast_to(block[None], cols_ref.shape).astype(bf16)


def net_rows(ref, net):
    blocks, both, width = ref.shape
    count = both // 2
    return ref[:, net * count : (net + 1) * count, :].reshape(blocks * count, width)


def codes_kernel(flags_ref, own_ref, other_ref, protos_ref, codes_ref, cols_ref):
    core = flags_ref[0]
    count = codes_ref.shape[0] // 2
    total = None
    for ref, place in ((own_ref, core), (other_ref, 1 - core)):
        scores = jnp.dot(net_rows(ref, 0), protos_ref[...], preferred_element_type=f32)
        codes = jnp.exp2(scores * (teacher_scale * LOG2E))
        codes_ref[pl.ds(pl.multiple_of(place * count, count), count), :] = codes.astype(bf16)
        sums = jnp.sum(codes, axis=0, keepdims=True)
        total = sums if total is None else total + sums
    spread_cols(total, cols_ref)


def first_codes(flags, own, other, protos, groups):
    blocks, both, width = own.shape
    count = blocks * both
    columns = protos.shape[1]
    return pl.pallas_call(
        codes_kernel,
        in_specs=[IN_SMEM] + [IN_VMEM] * 3,
        out_specs=(IN_VMEM, IN_VMEM),
        out_shape=(
            pltpu.VMEM((count, columns), bf16),
            jax.ShapeDtypeStruct((groups, columns // LANES, LANES), bf16),
        ),
        compiler_params=params(),
        cost_estimate=cost(2 * count * width * columns, count * columns, 2 * count * columns),
        name="first_codes",
    )(flags, own, other, protos)


def sum_lanes(block):
    ones = jnp.ones((16, LANES), bf16)
    sums = lax.dot_general(ones, block.astype(bf16), NT, preferred_element_type=f32)[0:1]
    lines = block.shape[0] // LANES
    return jnp.concatenate([sums[:, j * LANES : (j + 1) * LANES] for j in range(lines)], axis=0)


def row_pass_kernel(stage, *refs):
    recv_ref, codes_ref = refs[:2]
    norm_ref, out_ref = refs[2] if stage else None, refs[-1]
    count = codes_ref.shape[0]
    tiles = recv_ref.shape[1]
    lines = CHUNK // LANES
    scale = lane_row(1.0 / jnp.sum(recv_ref[...].astype(f32), axis=0), 0, tiles).astype(bf16)
    for i in range(count // CHUNK):
        blocks = []
        for k in range(lines):
            at = i * CHUNK + k * LANES
            total = None
            for g in range(0, tiles, 8):
                part = None
                for j in range(g, g + 8):
                    columns = slice(j * LANES, (j + 1) * LANES)
                    term = codes_ref[at : at + LANES, columns] * scale[:, columns]
                    part = term if part is None else part + term
                part = part.astype(f32)
                total = part if total is None else total + part
            blocks.append(total.astype(bf16))
        block = jnp.broadcast_to(sum_lanes(jnp.concatenate(blocks, axis=0))[None], (out_ref.shape[0], lines, LANES))
        out_ref[:, i * lines : (i + 1) * lines, :] = block.astype(bf16)
    first = count // LANES
    if stage == 1:
        for member in range(out_ref.shape[0]):
            line = norm_ref[member : member + 1, :]
            out_ref[member, first:, :] = jnp.broadcast_to(line, (EXTRA, LANES)).astype(bf16)
    if stage == 2:
        total = jnp.sum(norm_ref[:, first : first + 1, :].astype(f32), axis=0)
        high = total.astype(bf16).astype(f32)
        index = lax.broadcasted_iota(jnp.int32, (EXTRA, LANES), 0)
        extra = jnp.where(index == 0, high, jnp.where(index == 1, total - high, 0.0)).astype(bf16)
        out_ref[:, first:, :] = jnp.broadcast_to(extra[None], (out_ref.shape[0], EXTRA, LANES))


def row_pass(recv, codes, members, norm=None, stage=0):
    count, columns = codes.shape
    lines = count // LANES + (EXTRA if stage else 0)
    return pl.pallas_call(
        functools.partial(row_pass_kernel, stage),
        in_specs=[IN_VMEM] * (3 if stage else 2),
        out_specs=IN_VMEM,
        out_shape=jax.ShapeDtypeStruct((members, lines, LANES), bf16),
        compiler_params=params(),
        cost_estimate=cost(2 * count * columns, 0, 2 * count * columns),
        name="row_pass",
    )(recv, codes, *((norm,) if stage else ()))


def col_pass_kernel(recv_ref, codes_ref, cols_ref):
    count, columns = codes_ref.shape
    lines = CHUNK // LANES
    scale = 1.0 / jnp.sum(recv_ref[:, : count // LANES, :].astype(f32), axis=0)
    ones = jnp.ones((16, LANES), bf16)
    first = lax.broadcasted_iota(jnp.int32, (16, CHUNK), 0) == 0
    spreads = []
    for i in range(count // CHUNK):
        row = jnp.where(first, lane_row(scale, i * lines, lines), 0.0).astype(bf16)
        spreads.append(lax.dot_general(row, ones, TN, preferred_element_type=f32).astype(bf16))
    width = 8 * LANES
    totals = []
    for h in range(columns // width):
        total = jnp.zeros((16, width), f32)
        for i, spread in enumerate(spreads):
            for g in range(lines):
                parts = []
                for j in range(width // LANES):
                    part = None
                    for q in range(LANES // 16):
                        at = g * LANES + q * 16
                        lane = h * width + j * LANES
                        term = codes_ref[i * CHUNK + at : i * CHUNK + at + 16, lane : lane + LANES]
                        term = term * spread[at : at + 16]
                        part = term if part is None else part + term
                    parts.append(part.astype(f32))
                total = total + jnp.concatenate(parts, axis=1)
        totals.append(jnp.sum(total, axis=0, keepdims=True))
    spread_cols(jnp.concatenate(totals, axis=1), cols_ref)


def col_pass(recv, codes, groups):
    count, columns = codes.shape
    return pl.pallas_call(
        col_pass_kernel,
        in_specs=[IN_VMEM, IN_VMEM],
        out_specs=IN_VMEM,
        out_shape=jax.ShapeDtypeStruct((groups, columns // LANES, LANES), bf16),
        compiler_params=params(),
        cost_estimate=cost(2 * count * columns, 0, 2 * count * columns),
        name="col_pass",
    )(recv, codes)


def student_kernel(flags_ref, own_ref, other_ref, protos_ref, expo_ref, norm_ref, turned_ref):
    core = flags_ref[0]
    columns = protos_ref.shape[1]
    count = expo_ref.shape[0] // 2
    lines = count // LANES
    for half in range(2):
        rows = jnp.where(core == half, net_rows(own_ref, 1), net_rows(other_ref, 1))
        span = slice(half * count, (half + 1) * count)
        scores = jnp.dot(rows, protos_ref[...], preferred_element_type=f32)
        expo = jnp.exp2(scores * (student_scale * LOG2E))
        expo_ref[span, :] = expo.astype(bf16)
        part = expo[:, :LANES]
        for j in range(1, columns // LANES):
            part = part + expo[:, j * LANES : (j + 1) * LANES]
        norm_ref[half * lines : (half + 1) * lines, :] = sum_lanes(part)
        turned_ref[:, span] = rows.T


def student_expo(flags, own, other, protos):
    blocks, both, width = own.shape
    count = blocks * both
    columns = protos.shape[1]
    return pl.pallas_call(
        student_kernel,
        in_specs=[IN_SMEM] + [IN_VMEM] * 3,
        out_specs=(IN_VMEM,) * 3,
        out_shape=(
            pltpu.VMEM((count, columns), bf16),
            jax.ShapeDtypeStruct((count // LANES, LANES), f32),
            pltpu.VMEM((width, count), bf16),
        ),
        compiler_params=params(),
        cost_estimate=cost(2 * count * width * columns, count * columns, 2 * count * columns),
        name="student_expo",
    )(flags, own, other, protos)


def scaled_product(scale, turned_ref, codes_ref):
    turned = (turned_ref[...].astype(f32) * lane_row(scale, 0, scale.shape[0])).astype(bf16)
    return jnp.dot(turned, codes_ref[...], preferred_element_type=f32)


def grad_kernel(recv_ref, norm_ref, cols_ref, turned_ref, codes_ref, expo_ref, out_ref):
    members = recv_ref.shape[0]
    lines = codes_ref.shape[0] // LANES
    row_scale = 1.0 / jnp.sum(recv_ref[:, :lines, :].astype(f32), axis=0)
    norm = jnp.concatenate(
        [norm_ref[m, lines : lines + 1, :].astype(f32) + norm_ref[m, lines + 1 : lines + 2, :].astype(f32) for m in range(members)],
        axis=0,
    )
    mass = jnp.sum(cols_ref[...].astype(f32), axis=0)
    teach = scaled_product(row_scale, turned_ref, codes_ref) * lane_row(1.0 / mass, 0, cols_ref.shape[1])
    grad = grad_factor * (scaled_product(1.0 / norm, turned_ref, expo_ref) - teach)
    for piece in range(out_ref.shape[0]):
        out_ref[piece] = pack_piece(grad, piece, out_ref.shape[0]).astype(bf16)


def grad_pieces(recv, norm, cols, turned, codes, expo, pieces):
    count, columns = codes.shape
    width = turned.shape[0]
    return pl.pallas_call(
        grad_kernel,
        in_specs=[IN_VMEM] * 6,
        out_specs=IN_VMEM,
        out_shape=jax.ShapeDtypeStruct((pieces, width // 2, 2 * columns // pieces), bf16),
        compiler_params=params(),
        cost_estimate=cost(4 * count * width * columns, 0, 4 * count * columns),
        name="grad_pieces",
    )(recv, norm, cols, turned, codes, expo)


def add_kernel(recv_ref, out_ref):
    for piece in range(out_ref.shape[0]):
        out_ref[piece] = jnp.sum(recv_ref[:, piece].astype(f32), axis=0).astype(bf16)


def add_lines(recv):
    return pl.pallas_call(
        add_kernel,
        in_specs=[IN_VMEM],
        out_specs=IN_VMEM,
        out_shape=jax.ShapeDtypeStruct(recv.shape[1:], bf16),
        compiler_params=params(),
        name="add_lines",
    )(recv)


def back_kernel(recv_ref, weight_ref, out_ref):
    grad = jnp.sum(recv_ref[...].astype(f32), axis=0)
    weight = weight_ref[...]
    half = weight.shape[1] // 2

    def column_sum(values):
        total = jnp.sum(values, axis=0, keepdims=True)
        return total + jnp.concatenate([total[:, half:], total[:, :half]], axis=1)

    inverse = lax.rsqrt(column_sum(weight * weight) + epsilon)
    along = column_sum(grad * weight)
    back = (grad * inverse - weight * (inverse * inverse * inverse * along)).astype(bf16)
    out_ref[...] = back


def weight_back(recv, weight):
    return pl.pallas_call(
        back_kernel,
        in_specs=[IN_VMEM, IN_VMEM],
        out_specs=IN_VMEM,
        out_shape=jax.ShapeDtypeStruct(weight.shape, bf16),
        compiler_params=params(),
        name="weight_back",
    )(recv, weight)


def join_kernel(pieces_ref, out_ref):
    pieces, rows, lanes = pieces_ref.shape
    half = lanes // 2
    for pair in range(pieces // 2):
        at = [2 * (index % (pieces // 2)) + index // (pieces // 2) for index in (2 * pair, 2 * pair + 1)]
        left, right = pieces_ref[at[0]], pieces_ref[at[1]]
        columns = pl.ds(pair * lanes, lanes)
        out_ref[:rows, columns] = jnp.concatenate([left[:, :half], right[:, :half]], axis=1)
        out_ref[rows:, columns] = jnp.concatenate([left[:, half:], right[:, half:]], axis=1)


def join_pieces(pieces):
    count, rows, lanes = pieces.shape
    return pl.pallas_call(
        join_kernel,
        in_specs=[IN_VMEM],
        out_specs=IN_VMEM,
        out_shape=jax.ShapeDtypeStruct((2 * rows, count * lanes // 2), pieces.dtype),
        compiler_params=params(),
        name="join_pieces",
    )(pieces)


def exchange(values, axes):
    return lax.all_to_all(values, axes, 0, 0, tiled=True)


def shard_permutes(weight, pair):
    axes = ("core", "xhi", "xlo")
    first, second = [], []
    for core in range(2):
        for xhi in range(2):
            for xlo in range(2):
                here = core * 4 + xhi * 2 + xlo
                if xhi == core:
                    first.append((core * 4 + xhi * 2 + 1 - xlo, here))
                else:
                    first.append(((1 - core) * 4 + core * 2 + 1 - xlo, here))
                    second.append((core * 4 + (xhi if pair else core) * 2 + 1 - xlo, here))
    once = lax.ppermute(weight, axes, first)
    return once, lax.ppermute(once, axes, second)


def shards(teacher_patches, student_patches, mask_index, teacher_weight, student_weight):
    size = lax.axis_size
    column_peers, row_peers = size(COLUMN_PEERS), size(ROW_PEERS)
    shard_pieces = size(SHARD_PEERS)
    core, xhi, xlo = lax.axis_index("core"), lax.axis_index("xhi"), lax.axis_index("xlo")
    matched = (core == xhi).astype(jnp.int32)
    flags = jnp.stack([core, xlo, matched, lax.axis_index(SHARD_PEERS)]).astype(jnp.int32)

    teach_first, teach_second = shard_permutes(teacher_weight, True)
    stud_first, stud_second = shard_permutes(student_weight, False)
    line = masked_rows(mask_index.reshape(1, -1), teacher_patches, student_patches, size("z"))
    line = exchange(line, "z")
    (teach_protos,) = prototypes(flags, teacher_weight, teach_first, teach_second)
    line, teach_protos, stud_first, stud_second = lax.optimization_barrier((line, teach_protos, stud_first, stud_second))
    other = lax.ppermute(line, "core", [(0, 1), (1, 0)])
    stud_protos, weight = prototypes(flags, student_weight, stud_first, stud_second, shard_pieces)
    other, teach_protos, stud_protos, weight = lax.optimization_barrier((other, teach_protos, stud_protos, weight))

    codes, cols = first_codes(flags, line, other, teach_protos, column_peers)
    expo, norm, turned = student_expo(flags, line, other, stud_protos)
    cols, expo, norm, turned = lax.optimization_barrier((cols, expo, norm, turned))
    cols = exchange(cols, COLUMN_PEERS)
    rows = exchange(row_pass(cols, codes, row_peers, norm, 1), ROW_PEERS)
    cols = exchange(col_pass(rows, codes, column_peers), COLUMN_PEERS)
    rows = exchange(row_pass(cols, codes, row_peers, rows, 2), ROW_PEERS)
    norm = rows
    cols = exchange(col_pass(rows, codes, column_peers), COLUMN_PEERS)
    rows = exchange(row_pass(cols, codes, row_peers), ROW_PEERS)
    pieces = grad_pieces(rows, norm, cols, turned, codes, expo, 2 * shard_pieces)
    pieces = pieces.reshape((size(LINE_PEERS), size("y")) + pieces.shape[1:])
    pieces = exchange(add_lines(exchange(pieces, LINE_PEERS)), "y")
    mine = weight_back(pieces, weight)
    other = lax.ppermute(mine, ("core", "xhi"), [(1, 2), (2, 1)])
    piece = jnp.where(matched == 1, mine, other)
    return join_pieces(lax.all_gather(piece, ("y", "core"), axis=0))


def solution(mesh):
    split = Mesh(mesh.devices.reshape(8, 2, 8, 2, 2), ALL)
    rows = P(ALL, None)
    columns = P(None, SHARD)
    return jax.shard_map(
        shards,
        mesh=split,
        in_specs=(rows, rows, P(ALL), columns, columns),
        out_specs=columns,
        check_vma=False,
    )
```

```python
import functools
import math

import jax
import jax.numpy as jnp
from jax import lax
from jax.experimental import pallas as pl
from jax.experimental.pallas import tpu as pltpu
from jax.sharding import Mesh
from jax.sharding import PartitionSpec as P

ALL = ("y", "core", "z", "xhi", "xlo")
SHARD = ("z", "xhi", "xlo")
COLUMN_PEERS = ("y", "xhi", "xlo")
ROW_PEERS = ("core", "z")
LINE_PEERS = ("xlo", "xhi")
SHARD_PEERS = ("xhi", "y")
LANES = 128
CHUNK = 1024
EXTRA = 8
VMEM_LIMIT = 20 * 1024 * 1024
LOG2E = math.log2(math.e)
IN_VMEM = pl.BlockSpec(memory_space=pltpu.VMEM)
IN_HBM = pl.BlockSpec(memory_space=pltpu.HBM)
IN_SMEM = pl.BlockSpec(memory_space=pltpu.SMEM)

epsilon = 1e-06
teacher_scale = 1.0 / 0.07
student_scale = 1.0 / 0.1
grad_factor = 256.0 / 0.1
NT = (((1,), (1,)), ((), ()))
TN = (((0,), (0,)), ((), ()))
f32 = jnp.float32
bf16 = jnp.bfloat16


def params():
    return pltpu.CompilerParams(vmem_limit_bytes=VMEM_LIMIT)


def cost(flops, transcendentals, nbytes):
    return pl.CostEstimate(flops=flops, transcendentals=transcendentals, bytes_accessed=nbytes)


def lane_row(block, start, count):
    return jnp.concatenate([block[start + j : start + j + 1, :] for j in range(count)], axis=1)


def in_hbm(values):
    return pltpu.with_memory_space_constraint(values, pltpu.HBM)


def rows_kernel(mask_ref, teacher_ref, student_ref, out_ref, index_ref, held_ref, made_ref, sems):
    copies = [
        pltpu.make_async_copy(mask_ref, index_ref, sems.at[0]),
        pltpu.make_async_copy(teacher_ref, held_ref.at[0], sems.at[1]),
        pltpu.make_async_copy(student_ref, held_ref.at[1], sems.at[2]),
    ]
    for copy in copies:
        copy.start()
    copies[0].wait()
    patches = teacher_ref.shape[0]
    count = mask_ref.shape[1]
    chosen = lax.broadcasted_iota(jnp.int32, (patches, count), 0) == index_ref[...]
    chosen = chosen.astype(f32).astype(bf16)
    sends = []
    for part in range(2):
        copies[1 + part].wait()
        rows = lax.dot_general(chosen, held_ref[part], TN, preferred_element_type=f32)
        square = jnp.sum(rows * rows, axis=1, keepdims=True)
        span = pl.ds(part * count, count)
        made_ref[span, :] = (rows * lax.rsqrt(square + epsilon)).astype(bf16)
        for i in range(out_ref.shape[0]):
            sem = sems.at[3 + part * out_ref.shape[0] + i]
            sends.append(pltpu.make_async_copy(made_ref.at[span, :], out_ref.at[i, span, :], sem))
            sends[-1].start()
    for send in sends:
        send.wait()


def masked_rows(mask, teacher, student, copies):
    count, width = mask.shape[1], teacher.shape[1]
    return pl.pallas_call(
        rows_kernel,
        in_specs=[IN_HBM] * 3,
        out_specs=IN_HBM,
        out_shape=pltpu.HBM((copies, 2 * count, width), bf16),
        scratch_shapes=[
            pltpu.VMEM(mask.shape, jnp.int32),
            pltpu.VMEM((2,) + teacher.shape, bf16),
            pltpu.VMEM((2 * count, width), bf16),
            pltpu.SemaphoreType.DMA((3 + 2 * copies,)),
        ],
        compiler_params=params(),
        name="masked_rows",
    )(in_hbm(mask), in_hbm(teacher), in_hbm(student))


def two_shards(flags_ref, own_ref, first_ref, second_ref, act):
    @pl.when(flags_ref[2] == 1)
    def _():
        act(own_ref, first_ref)

    @pl.when(flags_ref[2] == 0)
    def _():
        act(second_ref, first_ref)


def protos_kernel(pieces, flags_ref, own_ref, first_ref, second_ref, out_ref, *rest):
    piece_ref, held_ref, sems = rest if pieces else (None,) + rest

    def bring(one, other):
        copies = [
            pltpu.make_async_copy(one, held_ref.at[0], sems.at[0]),
            pltpu.make_async_copy(other, held_ref.at[1], sems.at[1]),
        ]
        for copy in copies:
            copy.start()
        for copy in copies:
            copy.wait()

    two_shards(flags_ref, own_ref, first_ref, second_ref, bring)
    columns = own_ref.shape[1]
    xlo = flags_ref[1]
    for part, place in ((0, xlo), (1, 1 - xlo)):
        values = held_ref[part].astype(f32)
        square = jnp.sum(values * values, axis=0, keepdims=True)
        at = pl.multiple_of(place * columns, columns)
        out_ref[:, pl.ds(at, columns)] = (values * lax.rsqrt(square + epsilon)).astype(bf16)
    if pieces:
        index = flags_ref[3]
        half = columns // pieces
        block = held_ref[0, :, pl.ds(pl.multiple_of(index // 2 * LANES, LANES), LANES)].astype(f32)
        block = jnp.where(index % 2 == 0, block[:, :half], block[:, half:])
        rows = block.shape[0] // 2
        piece_ref[...] = jnp.concatenate([block[:rows], block[rows:]], axis=1)


def prototypes(flags, own, first, second, pieces=0):
    rows, columns = own.shape
    shapes = [jax.ShapeDtypeStruct((rows, 2 * columns), bf16)]
    if pieces:
        shapes.append(jax.ShapeDtypeStruct((rows // 2, 2 * columns // pieces), f32))
    return pl.pallas_call(
        functools.partial(protos_kernel, pieces),
        in_specs=[IN_SMEM] + [IN_HBM] * 3,
        out_specs=[IN_VMEM] * len(shapes),
        out_shape=shapes,
        scratch_shapes=[pltpu.VMEM((2, rows, columns), bf16), pltpu.SemaphoreType.DMA((2,))],
        compiler_params=params(),
        cost_estimate=cost(4 * rows * columns, 0, 8 * rows * columns),
        name="prototypes",
    )(flags, in_hbm(own), in_hbm(first), in_hbm(second))


def pack_piece(block, piece, pieces):
    rows, columns = block.shape
    width = columns // pieces
    part = block[:, piece * width : (piece + 1) * width]
    return jnp.concatenate([part[: rows // 2], part[rows // 2 :]], axis=1)


def spread_cols(total, cols_ref):
    lines = cols_ref.shape[1]
    block = jnp.concatenate([total[:, j * LANES : (j + 1) * LANES] for j in range(lines)], axis=0)
    cols_ref[...] = jnp.broadcast_to(block[None], cols_ref.shape).astype(bf16)


def net_rows(ref, net):
    blocks, both, width = ref.shape
    count = both // 2
    return ref[:, net * count : (net + 1) * count, :].reshape(blocks * count, width)


def codes_kernel(flags_ref, own_ref, other_ref, protos_ref, codes_ref, cols_ref):
    core = flags_ref[0]
    count = codes_ref.shape[0] // 2
    total = None
    for ref, place in ((own_ref, core), (other_ref, 1 - core)):
        scores = jnp.dot(net_rows(ref, 0), protos_ref[...], preferred_element_type=f32)
        codes = jnp.exp2(scores * (teacher_scale * LOG2E))
        codes_ref[pl.ds(pl.multiple_of(place * count, count), count), :] = codes.astype(bf16)
        sums = jnp.sum(codes, axis=0, keepdims=True)
        total = sums if total is None else total + sums
    spread_cols(total, cols_ref)


def first_codes(flags, own, other, protos, groups):
    blocks, both, width = own.shape
    count = blocks * both
    columns = protos.shape[1]
    return pl.pallas_call(
        codes_kernel,
        in_specs=[IN_SMEM] + [IN_VMEM] * 3,
        out_specs=(IN_VMEM, IN_VMEM),
        out_shape=(
            pltpu.VMEM((count, columns), bf16),
            jax.ShapeDtypeStruct((groups, columns // LANES, LANES), bf16),
        ),
        compiler_params=params(),
        cost_estimate=cost(2 * count * width * columns, count * columns, 2 * count * columns),
        name="first_codes",
    )(flags, own, other, protos)


def sum_lanes(block):
    ones = jnp.ones((16, LANES), bf16)
    sums = lax.dot_general(ones, block.astype(bf16), NT, preferred_element_type=f32)[0:1]
    lines = block.shape[0] // LANES
    return jnp.concatenate([sums[:, j * LANES : (j + 1) * LANES] for j in range(lines)], axis=0)


def row_pass_kernel(stage, *refs):
    recv_ref, codes_ref = refs[:2]
    norm_ref, out_ref = refs[2] if stage else None, refs[-1]
    count = codes_ref.shape[0]
    tiles = recv_ref.shape[1]
    lines = CHUNK // LANES
    scale = lane_row(1.0 / jnp.sum(recv_ref[...].astype(f32), axis=0), 0, tiles).astype(bf16)
    for i in range(count // CHUNK):
        blocks = []
        for k in range(lines):
            at = i * CHUNK + k * LANES
            total = None
            for g in range(0, tiles, 8):
                part = None
                for j in range(g, g + 8):
                    columns = slice(j * LANES, (j + 1) * LANES)
                    term = codes_ref[at : at + LANES, columns] * scale[:, columns]
                    part = term if part is None else part + term
                part = part.astype(f32)
                total = part if total is None else total + part
            blocks.append(total.astype(bf16))
        block = jnp.broadcast_to(sum_lanes(jnp.concatenate(blocks, axis=0))[None], (out_ref.shape[0], lines, LANES))
        out_ref[:, i * lines : (i + 1) * lines, :] = block.astype(bf16)
    first = count // LANES
    if stage == 1:
        for member in range(out_ref.shape[0]):
            line = norm_ref[member : member + 1, :]
            out_ref[member, first:, :] = jnp.broadcast_to(line, (EXTRA, LANES)).astype(bf16)
    if stage == 2:
        total = jnp.sum(norm_ref[:, first : first + 1, :].astype(f32), axis=0)
        high = total.astype(bf16).astype(f32)
        index = lax.broadcasted_iota(jnp.int32, (EXTRA, LANES), 0)
        extra = jnp.where(index == 0, high, jnp.where(index == 1, total - high, 0.0)).astype(bf16)
        out_ref[:, first:, :] = jnp.broadcast_to(extra[None], (out_ref.shape[0], EXTRA, LANES))


def row_pass(recv, codes, members, norm=None, stage=0):
    count, columns = codes.shape
    lines = count // LANES + (EXTRA if stage else 0)
    return pl.pallas_call(
        functools.partial(row_pass_kernel, stage),
        in_specs=[IN_VMEM] * (3 if stage else 2),
        out_specs=IN_VMEM,
        out_shape=jax.ShapeDtypeStruct((members, lines, LANES), bf16),
        compiler_params=params(),
        cost_estimate=cost(2 * count * columns, 0, 2 * count * columns),
        name="row_pass",
    )(recv, codes, *((norm,) if stage else ()))


def col_pass_kernel(recv_ref, codes_ref, cols_ref):
    count, columns = codes_ref.shape
    lines = CHUNK // LANES
    scale = 1.0 / jnp.sum(recv_ref[:, : count // LANES, :].astype(f32), axis=0)
    ones = jnp.ones((16, LANES), bf16)
    first = lax.broadcasted_iota(jnp.int32, (16, CHUNK), 0) == 0
    spreads = []
    for i in range(count // CHUNK):
        row = jnp.where(first, lane_row(scale, i * lines, lines), 0.0).astype(bf16)
        spreads.append(lax.dot_general(row, ones, TN, preferred_element_type=f32).astype(bf16))
    width = 8 * LANES
    totals = []
    for h in range(columns // width):
        total = jnp.zeros((16, width), f32)
        for i, spread in enumerate(spreads):
            for g in range(lines):
                parts = []
                for j in range(width // LANES):
                    part = None
                    for q in range(LANES // 16):
                        at = g * LANES + q * 16
                        lane = h * width + j * LANES
                        term = codes_ref[i * CHUNK + at : i * CHUNK + at + 16, lane : lane + LANES]
                        term = term * spread[at : at + 16]
                        part = term if part is None else part + term
                    parts.append(part.astype(f32))
                total = total + jnp.concatenate(parts, axis=1)
        totals.append(jnp.sum(total, axis=0, keepdims=True))
    spread_cols(jnp.concatenate(totals, axis=1), cols_ref)


def col_pass(recv, codes, groups):
    count, columns = codes.shape
    return pl.pallas_call(
        col_pass_kernel,
        in_specs=[IN_VMEM, IN_VMEM],
        out_specs=IN_VMEM,
        out_shape=jax.ShapeDtypeStruct((groups, columns // LANES, LANES), bf16),
        compiler_params=params(),
        cost_estimate=cost(2 * count * columns, 0, 2 * count * columns),
        name="col_pass",
    )(recv, codes)


def student_kernel(flags_ref, own_ref, other_ref, protos_ref, expo_ref, norm_ref, turned_ref):
    core = flags_ref[0]
    columns = protos_ref.shape[1]
    count = expo_ref.shape[0] // 2
    lines = count // LANES
    for half in range(2):
        rows = jnp.where(core == half, net_rows(own_ref, 1), net_rows(other_ref, 1))
        span = slice(half * count, (half + 1) * count)
        scores = jnp.dot(rows, protos_ref[...], preferred_element_type=f32)
        expo = jnp.exp2(scores * (student_scale * LOG2E))
        expo_ref[span, :] = expo.astype(bf16)
        part = expo[:, :LANES]
        for j in range(1, columns // LANES):
            part = part + expo[:, j * LANES : (j + 1) * LANES]
        norm_ref[half * lines : (half + 1) * lines, :] = sum_lanes(part)
        turned_ref[:, span] = rows.T


def student_expo(flags, own, other, protos):
    blocks, both, width = own.shape
    count = blocks * both
    columns = protos.shape[1]
    return pl.pallas_call(
        student_kernel,
        in_specs=[IN_SMEM] + [IN_VMEM] * 3,
        out_specs=(IN_VMEM,) * 3,
        out_shape=(
            pltpu.VMEM((count, columns), bf16),
            jax.ShapeDtypeStruct((count // LANES, LANES), f32),
            pltpu.VMEM((width, count), bf16),
        ),
        compiler_params=params(),
        cost_estimate=cost(2 * count * width * columns, count * columns, 2 * count * columns),
        name="student_expo",
    )(flags, own, other, protos)


def scaled_product(scale, turned_ref, codes_ref):
    turned = (turned_ref[...].astype(f32) * lane_row(scale, 0, scale.shape[0])).astype(bf16)
    return jnp.dot(turned, codes_ref[...], preferred_element_type=f32)


def grad_kernel(recv_ref, norm_ref, cols_ref, turned_ref, codes_ref, expo_ref, out_ref):
    members = recv_ref.shape[0]
    lines = codes_ref.shape[0] // LANES
    row_scale = 1.0 / jnp.sum(recv_ref[:, :lines, :].astype(f32), axis=0)
    norm = jnp.concatenate(
        [norm_ref[m, lines : lines + 1, :].astype(f32) + norm_ref[m, lines + 1 : lines + 2, :].astype(f32) for m in range(members)],
        axis=0,
    )
    mass = jnp.sum(cols_ref[...].astype(f32), axis=0)
    teach = scaled_product(row_scale, turned_ref, codes_ref) * lane_row(1.0 / mass, 0, cols_ref.shape[1])
    grad = grad_factor * (scaled_product(1.0 / norm, turned_ref, expo_ref) - teach)
    for piece in range(out_ref.shape[0]):
        out_ref[piece] = pack_piece(grad, piece, out_ref.shape[0]).astype(bf16)


def grad_pieces(recv, norm, cols, turned, codes, expo, pieces):
    count, columns = codes.shape
    width = turned.shape[0]
    return pl.pallas_call(
        grad_kernel,
        in_specs=[IN_VMEM] * 6,
        out_specs=IN_VMEM,
        out_shape=jax.ShapeDtypeStruct((pieces, width // 2, 2 * columns // pieces), bf16),
        compiler_params=params(),
        cost_estimate=cost(4 * count * width * columns, 0, 4 * count * columns),
        name="grad_pieces",
    )(recv, norm, cols, turned, codes, expo)


def add_kernel(recv_ref, out_ref):
    for piece in range(out_ref.shape[0]):
        out_ref[piece] = jnp.sum(recv_ref[:, piece].astype(f32), axis=0).astype(bf16)


def add_lines(recv):
    return pl.pallas_call(
        add_kernel,
        in_specs=[IN_VMEM],
        out_specs=IN_VMEM,
        out_shape=jax.ShapeDtypeStruct(recv.shape[1:], bf16),
        compiler_params=params(),
        name="add_lines",
    )(recv)


def back_kernel(recv_ref, weight_ref, out_ref):
    grad = jnp.sum(recv_ref[...].astype(f32), axis=0)
    weight = weight_ref[...]
    half = weight.shape[1] // 2

    def column_sum(values):
        total = jnp.sum(values, axis=0, keepdims=True)
        return total + jnp.concatenate([total[:, half:], total[:, :half]], axis=1)

    inverse = lax.rsqrt(column_sum(weight * weight) + epsilon)
    along = column_sum(grad * weight)
    back = (grad * inverse - weight * (inverse * inverse * inverse * along)).astype(bf16)
    out_ref[...] = back


def weight_back(recv, weight):
    return pl.pallas_call(
        back_kernel,
        in_specs=[IN_VMEM, IN_VMEM],
        out_specs=IN_VMEM,
        out_shape=jax.ShapeDtypeStruct(weight.shape, bf16),
        compiler_params=params(),
        name="weight_back",
    )(recv, weight)


def join_kernel(pieces_ref, out_ref):
    pieces, rows, lanes = pieces_ref.shape
    half = lanes // 2
    for pair in range(pieces // 2):
        at = [2 * (index % (pieces // 2)) + index // (pieces // 2) for index in (2 * pair, 2 * pair + 1)]
        left, right = pieces_ref[at[0]], pieces_ref[at[1]]
        columns = pl.ds(pair * lanes, lanes)
        out_ref[:rows, columns] = jnp.concatenate([left[:, :half], right[:, :half]], axis=1)
        out_ref[rows:, columns] = jnp.concatenate([left[:, half:], right[:, half:]], axis=1)


def join_pieces(pieces):
    count, rows, lanes = pieces.shape
    return pl.pallas_call(
        join_kernel,
        in_specs=[IN_VMEM],
        out_specs=IN_VMEM,
        out_shape=jax.ShapeDtypeStruct((2 * rows, count * lanes // 2), pieces.dtype),
        compiler_params=params(),
        name="join_pieces",
    )(pieces)


def exchange(values, axes):
    return lax.all_to_all(values, axes, 0, 0, tiled=True)


def shard_permutes(weight, pair):
    axes = ("core", "xhi", "xlo")
    first, second = [], []
    for core in range(2):
        for xhi in range(2):
            for xlo in range(2):
                here = core * 4 + xhi * 2 + xlo
                if xhi == core:
                    first.append((core * 4 + xhi * 2 + 1 - xlo, here))
                else:
                    first.append(((1 - core) * 4 + core * 2 + 1 - xlo, here))
                    second.append((core * 4 + (xhi if pair else core) * 2 + 1 - xlo, here))
    once = lax.ppermute(weight, axes, first)
    return once, lax.ppermute(once, axes, second)


def shards(teacher_patches, student_patches, mask_index, teacher_weight, student_weight):
    size = lax.axis_size
    column_peers, row_peers = size(COLUMN_PEERS), size(ROW_PEERS)
    shard_pieces = size(SHARD_PEERS)
    core, xhi, xlo = lax.axis_index("core"), lax.axis_index("xhi"), lax.axis_index("xlo")
    matched = (core == xhi).astype(jnp.int32)
    flags = jnp.stack([core, xlo, matched, lax.axis_index(SHARD_PEERS)]).astype(jnp.int32)

    teach_first, teach_second = shard_permutes(teacher_weight, True)
    stud_first, stud_second = shard_permutes(student_weight, False)
    line = masked_rows(mask_index.reshape(1, -1), teacher_patches, student_patches, size("z"))
    line = exchange(line, "z")
    (teach_protos,) = prototypes(flags, teacher_weight, teach_first, teach_second)
    line, teach_protos, stud_first, stud_second = lax.optimization_barrier((line, teach_protos, stud_first, stud_second))
    other = lax.ppermute(line, "core", [(0, 1), (1, 0)])
    stud_protos, weight = prototypes(flags, student_weight, stud_first, stud_second, shard_pieces)
    other, teach_protos, stud_protos, weight = lax.optimization_barrier((other, teach_protos, stud_protos, weight))

    codes, cols = first_codes(flags, line, other, teach_protos, column_peers)
    expo, norm, turned = student_expo(flags, line, other, stud_protos)
    cols, expo, norm, turned = lax.optimization_barrier((cols, expo, norm, turned))
    cols = exchange(cols, COLUMN_PEERS)
    rows = exchange(row_pass(cols, codes, row_peers, norm, 1), ROW_PEERS)
    cols = exchange(col_pass(rows, codes, column_peers), COLUMN_PEERS)
    rows = exchange(row_pass(cols, codes, row_peers, rows, 2), ROW_PEERS)
    norm = rows
    cols = exchange(col_pass(rows, codes, column_peers), COLUMN_PEERS)
    rows = exchange(row_pass(cols, codes, row_peers), ROW_PEERS)
    pieces = grad_pieces(rows, norm, cols, turned, codes, expo, 2 * shard_pieces)
    pieces = pieces.reshape((size(LINE_PEERS), size("y")) + pieces.shape[1:])
    pieces = exchange(add_lines(exchange(pieces, LINE_PEERS)), "y")
    mine = weight_back(pieces, weight)
    other = lax.ppermute(mine, ("core", "xhi"), [(1, 2), (2, 1)])
    piece = jnp.where(matched == 1, mine, other)
    return join_pieces(lax.all_gather(piece, ("y", "core"), axis=0))


def solution(mesh):
    split = Mesh(mesh.devices.reshape(8, 2, 8, 2, 2), ALL)
    rows = P(ALL, None)
    columns = P(None, SHARD)
    return jax.shard_map(
        shards,
        mesh=split,
        in_specs=(rows, rows, P(ALL), columns, columns),
        out_specs=columns,
        check_vma=False,
    )
```
